32 devices in a mesh: nest: 2 (over x), tile: 16 (over z, y, core).
Axes of the slice: x: 2, y: 2, z: 4, core: 2. Of those that a mesh axis runs over, the one named last changes fastest.
Arguments:
- fine_level: float32 [2, 1280, 640], P('nest', 'tile'), may hold values from -4 to 4
- fine_flux: float32 [2, 2, 1280, 640], P('nest', None, 'tile'), may hold values from -3 to 3
- fine_depth: float32 [2, 1280, 640], P('nest', 'tile'), may hold values from 0.5 to 2
- shoreline: int32 [2, 1280], P('nest', 'tile'), may hold values from 0 to 319
- extents: int32 [2, 16], P('nest', 'tile'), may hold values from 0 to 80, as said below
- intersection: int32 [2, 2], replicated, may hold values from 0 to 383, as said below
- parent_level: float32 [256, 512], P('tile'), may hold values from -4 to 4
- parent_flux: float32 [2, 256, 512], P(None, 'tile'), may hold values from -3 to 3
- parent_depth: float32 [256, 512], P('tile'), may hold values from 0.5 to 2
- wind_stress: float32 [2, 256, 512], P(None, 'tile'), may hold values from -3 to 3
Outputs:
- fine_level_out: float32 [2, 1280, 640], P('nest', 'tile')
- fine_flux_out: float32 [2, 2, 1280, 640], P('nest', None, 'tile')
- parent_level_out: float32 [256, 512], P('tile')
- parent_flux_out: float32 [2, 256, 512], P(None, 'tile')
The draws below stay inside these ranges and needn't reach their ends.
Inputs may be any that keep to these rules, and one draw needn't show every extreme that they name: `intersection`: row offsets are below 16; nest 0's row offset is at least 1 and nest 1's is 0. First columns are at most 383, and one nest's first column is exactly that. `extents`: within each nest, tiles are fully active up to one partly active tile, and inactive after it; nest 0 is fully active.
All inputs are finite; a program needn't handle non-finite values.
Results may differ from the reference program's by a relative error of at most 0.0003.
Values sent between devices are 32-bit elements; how exact they have to be, the bound alone decides.
A program may use at most 64 MiB of HBM per device.

```python
import math
import jax
import jax.numpy as jnp
from jax import lax

RD = 80
RATIO = 5
WF = 640
PC = 512
SUBSTEPS = 4
STEPS = 2
PRD = 16
FR = 1280
PR = 256


def draw_intersection(key, part):
    key_side = jax.random.fold_in(key, 11)
    key_row = jax.random.fold_in(key, 12)
    key_col = jax.random.fold_in(key, 13)
    last_col = PC - WF // RATIO - 1
    side = jax.random.randint(key_side, (), 0, 2).astype(jnp.int32)
    moving_row = jax.random.randint(key_row, (), 1, PRD).astype(jnp.int32)
    moving_col = jax.random.randint(key_col, (), 0, last_col + 1).astype(jnp.int32)
    col_first = jnp.where(side == 0, jnp.int32(last_col), moving_col).astype(jnp.int32)
    col_second = jnp.where(side == 0, moving_col, jnp.int32(last_col)).astype(jnp.int32)
    first = jnp.stack([moving_row, col_first])
    second = jnp.stack([jnp.int32(0), col_second])
    return jnp.stack([first, second]).astype(jnp.int32)


def draw_extents(key, part):
    tile_count = FR // RD
    length = jax.random.randint(key, (), FR // 2, FR - RD + 1).astype(jnp.int32)
    lengths = jnp.stack([jnp.int32(FR), length])
    starts = jnp.arange(tile_count, dtype=jnp.int32) * RD
    return jnp.clip(lengths[:, None] - starts[None, :], 0, RD).astype(jnp.int32)


def touch_ends(values, rng, low, high):
    longest = values.shape.index(max(values.shape))
    spots = []
    for shift in (0, 1):
        where = [jax.random.randint(jax.random.fold_in(rng, axis), (), 0, length) for axis, length in enumerate(values.shape)]
        where[longest] = (where[longest] + shift) % values.shape[longest]
        spots.append(tuple(where))
    return values.at[spots[0]].set(low).at[spots[1]].set(high)


def shard_levels(rng, extent, pieces, smallest, largest):
    factor_of = 1.0
    for axis_at, parts in pieces:
        steps = jax.random.uniform(jax.random.fold_in(jax.random.fold_in(rng, 6), axis_at), (parts,), jnp.float32, smallest / len(pieces), largest / len(pieces))
        factor_of = factor_of * jnp.repeat(jnp.exp(steps), extent[axis_at] // parts).reshape((-1,) + (1,) * (len(extent) - 1 - axis_at))
    return factor_of


def noise(stream_key, shape, deviation, reach, split=(), kind=jnp.bfloat16):
    values = deviation * jax.random.normal(stream_key, shape, jnp.float32)
    if split:
        values = values * shard_levels(stream_key, shape, split, -0.22, 0.18)
    return jnp.clip(values, -reach, reach).astype(kind)


def setup_inputs(seed: int = 0) -> dict:
    key_of = jax.random.split(jax.random.key(seed), 11)
    return {
        "fine_level": noise(key_of[0], (2, FR, WF), 0.5, 4.0, ((0, 2), (1, 16)), jnp.float32),
        "fine_flux": noise(key_of[1], (2, 2, FR, WF), 0.3, 3.0, ((0, 2), (2, 16)), jnp.float32),
        "fine_depth": jnp.clip(jnp.exp(math.log(2.0) - 1.3862944 * jax.random.uniform(key_of[2], (2, FR, WF), jnp.float32) ** shard_levels(key_of[2], (2, FR, WF), ((0, 2), (1, 16)), -0.2, 0.2)), 0.5, 2.0),
        "shoreline": touch_ends(jax.random.randint(key_of[3], (2, FR), 0, WF // 2), jax.random.fold_in(key_of[3], 1), 0, (WF // 2) - 1).astype(jnp.int32),
        "extents": draw_extents(jax.random.fold_in(key_of[10], 71), 0),
        "intersection": draw_intersection(jax.random.fold_in(key_of[10], 71), 0),
        "parent_level": noise(key_of[6], (PR, PC), 0.5, 4.0, ((0, 16),), jnp.float32),
        "parent_flux": noise(key_of[7], (2, PR, PC), 0.3, 3.0, ((1, 16),), jnp.float32),
        "parent_depth": jnp.clip(jnp.exp(math.log(2.0) - 1.3862944 * jax.random.uniform(key_of[8], (PR, PC), jnp.float32) ** shard_levels(key_of[8], (PR, PC), ((0, 16),), -0.2, 0.2)), 0.5, 2.0),
        "wind_stress": noise(key_of[9], (2, PR, PC), 0.3, 3.0, ((1, 16),), jnp.float32),
    }


DT_FINE = 0.4
DT_COARSE = 1.6
DX_COARSE = 5.0
FRICTION = 0.05

def shift_up(values):
    return jnp.concatenate([values[1:], jnp.zeros_like(values[:1])], axis=0)

def shift_left(values):
    return jnp.concatenate([values[:, 1:], jnp.zeros_like(values[:, :1])], axis=1)

def from_north(values):
    return jnp.concatenate([jnp.zeros_like(values[:1]), values[:-1]], axis=0)

def from_west(values):
    return jnp.concatenate([jnp.zeros_like(values[:, :1]), values[:, :-1]], axis=1)

def parent_step(surface, fluxes, depths, wind):
    height, breadth = surface.shape
    damping = 1.0 / (1.0 + DT_COARSE * FRICTION)
    col_open = (jnp.arange(breadth) < breadth - 1).astype(jnp.float32)[None, :]
    row_open = (jnp.arange(height) < height - 1).astype(jnp.float32)[:, None]
    depth_x = 0.5 * (depths + shift_left(depths))
    depth_y = 0.5 * (depths + shift_up(depths))
    new_x = col_open * (fluxes[0] - DT_COARSE / DX_COARSE * depth_x * (shift_left(surface) - surface) + DT_COARSE * wind[0]) * damping
    new_y = row_open * (fluxes[1] - DT_COARSE / DX_COARSE * depth_y * (shift_up(surface) - surface) + DT_COARSE * wind[1]) * damping
    new_surface = surface - DT_COARSE / DX_COARSE * (new_x - from_west(new_x) + new_y - from_north(new_y))
    return (new_surface, jnp.stack([new_x, new_y]))

def fine_substep(surface, flux_x, flux_y, depths, active, edge_level, edge_flux):
    damping = 1.0 / (1.0 + DT_FINE * FRICTION)
    face_x = active[:, :-1] * active[:, 1:]
    depth_x = 0.5 * (depths[:, :-1] + depths[:, 1:])
    inner_x = face_x * (flux_x[:, :-1] - DT_FINE * depth_x * (surface[:, 1:] - surface[:, :-1])) * damping
    east_x = active[:, -1] * (edge_flux + jnp.sqrt(depths[:, -1]) * (surface[:, -1] - edge_level))
    new_x = jnp.concatenate([inner_x, east_x[:, None]], axis=1)
    face_y = active * shift_up(active)
    depth_y = 0.5 * (depths + shift_up(depths))
    new_y = face_y * (flux_y - DT_FINE * depth_y * (shift_up(surface) - surface)) * damping
    new_surface = surface - DT_FINE * (new_x - from_west(new_x) + new_y - from_north(new_y))
    return (new_surface, new_x, new_y)

def block_sum(values):
    height, breadth = values.shape
    return values.reshape(height // RATIO, RATIO, breadth // RATIO, RATIO).sum(axis=(1, 3))

def sea_edge(surface, fluxes, placement, fine_rows, parent_width, parent_rows):
    rows_parent = jnp.minimum(placement[0] + jnp.arange(fine_rows, dtype=jnp.int32) // RATIO, parent_rows - 1).astype(jnp.int32)
    level_col = lax.dynamic_slice_in_dim(surface, (placement[1] + parent_width).astype(jnp.int32), 1, 1)[:, 0]
    flux_col = lax.dynamic_slice_in_dim(fluxes[0], (placement[1] + parent_width - 1).astype(jnp.int32), 1, 1)[:, 0]
    return (jnp.take(level_col, rows_parent), jnp.take(flux_col, rows_parent))

def reference(fine_level, fine_flux, fine_depth, shoreline, extents, intersection, parent_level, parent_flux, parent_depth, wind_stress):
    fine_rows, breadth = (fine_level.shape[1], fine_level.shape[2])
    parent_rows, parent_cols = parent_level.shape
    parent_width = breadth // RATIO
    tile_rows = parent_rows // (fine_rows // RD)
    rows_index = jnp.arange(fine_rows, dtype=jnp.int32)
    columns = jnp.arange(breadth, dtype=jnp.int32)
    actives = []
    for member in range(2):
        row_limit = jnp.repeat(extents[member], RD, total_repeat_length=fine_rows)
        live_row = (rows_index % RD < row_limit) & (intersection[member, 0] + rows_index // RATIO < parent_rows)
        actives.append(((columns[None, :] >= shoreline[member][:, None]) & live_row[:, None]).astype(jnp.float32))
    surfaces = [fine_level[0], fine_level[1]]
    flux_xs = [fine_flux[0, 0], fine_flux[1, 0]]
    flux_ys = [fine_flux[0, 1], fine_flux[1, 1]]
    parent_surface, parent_fluxes = (parent_level, parent_flux)
    zero_index = jnp.zeros((), jnp.int32)
    for coarse_step in range(STEPS):
        old_edges = [sea_edge(parent_surface, parent_fluxes, intersection[member], fine_rows, parent_width, parent_rows) for member in range(2)]
        parent_surface, parent_fluxes = parent_step(parent_surface, parent_fluxes, parent_depth, wind_stress)
        totals = jnp.zeros((4, parent_rows, parent_cols), jnp.float32)
        for member in range(2):
            old_level, old_flux = old_edges[member]
            new_level, new_flux = sea_edge(parent_surface, parent_fluxes, intersection[member], fine_rows, parent_width, parent_rows)
            for substep in range(SUBSTEPS):
                weight_new = (substep + 0.5) / SUBSTEPS
                edge_level = (1.0 - weight_new) * old_level + weight_new * new_level
                edge_flux = (1.0 - weight_new) * old_flux + weight_new * new_flux
                surfaces[member], flux_xs[member], flux_ys[member] = fine_substep(surfaces[member], flux_xs[member], flux_ys[member], fine_depth[member], actives[member], edge_level, edge_flux)
            active = actives[member]
            block_sums = jnp.stack([block_sum(active), block_sum(active * surfaces[member]), block_sum(active * flux_xs[member]), block_sum(active * flux_ys[member])])
            padded = jnp.zeros((4, parent_rows + tile_rows, parent_cols), jnp.float32)
            placed = lax.dynamic_update_slice(padded, block_sums, (zero_index, intersection[member, 0].astype(jnp.int32), intersection[member, 1].astype(jnp.int32)))
            totals = totals + placed[:, :parent_rows]
        shares = totals / (RATIO * RATIO)
        retained = 1.0 - shares[0]
        parent_surface = parent_surface * retained + shares[1]
        parent_fluxes = parent_fluxes * retained[None] + shares[2:]
    fine_out = jnp.stack(surfaces)
    flux_out = jnp.stack([jnp.stack([flux_xs[0], flux_ys[0]]), jnp.stack([flux_xs[1], flux_ys[1]])])
    return (fine_out, flux_out, parent_surface, parent_fluxes)
```

```python
import functools

import jax
import jax.numpy as jnp
from jax import lax
from jax.experimental import pallas as pl
from jax.experimental.pallas import tpu as pltpu
from jax.sharding import PartitionSpec as P

RATIO = 5
SUBSTEPS = 4
DT_FINE = 0.4
DT_COARSE = 1.6
DX_COARSE = 5.0
FRICTION = 0.05
RF = 1.0 / (1.0 + DT_FINE * FRICTION)
RP = 1.0 / (1.0 + DT_COARSE * FRICTION)
CP = DT_COARSE / DX_COARSE
FAR = 1.0e6
WIN = 112
CH = 16


def parts_of(x, n):
    out = []
    for _ in range(n):
        hi = x.astype(jnp.bfloat16)
        out.append(hi)
        x = x - hi.astype(jnp.float32)
    return out


def mm(a, b):
    return lax.dot_general(a, b, (((1,), (0,)), ((), ())), preferred_element_type=jnp.float32)


def left_hot(hot, x, n):
    return sum(mm(hot, p) for p in parts_of(x, n))


def right_hot(x, hot, n):
    return sum(mm(p, hot) for p in parts_of(x, n))


def hot_of(mask):
    return jnp.where(mask, 1.0, 0.0).astype(jnp.bfloat16)


def iota(shape, axis):
    return lax.broadcasted_iota(jnp.int32, shape, axis)


def fdiv5(x):
    return jnp.floor((x.astype(jnp.float32) + 0.5) * 0.2).astype(jnp.int32)


def shift_rows(x, by):
    return pltpu.roll(x, by % x.shape[0], 0)


def shift_cols(x, by):
    return pltpu.roll(x, by % x.shape[1], 1)


def parent_step(e, ux, uy, hx, hy, wx, wy, col_open, row_open):
    nx = col_open * (ux - CP * hx * (shift_cols(e, -1) - e) + DT_COARSE * wx) * RP
    ny = row_open * (uy - CP * hy * (shift_rows(e, -1) - e) + DT_COARSE * wy) * RP
    return nx, ny


def kernel(
    T, height, breadth, ph, pc,
    fl, ff, fd, shore, ext, inter, plev_h, pflux_h, pdep_h, wind_h,
    fl_out, ff_out, pl_out, pf_out,
    e, q, dep, lim, fxr, cx, fyr, cy, sea0, sead, er, qr, pfv, wv,
    shv, exs, ins, xlev, xdep, xuy, xwy, pws, pwb, pks, pkb, ss1, fs1, ss2, fs2, p2s, p2b,
    sa, ra, sb, rb, sc, rc, sd, rd, se, re_, sl_,
):
    k = lax.axis_index("nest")
    t = lax.axis_index("tile")
    ko = 1 - k
    top = 16
    rows = height + 32

    def have(d):
        return (t + d >= 0) & (t + d < T)

    small = [
        pltpu.make_async_copy(src, dst, sl_.at[7 + i])
        for i, (src, dst) in enumerate(((shore, shv), (ext, exs), (inter, ins)))
    ]
    for c in small:
        c.start()
    barrier = pltpu.get_barrier_semaphore()
    greet = [(k, -2), (k, -1), (k, 1), (k, 2)] + [(ko, d) for d in (-2, -1, 0, 1, 2)]
    count = 1
    for nest, d in greet:
        if d == 0:
            pl.semaphore_signal(barrier, inc=1, device_id=(nest, t), device_id_type=pl.DeviceIdType.MESH)
        else:
            @pl.when(have(d))
            def _():
                pl.semaphore_signal(barrier, inc=1, device_id=(nest, t + d), device_id_type=pl.DeviceIdType.MESH)
            count = count + have(d).astype(jnp.int32)

    class Push:
        def __init__(self, src, dst, ssem, rsem, nest, d):
            self.d, self.dst = d, dst
            self.c = pltpu.make_async_remote_copy(
                src_ref=src, dst_ref=dst, send_sem=ssem, recv_sem=rsem,
                device_id=(nest, t + d), device_id_type=pl.DeviceIdType.MESH)

        def start(self):
            if self.d == 0:
                self.c.start()
            else:
                pl.when(have(self.d))(lambda: self.c.start())

        def sent(self):
            if self.d == 0:
                self.c.wait_send()
            else:
                pl.when(have(self.d))(lambda: self.c.wait_send())

        def arrive(self, fill=0.0):
            if self.d == 0:
                self.c.wait_recv()
            else:
                pl.when(have(-self.d))(lambda: self.c.wait_recv())

                @pl.when(jnp.logical_not(have(-self.d)))
                def _():
                    self.dst[...] = jnp.full(self.dst.shape, fill, jnp.float32)

    mid = slice(top, top + height)
    own = slice(8, 8 + ph)
    local = [
        pltpu.make_async_copy(src, dst, sl_.at[i])
        for i, (src, dst) in enumerate((
            (plev_h, xlev.at[own, :]), (pflux_h, pfv), (pdep_h, xdep.at[own, :]), (wind_h, wv),
            (fd.at[0], dep.at[mid, :]), (fl.at[0], e.at[mid, :]), (ff.at[0], q.at[:, mid, :]),
        ))
    ]
    for c in local:
        c.start()

    pl.semaphore_wait(barrier, count)
    round_a = []
    n = 0
    for d in (1, -1):
        hown = slice(height - 8, height) if d == 1 else slice(0, 8)
        lown = slice(top + height - 8, top + height) if d == 1 else slice(top, top + 8)
        to = slice(top - 8, top) if d == 1 else slice(top + height, top + height + 8)
        pown = slice(ph - 8, ph) if d == 1 else slice(0, 8)
        pto = slice(0, 8) if d == 1 else slice(8 + ph, 16 + ph)
        slot = 0 if d == 1 else 2
        for src, dst in (
            (pws.at[:, :, :], pwb.at[:, slot * ph:(slot + 1) * ph, :]),
            (lim.at[lown, :], lim.at[to, :]),
            (fd.at[0, hown, :], dep.at[to, :]),
            (fl.at[0, hown, :], e.at[to, :]),
            (ff.at[0, :, hown, :], q.at[:, to, :]),
            (plev_h.at[pown, :], xlev.at[pto, :]),
            (pdep_h.at[pown, :], xdep.at[pto, :]),
            (pflux_h.at[1, pown, :], xuy.at[pto, :]),
            (wind_h.at[1, pown, :], xwy.at[pto, :]),
        ):
            round_a.append(Push(src, dst, sa.at[n], ra.at[n], k, d))
            n += 1
    round_a.append(Push(pws.at[:, :, :], pwb.at[:, 3 * ph:4 * ph, :], sa.at[n], ra.at[n], k, -2))
    fine_halo = round_a[1:5] + round_a[10:14]
    windows = [round_a[0], round_a[9], round_a[18]]
    parent_halo = round_a[5:9] + round_a[14:18]
    early = round_a[2:5] + round_a[11:14]
    for c in early:
        c.start()
    for c in small:
        c.wait()
    offset = jnp.where(k == 0, ins[0, 0], ins[1, 0])
    col_a = jnp.where(k == 0, ins[0, 1], ins[1, 1])
    col_b = jnp.where(k == 0, ins[1, 1], ins[0, 1])

    diag = iota((height, height), 0) == iota((height, height), 1)
    limit = jnp.sum(jnp.where(diag, shv[...].astype(jnp.float32), 0.0), axis=1, keepdims=True)
    r = iota((height, 128), 0)
    live = (r < exs[0, 0]) & (offset + t * (height // RATIO) + fdiv5(r) < ph * T)
    lim[top:top + height, :] = jnp.where(live, limit, FAR)

    lane512 = iota((pc, 128), 0)
    take = hot_of(lane512 == col_a + WIN + (iota((pc, 128), 1) & 31))
    for c in local[:4]:
        c.wait()
    plev, pdep = xlev[own, :], xdep[own, :]
    xuy[own, :] = pfv[1]
    xwy[own, :] = wv[1]
    stack = jnp.concatenate([plev, pfv[0], pfv[1], pdep, wv[0], wv[1]], axis=0)
    win = right_hot(stack, take, 3)
    group = iota((ph, 128), 1) >> 5
    pack0 = jnp.zeros((ph, 128), jnp.float32)
    pack1 = jnp.zeros((ph, 128), jnp.float32)
    for i in range(4):
        pack0 = jnp.where(group == i, win[i * ph:(i + 1) * ph], pack0)
    for i in range(2):
        pack1 = jnp.where(group == i, win[(4 + i) * ph:(5 + i) * ph], pack1)
    pws[0] = pack0
    pws[1] = pack1

    for c in [round_a[1], round_a[10]] + windows + parent_halo:
        c.start()

    zpad = jnp.zeros((8, breadth), jnp.float32)
    for s in (slice(0, 8), slice(rows - 8, rows)):
        e[s, :] = zpad
        dep[s, :] = zpad
        q[0, s, :] = zpad
        q[1, s, :] = zpad
        lim[s, :] = jnp.full((8, 128), FAR, jnp.float32)
    pwb[:, ph:2 * ph, :] = pws[...]

    colc = iota((CH, breadth), 1)
    last = colc == breadth - 1
    reps = breadth // 128

    def coefficients(r0):
        sl = slice(r0, r0 + CH)
        ss = slice(r0 + 1, r0 + CH + 1)
        colf = colc.astype(jnp.float32)
        wide = lambda s: jnp.concatenate([lim[s, :]] * reps, axis=1)
        act = jnp.where(colf >= wide(sl), 1.0, 0.0)
        act_s = jnp.where(colf >= wide(ss), 1.0, 0.0)
        d0 = dep[sl, :]
        fx = jnp.where(last, 0.0, act * shift_cols(act, -1))
        fxr[sl, :] = fx * RF
        cx[sl, :] = jnp.where(
            last, act * jnp.sqrt(d0), (DT_FINE * RF * 0.5) * fx * (d0 + shift_cols(d0, -1)))
        fy = act * act_s
        fyr[sl, :] = fy * RF
        cy[sl, :] = (DT_FINE * RF * 0.5) * fy * (d0 + dep[ss, :])

    local[4].wait()
    for r0 in range(8 + CH, rows - 8 - CH, CH):
        coefficients(r0)
    for c in local[5:]:
        c.wait()
    for c in fine_halo:
        c.arrive(FAR if c is round_a[1] or c is round_a[10] else 0.0)
    coefficients(8)
    coefficients(rows - 8 - CH)

    def window_step(we, wux, wuy):
        nx, ny = parent_step(we, wux, wuy, whx, why, wwx, wwy, w_col_open, w_row_open)
        ne = we - CP * (nx - shift_cols(nx, 1) + ny - shift_rows(ny, 1))
        return ne, nx, ny

    lane = iota((4 * ph, 128), 1)
    lane_f = iota((rows - 16, 128), 1)
    lev_at = 128 - WIN
    flux_at = 127 - WIN

    def set_sea(oe, oux, ne, nux):
        z = jnp.where(lane == 127, shift_cols(oe, 127 - lev_at), 0.0)
        z = jnp.where(lane == 126, shift_cols(oux, 126 - flux_at), z)
        z = jnp.where(lane == 125, shift_cols(ne, 125 - lev_at), z)
        z = jnp.where(lane == 124, shift_cols(nux, 124 - flux_at), z)
        s = left_hot(spread, z, 3)
        act = jnp.where(float(breadth - 1) >= lim[inner, :], 1.0, 0.0)
        cel = cx[inner, breadth - 128:]
        old = act * shift_cols(s, 1) - cel * s
        new = act * shift_cols(s, 3) - cel * shift_cols(s, 2)
        keep = lane_f == 127
        sea0[inner, :] = jnp.where(keep, old, 0.0)
        sead[inner, :] = jnp.where(keep, new - old, 0.0)

    def substep(step, carry):
        for r0 in range(8, rows - 8, CH):
            sl = slice(r0, r0 + CH)
            e0 = e[sl, :]
            east = jnp.where(last, 0.0, shift_cols(e0, -1))
            nx = fxr[sl, :] * q[0, sl, :] - cx[sl, :] * (east - e0)
            ny = fyr[sl, :] * q[1, sl, :] - cy[sl, :] * (e[slice(r0 + 1, r0 + CH + 1), :] - e0)
            q[0, sl, :] = nx
            q[1, sl, :] = ny
            west = jnp.where(colc == 0, 0.0, shift_cols(nx, 1))
            north = q[1, slice(r0 - 1, r0 + CH - 1), :]
            e[sl, :] = e0 - DT_FINE * (nx - west + ny - north)
        return carry

    edge = slice(breadth - 128, breadth)
    inner = slice(8, rows - 8)

    def all_but_edge():
        er[...] = e[:, edge]
        qr[...] = q[:, :, edge]
        lax.fori_loop(0, SUBSTEPS, substep, 0)

    def edge_columns():
        for n in range(SUBSTEPS):
            w = (n + 0.5) / SUBSTEPS
            e0 = er[inner, :]
            east = jnp.where(lane_f == 127, 0.0, shift_cols(e0, -1))
            sea = sea0[inner, :] + w * sead[inner, :]
            nx = fxr[inner, edge] * qr[0, inner, :] - cx[inner, edge] * (east - e0) + sea
            ny = fyr[inner, edge] * qr[1, inner, :] - cy[inner, edge] * (er[9:rows - 7, :] - e0)
            qr[0, inner, :] = nx
            qr[1, inner, :] = ny
            north = qr[1, 7:rows - 9, :]
            er[inner, :] = e0 - DT_FINE * (nx - shift_cols(nx, 1) + ny - north)
        keep = lane_f >= 64
        e[inner, edge] = jnp.where(keep, er[inner, :], e[inner, edge])
        for i in range(2):
            q[i, inner, edge] = jnp.where(keep, qr[i, inner, :], q[i, inner, edge])

    def restrict(with_count):
        colf = iota((height, breadth), 1).astype(jnp.float32)
        wet = colf >= jnp.concatenate([lim[mid, :]] * reps, axis=1)
        act = jnp.where(wet, 1.0, 0.0)
        part = [
            mm(rowsum, act.astype(jnp.bfloat16)),
            left_hot(rowsum, act * e[mid, :], 2),
            left_hot(rowsum, q[0, mid, :], 2),
            left_hot(rowsum, q[1, mid, :], 2),
        ]
        if not with_count:
            part = part[1:]
        return right_hot(jnp.concatenate(part, axis=0), colsum, 2)

    all_but_edge()

    prow = iota((32, height), 0)
    rowsum = hot_of(prow == offset + fdiv5(iota((32, height), 1)))
    colsum = hot_of(fdiv5(iota((breadth, 128), 0)) == iota((breadth, 128), 1))
    j128 = iota((128, 128), 0)
    l128 = iota((128, 128), 1) & 31
    pick_same = hot_of(j128 == WIN + l128)
    pick_other = hot_of(j128 == col_b - col_a + WIN + l128)
    place_a = hot_of(iota((128, pc), 1) == col_a + iota((128, pc), 0))
    place_b = hot_of(iota((128, pc), 1) == col_b + iota((128, pc), 0))
    spread = hot_of(
        iota((rows - 16, 4 * ph), 1)
        == ph + offset + fdiv5(iota((rows - 16, 4 * ph), 0) + 32) - 8
    )

    for c in windows:
        c.arrive()
    wrow = (t - 1) * ph + iota((4 * ph, 128), 0)
    wcol = col_a + WIN + iota((4 * ph, 128), 1)
    w_row_open = jnp.where((wrow >= 0) & (wrow < ph * T - 1), 1.0, 0.0)
    w_col_open = jnp.where(wcol < pc - 1, 1.0, 0.0)
    b0 = pwb[0]
    b1 = pwb[1]
    we, wux, wuy, wd = b0, shift_cols(b0, -32), shift_cols(b0, -64), shift_cols(b0, -96)
    wwx, wwy = b1, shift_cols(b1, -32)
    whx = 0.5 * (wd + shift_cols(wd, -1))
    why = 0.5 * (wd + shift_rows(wd, -1))

    n1e, n1x, n1y = window_step(we, wux, wuy)
    set_sea(we, wux, n1e, n1x)
    edge_columns()

    s1 = restrict(True)
    glane = iota((32, 128), 1) >> 5

    def packed(pick):
        res = right_hot(s1, pick, 2)
        out = res[0:32]
        for i in range(1, 4):
            out = jnp.where(glane == i, res[32 * i:32 * (i + 1)], out)
        return out

    pks[0] = packed(pick_same)
    pks[1] = packed(pick_other)
    round_b = []
    n = 0
    for nest, src, ds in ((ko, 1, (0, 1, -1, 2, -2)), (k, 0, (1, -1))):
        for d in ds:
            round_b.append(Push(pks.at[src], pkb.at[n], sb.at[n], rb.at[n], nest, d))
            n += 1
    for c in round_b:
        c.start()

    def full_pushes(src, dst, s_sem, r_sem):
        return [
            Push(src.at[:, 0:ph, :], dst.at[0], s_sem.at[0], r_sem.at[0], ko, 0),
            Push(src.at[:, ph:2 * ph, :], dst.at[1], s_sem.at[1], r_sem.at[1], k, 1),
            Push(src.at[:, ph:2 * ph, :], dst.at[2], s_sem.at[2], r_sem.at[2], ko, 1),
        ]

    for i in range(4):
        ss1[i] = s1[32 * i:32 * (i + 1)]
    round_c = full_pushes(ss1, fs1, sc, rc)
    for c in round_c:
        c.start()

    all_but_edge()

    for c in parent_halo:
        c.arrive()
    xn = 16 + ph
    grow = t * ph - 8 + iota((xn, pc), 0)
    row_open = jnp.where((grow >= 0) & (grow < ph * T - 1), 1.0, 0.0)
    gcol = iota((ph, pc), 1)
    col_open = jnp.where(gcol < pc - 1, 1.0, 0.0)
    xd = xdep[...]
    hy_p = 0.5 * (xd + shift_rows(xd, -1))
    d_own = pdep
    hx_p = 0.5 * (d_own + shift_cols(d_own, -1))

    def tile_step(xe, xu, ux):
        ny = row_open * (xu - CP * hy_p * (shift_rows(xe, -1) - xe) + DT_COARSE * xwy[...]) * RP
        eo = xe[8:8 + ph]
        nx = col_open * (ux - CP * hx_p * (shift_cols(eo, -1) - eo) + DT_COARSE * wv[0]) * RP
        west = jnp.where(gcol == 0, 0.0, shift_cols(nx, 1))
        north = shift_rows(ny, 1)[8:8 + ph]
        nyo = ny[8:8 + ph]
        return eo - CP * (nx - west + nyo - north), nx, nyo

    t1e, t1x, t1y = tile_step(xlev[...], xuy[...], pfv[0])

    for c in round_c:
        c.arrive()

    def spread_sums(own_top, fs, comps):
        mine = jnp.concatenate([own_top[i] + fs[1, i] for i in range(comps)], axis=0)
        theirs = jnp.concatenate([fs[0, i] + fs[2, i] for i in range(comps)], axis=0)
        both = right_hot(mine, place_a, 2) + right_hot(theirs, place_b, 2)
        both = both * (1.0 / (RATIO * RATIO))
        return [both[i * ph:(i + 1) * ph] for i in range(comps)]

    g = spread_sums([s1[32 * i:32 * i + ph] for i in range(4)], fs1, 4)
    retained = 1.0 - g[0]
    t1e = t1e * retained + g[1]
    t1x = t1x * retained + g[2]
    t1y = t1y * retained + g[3]
    p2s[0] = t1e
    p2s[1] = t1y
    round_d = [
        Push(p2s.at[:, ph - 8:ph, :], p2b.at[0], sd.at[0], rd.at[0], k, 1),
        Push(p2s.at[:, 0:8, :], p2b.at[1], sd.at[1], rd.at[1], k, -1),
    ]
    for c in round_d:
        c.start()
    for c in round_b:
        c.arrive()
    zero16 = jnp.zeros((ph, 128), jnp.float32)
    near = pkb[0] + pks[0]
    prev = pkb[1] + pkb[5]
    nxt = pkb[2] + pkb[6]
    sums = jnp.concatenate([
        prev[0:ph] + pkb[3][ph:2 * ph],
        near[0:ph] + prev[ph:2 * ph],
        nxt[0:ph] + near[ph:2 * ph],
        pkb[4][0:ph] + nxt[ph:2 * ph],
    ], axis=0) * (1.0 / (RATIO * RATIO))
    keep = 1.0 - sums
    u1e = n1e * keep + shift_cols(sums, -32)
    u1x = n1x * keep + shift_cols(sums, -64)
    u1y = n1y * keep + shift_cols(sums, -96)
    n2e, n2x, _ = window_step(u1e, u1x, u1y)
    set_sea(u1e, u1x, n2e, n2x)
    edge_columns()

    s2 = restrict(False)
    for i in range(3):
        ss2[i] = s2[32 * i:32 * (i + 1)]
    round_e = full_pushes(ss2, fs2, se, re_)
    for c in round_e:
        c.start()
    fl_out[0] = e[mid, :]
    ff_out[0] = q[:, mid, :]
    for c in round_d:
        c.arrive()
    t2e, t2x, t2y = tile_step(
        jnp.concatenate([p2b[0, 0], t1e, p2b[1, 0]], axis=0),
        jnp.concatenate([p2b[0, 1], t1y, p2b[1, 1]], axis=0),
        t1x,
    )
    for c in round_e:
        c.arrive()
    g = spread_sums([s2[32 * i:32 * i + ph] for i in range(3)], fs2, 3)
    pl_out[...] = t2e * retained + g[0]
    pf_out[0] = t2x * retained + g[1]
    pf_out[1] = t2y * retained + g[2]
    for c in round_a + round_b + round_c + round_d + round_e:
        c.sent()


def store(*refs):
    outs = [pltpu.make_async_copy(refs[i], refs[4 + i], refs[8].at[i]) for i in range(4)]
    for i in (1, 0, 3, 2):
        outs[i].start()
    for c in outs:
        c.wait()


def on_device(fl, ff, fd, shore, ext, inter, plev, pflux, pdep, wind):
    _, height, breadth = fl.shape
    ph, pc = plev.shape
    T = lax.axis_size("tile")
    rows = height + 32
    f32 = jnp.float32
    fine = pltpu.VMEM((rows, breadth), f32)
    strip = pltpu.VMEM((rows, 128), f32)
    ext_p = pltpu.VMEM((ph + 16, pc), f32)
    dma = pltpu.SemaphoreType.DMA
    vm = pl.BlockSpec(memory_space=pltpu.VMEM)
    hb = pl.BlockSpec(memory_space=pltpu.HBM)
    outs = pl.pallas_call(
        functools.partial(kernel, T, height, breadth, ph, pc),
        out_shape=[pltpu.VMEM(x.shape, f32) for x in (fl, ff, plev, pflux)],
        in_specs=[hb] * 10,
        out_specs=[vm] * 4,
        scratch_shapes=[
            fine, pltpu.VMEM((2, rows, breadth), f32), fine, strip,
            fine, fine, fine, fine, strip, strip, strip, pltpu.VMEM((2, rows, 128), f32),
            pltpu.VMEM((2, ph, pc), f32), pltpu.VMEM((2, ph, pc), f32),
            pltpu.VMEM((1, height), jnp.int32), pltpu.SMEM((1, 1), jnp.int32), pltpu.SMEM((2, 2), jnp.int32),
            ext_p, ext_p, ext_p, ext_p,
            pltpu.VMEM((2, ph, 128), f32), pltpu.VMEM((2, 4 * ph, 128), f32),
            pltpu.VMEM((2, 2 * ph, 128), f32), pltpu.VMEM((7, 2 * ph, 128), f32),
            pltpu.VMEM((4, 2 * ph, 128), f32), pltpu.VMEM((3, 4, ph, 128), f32),
            pltpu.VMEM((3, 2 * ph, 128), f32), pltpu.VMEM((3, 3, ph, 128), f32),
            pltpu.VMEM((2, ph, pc), f32), pltpu.VMEM((2, 2, 8, pc), f32),
            dma((19,)), dma((19,)), dma((7,)), dma((7,)), dma((3,)), dma((3,)),
            dma((2,)), dma((2,)), dma((3,)), dma((3,)), dma((10,)),
        ],
        compiler_params=pltpu.CompilerParams(
            collective_id=0, has_side_effects=True, vmem_limit_bytes=48 * 1024 * 1024),
        name="nested",
    )(*[pltpu.with_memory_space_constraint(x, pltpu.HBM) if x is not ext else x for x in (fl, ff, fd, shore, ext, inter, plev, pflux, pdep, wind)])
    return pl.pallas_call(
        store,
        out_shape=[jax.ShapeDtypeStruct(x.shape, f32) for x in (fl, ff, plev, pflux)],
        in_specs=[vm] * 4,
        out_specs=[hb] * 4,
        scratch_shapes=[dma((4,))],
        compiler_params=pltpu.CompilerParams(vmem_limit_bytes=48 * 1024 * 1024),
        name="store",
    )(*outs)


def solution(mesh):
    in_specs = (
        P("nest", "tile", None),
        P("nest", None, "tile", None),
        P("nest", "tile", None),
        P("nest", "tile"),
        P("nest", "tile"),
        P(),
        P("tile", None),
        P(None, "tile", None),
        P("tile", None),
        P(None, "tile", None),
    )
    out_specs = (
        P("nest", "tile", None),
        P("nest", None, "tile", None),
        P("tile", None),
        P(None, "tile", None),
    )
    return jax.shard_map(
        on_device, mesh=mesh, in_specs=in_specs, out_specs=out_specs, check_vma=False
    )
```

```python
import functools

import jax
import jax.numpy as jnp
from jax import lax
from jax.experimental import pallas as pl
from jax.experimental.pallas import tpu as pltpu
from jax.sharding import PartitionSpec as P

RATIO = 5
SUBSTEPS = 4
DT_FINE = 0.4
DT_COARSE = 1.6
DX_COARSE = 5.0
FRICTION = 0.05
RF = 1.0 / (1.0 + DT_FINE * FRICTION)
RP = 1.0 / (1.0 + DT_COARSE * FRICTION)
CP = DT_COARSE / DX_COARSE
FAR = 1.0e6
WIN = 112
CH = 16


def parts_of(x, n):
    out = []
    for _ in range(n):
        hi = x.astype(jnp.bfloat16)
        out.append(hi)
        x = x - hi.astype(jnp.float32)
    return out


def mm(a, b):
    return lax.dot_general(a, b, (((1,), (0,)), ((), ())), preferred_element_type=jnp.float32)


def left_hot(hot, x, n):
    return sum(mm(hot, p) for p in parts_of(x, n))


def right_hot(x, hot, n):
    return sum(mm(p, hot) for p in parts_of(x, n))


def hot_of(mask):
    return jnp.where(mask, 1.0, 0.0).astype(jnp.bfloat16)


def iota(shape, axis):
    return lax.broadcasted_iota(jnp.int32, shape, axis)


def fdiv5(x):
    return jnp.floor((x.astype(jnp.float32) + 0.5) * 0.2).astype(jnp.int32)


def shift_rows(x, by):
    return pltpu.roll(x, by % x.shape[0], 0)


def shift_cols(x, by):
    return pltpu.roll(x, by % x.shape[1], 1)


def parent_step(e, ux, uy, hx, hy, wx, wy, col_open, row_open):
    nx = col_open * (ux - CP * hx * (shift_cols(e, -1) - e) + DT_COARSE * wx) * RP
    ny = row_open * (uy - CP * hy * (shift_rows(e, -1) - e) + DT_COARSE * wy) * RP
    return nx, ny


def kernel(
    T, height, breadth, ph, pc,
    fl, ff, fd, shore, ext, inter, plev_h, pflux_h, pdep_h, wind_h,
    fl_out, ff_out, pl_out, pf_out,
    e, q, dep, lim, fxr, cx, fyr, cy, sea0, sead, er, qr, be, bq,
    plv, pfv, pdv, wv, shv, exs, ins, pws, pwb, hs, hr, pks, pkb,
    cs, c0a, c0b, c1, es, e0a, e0b, e1, gs, g0a, g0b, g1,
    ssem, rsem, lsem,
):
    k = lax.axis_index("nest")
    t = lax.axis_index("tile")
    ko = 1 - k
    top = 16
    rows = height + 32
    mid = slice(top, top + height)
    inner = slice(8, rows - 8)
    edge = slice(breadth - 128, breadth)
    halo_n = slice(top - 8, top)
    halo_s = slice(top + height, top + height + 8)

    def have(d):
        return (t + d >= 0) & (t + d < T)

    locals_ = [
        pltpu.make_async_copy(src, dst, lsem.at[i])
        for i, (src, dst) in enumerate((
            (shore, shv), (ext, exs), (inter, ins),
            (plev_h, plv), (pflux_h, pfv), (pdep_h, pdv), (wind_h, wv),
            (fd.at[0], dep.at[mid, :]), (fl.at[0], e.at[mid, :]), (ff.at[0], q.at[:, mid, :]),
        ))
    ]
    for c in locals_:
        c.start()

    for buf in (pwb, pkb, c0a, c0b, c1, e0a, e0b, e1, g0a, g0b, g1, hr):
        buf[...] = jnp.zeros(buf.shape, jnp.float32)
    zrow = jnp.zeros((8, breadth), jnp.float32)
    far = jnp.full((8, 128), FAR, jnp.float32)
    for missing, s, b, bs in ((-1, halo_n, 0, slice(8, 16)), (1, halo_s, 1, slice(24, 32))):
        @pl.when(jnp.logical_not(have(missing)))
        def _():
            dep[s, :] = zrow
            lim[s, :] = far
            be[b, bs, :] = zrow
            bq[b, 0, bs, :] = zrow
            bq[b, 1, bs, :] = zrow

    barrier = pltpu.get_barrier_semaphore()

    def greet(nest, d, only=None):
        ok = have(d)
        if only is not None:
            ok = ok & (k == only)

        @pl.when(ok)
        def _():
            pl.semaphore_signal(barrier, inc=1, device_id=(nest, t + d), device_id_type=pl.DeviceIdType.MESH)

    def expect(d, only=None):
        ok = have(d)
        if only is not None:
            ok = ok & (k == only)
        return ok.astype(jnp.int32)

    for d in (1, -1):
        greet(k, d)
    greet(ko, 0)
    greet(ko, -1)
    greet(k, 2, 0)
    greet(ko, 1, 0)
    greet(ko, 2, 0)
    greet(ko, -2, 1)
    count = (expect(1) + expect(-1) + 1 + expect(1) + expect(-2, 0) + expect(2, 0)
             + expect(-1, 1) + expect(-2, 1))

    pushes = []

    class Push:
        def __init__(self, src, dst, same, d, only=None):
            n = len(pushes)
            pushes.append(self)
            self.go, self.come = have(d), have(-d)
            if only is not None:
                self.go = self.go & (k == only)
                self.come = self.come & (k == (only if same else 1 - only))
            self.c = pltpu.make_async_remote_copy(
                src_ref=src, dst_ref=dst, send_sem=ssem.at[n], recv_sem=rsem.at[n],
                device_id=(k if same else ko, t + d), device_id_type=pl.DeviceIdType.MESH)

        def start(self):
            pl.when(self.go)(lambda: self.c.start())

        def sent(self):
            pl.when(self.go)(lambda: self.c.wait_send())

        def arrive(self):
            pl.when(self.come)(lambda: self.c.wait_recv())

    def start(group):
        for c in group:
            c.start()
        return group

    def arrive(group):
        for c in group:
            c.arrive()

    pl.semaphore_wait(barrier, count)
    halo = []
    for d in (1, -1):
        own = slice(height - 8, height) if d == 1 else slice(0, 8)
        to = halo_n if d == 1 else halo_s
        b, bs = (0, slice(8, 16)) if d == 1 else (1, slice(24, 32))
        halo += [
            Push(fd.at[0, own, :], dep.at[to, :], True, d),
            Push(fl.at[0, own, :], be.at[b, bs, :], True, d),
            Push(ff.at[0, :, own, :], bq.at[b, :, bs, :], True, d),
        ]
    start(halo)

    for c in locals_[:3]:
        c.wait()
    offset = jnp.where(k == 0, ins[0, 0], ins[1, 0])
    col_a = jnp.where(k == 0, ins[0, 1], ins[1, 1])
    col_b = jnp.where(k == 0, ins[1, 1], ins[0, 1])

    diag = iota((height, height), 0) == iota((height, height), 1)
    limit = jnp.sum(jnp.where(diag, shv[...].astype(jnp.float32), 0.0), axis=1, keepdims=True)
    r = iota((height, 128), 0)
    live = (r < exs[0, 0]) & (offset + t * (height // RATIO) + fdiv5(r) < ph * T)
    lim[mid, :] = jnp.where(live, limit, FAR)
    limits = [
        Push(lim.at[top + height - 8:top + height, :], lim.at[halo_n, :], True, 1),
        Push(lim.at[top:top + 8, :], lim.at[halo_s, :], True, -1),
    ]
    start(limits)

    take = hot_of(iota((pc, 128), 0) == col_a + WIN + (iota((pc, 128), 1) & 31))
    for c in locals_[3:7]:
        c.wait()
    parent = [plv[...], pdv[...], pfv[1], pfv[0], wv[0], wv[1]]
    stack = jnp.concatenate([parent[0], parent[3], parent[2], parent[1], parent[4], parent[5]], axis=0)
    win = right_hot(stack, take, 3)
    group = iota((ph, 128), 1) >> 5
    pack0 = jnp.zeros((ph, 128), jnp.float32)
    pack1 = jnp.zeros((ph, 128), jnp.float32)
    for i in range(4):
        pack0 = jnp.where(group == i, win[i * ph:(i + 1) * ph], pack0)
    for i in range(2):
        pack1 = jnp.where(group == i, win[(4 + i) * ph:(5 + i) * ph], pack1)
    pws[0] = pack0
    pws[1] = pack1
    windows = [
        Push(pws.at[:, 8:ph, :], pwb.at[:, 8:ph, :], True, 1),
        Push(pws.at[:, :, :], pwb.at[:, 2 * ph:3 * ph, :], True, -1),
        Push(pws.at[:, 0:8, :], pwb.at[:, 3 * ph:3 * ph + 8, :], True, -2, 0),
    ]
    start(windows)
    pwb[:, ph:2 * ph, :] = pws[...]

    pair = iota((8, pc), 0) >> 1
    for at, tile, first in ((0, slice(ph - 8, ph), 2), (1, slice(0, 8), 0)):
        for part, members in ((0, parent[:4]), (1, parent[4:])):
            out = jnp.zeros((8, pc), jnp.float32)
            for i, x in enumerate(members):
                out = jnp.where(pair == i, shift_rows(x[tile], 2 * i + first), out)
            hs[at, 8 * part:8 * part + 8, :] = out
    parent_halo = [
        Push(hs.at[0], hr.at[0], True, 1),
        Push(hs.at[1], hr.at[1], True, -1),
    ]
    start(parent_halo)

    for s in (slice(0, 8), slice(rows - 8, rows)):
        e[s, :] = zrow
        dep[s, :] = zrow
        q[0, s, :] = zrow
        q[1, s, :] = zrow
        lim[s, :] = far
        er[s, :] = zrow[:, :128]
        qr[0, s, :] = zrow[:, :128]
        qr[1, s, :] = zrow[:, :128]
    for b in range(2):
        for s in (slice(0, 8), slice(32, 40)):
            be[b, s, :] = zrow
            bq[b, 1, s, :] = zrow

    colc = iota((CH, breadth), 1)
    last = colc == breadth - 1
    reps = breadth // 128

    def coefficients(r0):
        sl = slice(r0, r0 + CH)
        ss = slice(r0 + 1, r0 + CH + 1)
        colf = colc.astype(jnp.float32)
        wide = lambda s: jnp.concatenate([lim[s, :]] * reps, axis=1)
        act = jnp.where(colf >= wide(sl), 1.0, 0.0)
        act_s = jnp.where(colf >= wide(ss), 1.0, 0.0)
        d0 = dep[sl, :]
        fx = jnp.where(last, 0.0, act * shift_cols(act, -1))
        fxr[sl, :] = fx * RF
        cx[sl, :] = jnp.where(
            last, act * jnp.sqrt(d0), (DT_FINE * RF * 0.5) * fx * (d0 + shift_cols(d0, -1)))
        fy = act * act_s
        fyr[sl, :] = fy * RF
        cy[sl, :] = (DT_FINE * RF * 0.5) * fy * (d0 + dep[ss, :])

    def advance(ef, qf, r0, n, off):
        sl = slice(r0, r0 + n)
        co = slice(r0 + off, r0 + off + n)
        col = iota((n, breadth), 1)
        e0 = ef[sl, :]
        east = jnp.where(col == breadth - 1, 0.0, shift_cols(e0, -1))
        nx = fxr[co, :] * qf[0, sl, :] - cx[co, :] * (east - e0)
        ny = fyr[co, :] * qf[1, sl, :] - cy[co, :] * (ef[r0 + 1:r0 + n + 1, :] - e0)
        qf[0, sl, :] = nx
        qf[1, sl, :] = ny
        west = jnp.where(col == 0, 0.0, shift_cols(nx, 1))
        north = qf[1, r0 - 1:r0 + n - 1, :]
        ef[sl, :] = e0 - DT_FINE * (nx - west + ny - north)

    locals_[7].wait()
    for r0 in range(8 + CH, rows - 8 - CH, CH):
        coefficients(r0)
    for c in locals_[8:]:
        c.wait()
    be[0, 16:32, :] = e[top:top + 16, :]
    be[1, 8:24, :] = e[top + height - 16:top + height, :]
    er[mid, :] = e[mid, edge]
    for i in range(2):
        bq[0, i, 16:32, :] = q[i, top:top + 16, :]
        bq[1, i, 8:24, :] = q[i, top + height - 16:top + height, :]
        qr[i, mid, :] = q[i, mid, edge]

    def inside(step, carry):
        for r0 in range(8 + CH, rows - 8 - CH, CH):
            advance(e, q, r0, CH, 0)
        return carry

    lax.fori_loop(0, SUBSTEPS, inside, 0)

    lane = iota((4 * ph, 128), 1)
    lane_f = iota((rows - 16, 128), 1)
    lev_at = 128 - WIN
    flux_at = 127 - WIN
    rowsum = hot_of(iota((32, height), 0) == offset + fdiv5(iota((32, height), 1)))
    l32 = iota((128, 128), 1) & 31
    sum_same = hot_of(fdiv5(iota((128, 128), 0) + (breadth - 128)) == WIN + l32)
    begin = 0
    for s in range(128, breadth - 255, 128):
        begin = jnp.where(RATIO * (col_b - col_a + 127) >= s, s, begin)
    sum_other = hot_of(
        fdiv5(iota((256, 128), 0) + begin) == col_b - col_a + WIN + (iota((256, 128), 1) & 31))
    spread = hot_of(
        iota((rows - 16, 4 * ph), 1)
        == ph + offset + fdiv5(iota((rows - 16, 4 * ph), 0) + 32) - 8
    )
    wrow = (t - 1) * ph + iota((4 * ph, 128), 0)
    wcol = col_a + WIN + iota((4 * ph, 128), 1)
    w_row_open = jnp.where((wrow >= 0) & (wrow < ph * T - 1), 1.0, 0.0)
    w_col_open = jnp.where(wcol < pc - 1, 1.0, 0.0)

    arrive(halo)
    arrive(limits)
    arrive(windows)

    er[halo_n, :] = be[0, 8:16, edge]
    er[halo_s, :] = be[1, 24:32, edge]
    for i in range(2):
        qr[i, halo_n, :] = bq[0, i, 8:16, edge]
        qr[i, halo_s, :] = bq[1, i, 24:32, edge]
    coefficients(8)
    coefficients(rows - 8 - CH)

    b0 = pwb[0]
    b1 = pwb[1]
    we, wux, wuy, wd = b0, shift_cols(b0, -32), shift_cols(b0, -64), shift_cols(b0, -96)
    wwx, wwy = b1, shift_cols(b1, -32)
    whx = 0.5 * (wd + shift_cols(wd, -1))
    why = 0.5 * (wd + shift_rows(wd, -1))

    def window_step(we, wux, wuy):
        nx, ny = parent_step(we, wux, wuy, whx, why, wwx, wwy, w_col_open, w_row_open)
        ne = we - CP * (nx - shift_cols(nx, 1) + ny - shift_rows(ny, 1))
        return ne, nx, ny

    def set_sea(oe, oux, ne, nux):
        z = jnp.where(lane == 127, shift_cols(oe, 127 - lev_at), 0.0)
        z = jnp.where(lane == 126, shift_cols(oux, 126 - flux_at), z)
        z = jnp.where(lane == 125, shift_cols(ne, 125 - lev_at), z)
        z = jnp.where(lane == 124, shift_cols(nux, 124 - flux_at), z)
        s = left_hot(spread, z, 3)
        act = jnp.where(float(breadth - 1) >= lim[inner, :], 1.0, 0.0)
        cel = cx[inner, breadth - 128:]
        old = act * shift_cols(s, 1) - cel * s
        new = act * shift_cols(s, 3) - cel * shift_cols(s, 2)
        keep = lane_f == 127
        sea0[inner, :] = jnp.where(keep, old, 0.0)
        sead[inner, :] = jnp.where(keep, new - old, 0.0)

    def edge_columns():
        for n in range(SUBSTEPS):
            w = (n + 0.5) / SUBSTEPS
            e0 = er[inner, :]
            east = jnp.where(lane_f == 127, 0.0, shift_cols(e0, -1))
            sea = sea0[inner, :] + w * sead[inner, :]
            nx = fxr[inner, edge] * qr[0, inner, :] - cx[inner, edge] * (east - e0) + sea
            ny = fyr[inner, edge] * qr[1, inner, :] - cy[inner, edge] * (er[9:rows - 7, :] - e0)
            qr[0, inner, :] = nx
            qr[1, inner, :] = ny
            north = qr[1, 7:rows - 9, :]
            er[inner, :] = e0 - DT_FINE * (nx - shift_cols(nx, 1) + ny - north)

    def merge_edge(where):
        n = where.stop - where.start
        keep = iota((n, 128), 1) >= 64
        e[where, edge] = jnp.where(keep, er[where, :], e[where, edge])
        for i in range(2):
            q[i, where, edge] = jnp.where(keep, qr[i, where, :], q[i, where, edge])

    for n in range(SUBSTEPS):
        for r0 in (8, 16, 24):
            advance(be.at[0], bq.at[0], r0, 8, 0)
            advance(be.at[1], bq.at[1], r0, 8, rows - 40)
    r8 = iota((8, breadth), 0)
    for dst, bnd in ((e, lambda b: be.at[b]), (q.at[0], lambda b: bq.at[b, 0]), (q.at[1], lambda b: bq.at[b, 1])):
        dst[8:24, :] = bnd(0)[8:24, :]
        dst[24:32, :] = jnp.where(r8 < 4, bnd(0)[24:32, :], dst[24:32, :])
        dst[rows - 32:rows - 24, :] = jnp.where(r8 >= 4, bnd(1)[8:16, :], dst[rows - 32:rows - 24, :])
        dst[rows - 24:rows - 8, :] = bnd(1)[16:32, :]

    n1e, n1x, n1y = window_step(we, wux, wuy)
    set_sea(we, wux, n1e, n1x)
    edge_columns()
    merge_edge(inner)

    glane = iota((32, 128), 1) >> 5

    def packed(res, n):
        out = res[0:32]
        for i in range(1, n):
            out = jnp.where(glane == i, res[32 * i:32 * (i + 1)], out)
        return out

    def wet(width, start):
        colf = (iota((height, width), 1) + start).astype(jnp.float32)
        return jnp.where(colf >= jnp.concatenate([lim[mid, :]] * (width // 128), axis=1), 1.0, 0.0)

    def restrict(act, lev, qx, qy, columns, with_count):
        part = [
            left_hot(rowsum, act * lev, 2),
            left_hot(rowsum, qx, 2),
            left_hot(rowsum, qy, 2),
        ]
        if with_count:
            part = [mm(rowsum, act.astype(jnp.bfloat16))] + part
        return right_hot(jnp.concatenate(part, axis=0), columns, 2)

    pks[0] = packed(restrict(wet(128, breadth - 128), er[mid, :], qr[0, mid, :], qr[1, mid, :], sum_same, True), 4)

    def there(ref):
        out = ref[mid, 0:256]
        for s in range(128, breadth - 255, 128):
            out = jnp.where(begin == s, ref[mid, s:s + 256], out)
        return out

    pks[1] = packed(restrict(wet(256, begin), there(e), there(q.at[0]), there(q.at[1]), sum_other, True), 4)
    near = start([
        Push(pks.at[1], pkb.at[0], False, 0),
        Push(pks.at[1, 8:32, :], pkb.at[1, 8:32, :], False, 1),
        Push(pks.at[1, 0:16, :], pkb.at[2, 0:16, :], False, -1, 1),
        Push(pks.at[1, 24:32, :], pkb.at[3, 24:32, :], False, 2, 0),
        Push(pks.at[1, 0:8, :], pkb.at[4, 0:8, :], False, -2, 1),
        Push(pks.at[0, 8:32, :], pkb.at[5, 8:32, :], True, 1),
        Push(pks.at[0, 0:24, :], pkb.at[6, 0:24, :], True, -1),
    ])

    colsum = hot_of(fdiv5(iota((breadth, 128), 0)) == iota((breadth, 128), 1))
    s1 = restrict(wet(breadth, 0), e[mid, :], q[0, mid, :], q[1, mid, :], colsum, True)
    for i in range(4):
        cs[i] = s1[32 * i:32 * (i + 1)]

    sums1 = start([
        Push(cs.at[:, 0:24, :], c0a.at[:, 8:32, :], False, 0, 0),
        Push(cs.at[:, 0:16, :], c1.at[:, 8:24, :], False, 0, 1),
        Push(cs.at[:, 8:32, :], c0b.at[:, 0:24, :], True, 1, 0),
        Push(cs.at[:, 8:32, :], c0b.at[:, 0:24, :], False, 1, 0),
        Push(cs.at[:, 8:16, :], c1.at[:, 0:8, :], True, 1, 1),
        Push(cs.at[:, 8:16, :], c1.at[:, 0:8, :], False, 1, 1),
        Push(cs.at[:, 0:8, :], c1.at[:, 24:32, :], True, -1, 1),
        Push(cs.at[:, 0:8, :], c1.at[:, 24:32, :], False, -1, 1),
    ])

    er[...] = e[:, edge]
    qr[...] = q[:, :, edge]

    def everywhere(step, carry):
        for r0 in range(8, rows - 8, CH):
            advance(e, q, r0, CH, 0)
        return carry

    lax.fori_loop(0, SUBSTEPS, everywhere, 0)

    bulk = hot_of((fdiv5(iota((breadth, 128), 0)) == iota((breadth, 128), 1)) & (iota((breadth, 128), 1) < breadth // RATIO - 1))
    s2 = restrict(wet(breadth, 0), e[mid, :], q[0, mid, :], q[1, mid, :], bulk, False)
    for i in range(3):
        es[i] = s2[32 * i:32 * (i + 1)]

    def final_sums(src, a0, b0, one, idx):
        return start([
            Push(src.at[idx(0)], a0, False, 0, 0),
            Push(src.at[idx(0)], one, False, 0, 1),
            Push(src.at[idx(1)], b0, True, 1, 0),
            Push(src.at[idx(1)], b0, False, 1, 0),
        ])

    sums2 = final_sums(es, e0a, e0b, e1, lambda i: (slice(None), slice(ph * i, ph * (i + 1)), slice(None)))

    xn = 16 + ph
    grow = t * ph - 8 + iota((xn, pc), 0)
    row_open = jnp.where((grow >= 0) & (grow < ph * T - 1), 1.0, 0.0)
    gcol = iota((xn, pc), 1)
    col_open = jnp.where(gcol < pc - 1, 1.0, 0.0)
    col_0 = jnp.where(k == 0, col_a, col_b)
    col_1 = jnp.where(k == 0, col_b, col_a)
    place_0 = hot_of(iota((128, pc), 1) == col_0 + iota((128, pc), 0))
    place_1 = hot_of(iota((128, pc), 1) == col_1 + iota((128, pc), 0))

    arrive(near)
    beside = pkb[0] + pks[0]
    prev = pkb[1] + pkb[5]
    nxt = pkb[2] + pkb[6]
    sums = jnp.concatenate([
        prev[0:ph] + pkb[3][ph:2 * ph],
        beside[0:ph] + prev[ph:2 * ph],
        nxt[0:ph] + beside[ph:2 * ph],
        pkb[4][0:ph] + nxt[ph:2 * ph],
    ], axis=0) * (1.0 / (RATIO * RATIO))
    keep = 1.0 - sums
    u1e = n1e * keep + shift_cols(sums, -32)
    u1x = n1x * keep + shift_cols(sums, -64)
    u1y = n1y * keep + shift_cols(sums, -96)
    n2e, n2x, _ = window_step(u1e, u1x, u1y)
    set_sea(u1e, u1x, n2e, n2x)
    edge_columns()

    sum_last = hot_of(iota((128, 128), 0) >= 128 - RATIO)
    gs[...] = packed(restrict(wet(128, breadth - 128), er[mid, :], qr[0, mid, :], qr[1, mid, :], sum_last, False), 3)
    sums3 = final_sums(gs, g0a, g0b, g1, lambda i: (slice(ph * i, ph * (i + 1)), slice(None)))

    merge_edge(mid)
    fl_out[0] = e[mid, :]
    ff_out[0] = q[:, mid, :]

    arrive(parent_halo)

    def extended(own, i):
        part, j = (0, i) if i < 4 else (8, i - 4)
        return jnp.concatenate([
            shift_rows(hr[0, part:part + 8, :], 6 - 2 * j), own, shift_rows(hr[1, part:part + 8, :], -2 * j)], axis=0)

    xe, xd, xuy, xux, xwx, xwy = [
        extended(x, i) for i, x in enumerate((plv[...], pdv[...], pfv[1], pfv[0], wv[0], wv[1]))]
    hx_p = 0.5 * (xd + shift_cols(xd, -1))
    hy_p = 0.5 * (xd + shift_rows(xd, -1))

    def tile_step(xe, ux, uy):
        nx, ny = parent_step(xe, ux, uy, hx_p, hy_p, xwx, xwy, col_open, row_open)
        west = jnp.where(gcol == 0, 0.0, shift_cols(nx, 1))
        return xe - CP * (nx - west + ny - shift_rows(ny, 1)), nx, ny

    t1e, t1x, t1y = tile_step(xe, xux, xuy)

    arrive(sums1)

    @pl.when(k == 0)
    def _():
        c0a[:, 8:32, :] = cs[:, 0:24, :]

    @pl.when(k == 1)
    def _():
        c1[:, 8:24, :] = cs[:, 0:16, :]

    def spread_sums(a0, b0, one, comps):
        nest0 = jnp.concatenate([a0[i] + b0[i] for i in range(comps)], axis=0)
        nest1 = jnp.concatenate([one[i] for i in range(comps)], axis=0)
        both = right_hot(nest0, place_0, 2) + right_hot(nest1, place_1, 2)
        both = both * (1.0 / (RATIO * RATIO))
        n = both.shape[0] // comps
        return [both[i * n:(i + 1) * n] for i in range(comps)]

    g = spread_sums(c0a, c0b, c1, 4)
    retained = 1.0 - g[0]
    t2 = tile_step(t1e * retained + g[1], t1x * retained + g[2], t1y * retained + g[3])
    own_p = slice(8, 8 + ph)
    held = retained[own_p]

    arrive(sums2)

    @pl.when(k == 0)
    def _():
        e0a[...] = es[:, 0:ph, :]
        g0a[...] = gs[0:ph, :]

    @pl.when(k == 1)
    def _():
        e1[...] = es[:, 0:ph, :]
        g1[...] = gs[0:ph, :]

    g = spread_sums(e0a, e0b, e1, 3)
    base = [t2[i][own_p] * held + g[i] for i in range(3)]
    at_0 = gcol[own_p] == col_0 + (breadth // RATIO - 1)
    at_1 = gcol[own_p] == col_1 + (breadth // RATIO - 1)
    arrive(sums3)
    z0 = (g0a[...] + g0b[...]) * (1.0 / (RATIO * RATIO))
    z1 = g1[...] * (1.0 / (RATIO * RATIO))
    outs = []
    for i in range(3):
        v0 = jnp.broadcast_to(z0[:, 32 * i:32 * i + 1], (ph, pc))
        v1 = jnp.broadcast_to(z1[:, 32 * i:32 * i + 1], (ph, pc))
        outs.append(base[i] + jnp.where(at_0, v0, 0.0) + jnp.where(at_1, v1, 0.0))
    pl_out[...] = outs[0]
    pf_out[0] = outs[1]
    pf_out[1] = outs[2]
    for c in pushes:
        c.sent()


def store(*refs):
    outs = [pltpu.make_async_copy(refs[i], refs[4 + i], refs[8].at[i]) for i in range(4)]
    for i in (1, 0, 3, 2):
        outs[i].start()
    for c in outs:
        c.wait()


def on_device(fl, ff, fd, shore, ext, inter, plev, pflux, pdep, wind):
    _, height, breadth = fl.shape
    ph, pc = plev.shape
    T = lax.axis_size("tile")
    rows = height + 32
    f32 = jnp.float32

    def vmem(*shape):
        return pltpu.VMEM(shape, f32)

    fine, strip = vmem(rows, breadth), vmem(rows, 128)
    dma = pltpu.SemaphoreType.DMA
    vm = pl.BlockSpec(memory_space=pltpu.VMEM)
    hb = pl.BlockSpec(memory_space=pltpu.HBM)
    pin = lambda x: pltpu.with_memory_space_constraint(x, pltpu.HBM)
    outs = pl.pallas_call(
        functools.partial(kernel, T, height, breadth, ph, pc),
        out_shape=[pltpu.VMEM(x.shape, f32) for x in (fl, ff, plev, pflux)],
        in_specs=[hb] * 10,
        out_specs=[vm] * 4,
        scratch_shapes=[
            fine, vmem(2, rows, breadth), fine, strip,
            fine, fine, fine, fine, strip, strip, strip, vmem(2, rows, 128),
            vmem(2, 40, breadth), vmem(2, 2, 40, breadth),
            vmem(ph, pc), vmem(2, ph, pc), vmem(ph, pc), vmem(2, ph, pc),
            pltpu.VMEM((1, height), jnp.int32), pltpu.SMEM((1, 1), jnp.int32), pltpu.SMEM((2, 2), jnp.int32),
            vmem(2, ph, 128), vmem(2, 4 * ph, 128), vmem(2, 16, pc), vmem(2, 16, pc),
            vmem(2, 2 * ph, 128), vmem(7, 2 * ph, 128),
            vmem(4, 2 * ph, 128), vmem(4, 2 * ph, 128), vmem(4, 2 * ph, 128), vmem(4, 2 * ph, 128),
            vmem(3, 2 * ph, 128), vmem(3, ph, 128), vmem(3, ph, 128), vmem(3, ph, 128),
            vmem(2 * ph, 128), vmem(ph, 128), vmem(ph, 128), vmem(ph, 128),
            dma((36,)), dma((36,)), dma((10,)),
        ],
        compiler_params=pltpu.CompilerParams(
            collective_id=0, has_side_effects=True, vmem_limit_bytes=48 * 1024 * 1024),
        name="nested",
    )(pin(fl), pin(ff), pin(fd), pin(shore), ext, pin(inter), pin(plev), pin(pflux), pin(pdep), pin(wind))
    return pl.pallas_call(
        store,
        out_shape=[jax.ShapeDtypeStruct(x.shape, f32) for x in (fl, ff, plev, pflux)],
        in_specs=[vm] * 4,
        out_specs=[hb] * 4,
        scratch_shapes=[dma((4,))],
        compiler_params=pltpu.CompilerParams(vmem_limit_bytes=48 * 1024 * 1024),
        name="store",
    )(*outs)


def solution(mesh):
    in_specs = (
        P("nest", "tile", None),
        P("nest", None, "tile", None),
        P("nest", "tile", None),
        P("nest", "tile"),
        P("nest", "tile"),
        P(),
        P("tile", None),
        P(None, "tile", None),
        P("tile", None),
        P(None, "tile", None),
    )
    out_specs = (
        P("nest", "tile", None),
        P("nest", None, "tile", None),
        P("tile", None),
        P(None, "tile", None),
    )
    return jax.shard_map(
        on_device, mesh=mesh, in_specs=in_specs, out_specs=out_specs, check_vma=False
    )
```

```python
import functools

import jax
import jax.numpy as jnp
from jax import lax
from jax.experimental import pallas as pl
from jax.experimental.pallas import tpu as pltpu
from jax.sharding import PartitionSpec as P

RATIO = 5
SUBSTEPS = 4
DT_FINE = 0.4
DT_COARSE = 1.6
DX_COARSE = 5.0
FRICTION = 0.05
RF = 1.0 / (1.0 + DT_FINE * FRICTION)
RP = 1.0 / (1.0 + DT_COARSE * FRICTION)
CP = DT_COARSE / DX_COARSE
FAR = 1.0e6
WIN = 120
CH = 16


def parts_of(x, n):
    out = []
    for _ in range(n):
        hi = x.astype(jnp.bfloat16)
        out.append(hi)
        x = x - hi.astype(jnp.float32)
    return out


def mm(a, b):
    return lax.dot_general(a, b, (((1,), (0,)), ((), ())), preferred_element_type=jnp.float32)


def left_hot(hot, x, n):
    return sum(mm(hot, p) for p in parts_of(x, n))


def right_hot(x, hot, n):
    return sum(mm(p, hot) for p in parts_of(x, n))


def hot_of(mask):
    return jnp.where(mask, 1.0, 0.0).astype(jnp.bfloat16)


def iota(shape, axis):
    return lax.broadcasted_iota(jnp.int32, shape, axis)


def fdiv5(x):
    return jnp.floor((x.astype(jnp.float32) + 0.5) * 0.2).astype(jnp.int32)


def shift_rows(x, by):
    return pltpu.roll(x, by % x.shape[0], 0)


def shift_cols(x, by):
    return pltpu.roll(x, by % x.shape[1], 1)


def parent_step(e, ux, uy, hx, hy, wx, wy, col_open, row_open):
    nx = col_open * (ux - CP * hx * (shift_cols(e, -1) - e) + DT_COARSE * wx) * RP
    ny = row_open * (uy - CP * hy * (shift_rows(e, -1) - e) + DT_COARSE * wy) * RP
    return nx, ny


def kernel(
    T, height, breadth, ph, pc,
    fl, ff, fd, shore, ext, inter, plev_h, pflux_h, pdep_h, wind_h,
    fl_out, ff_out, pl_out, pf_out,
    e, q, dep, lim, fxr, cx, fyr, cy, cxe, sea0, sead, er, qr, be, bq,
    plv, pfv, pdv, wv, shv, exs, ins, pws, pwb, hs, hr, pks, pkb,
    cs, c0a, c0b, c1, es, e0a, e0b, e1, gs, g0a, g0b, g1,
    ssem, rsem, lsem,
):
    k = lax.axis_index("nest")
    t = lax.axis_index("tile")
    ko = 1 - k
    top = 16
    rows = height + 32
    mid = slice(top, top + height)
    inner = slice(8, rows - 8)
    edge = slice(breadth - 128, breadth)
    halo_n = slice(top - 8, top)
    halo_s = slice(top + height, top + height + 8)

    def have(d):
        return (t + d >= 0) & (t + d < T)

    locals_ = [
        pltpu.make_async_copy(src, dst, lsem.at[i])
        for i, (src, dst) in enumerate((
            (shore, shv), (ext, exs), (inter, ins),
            (plev_h, plv), (pflux_h, pfv), (pdep_h, pdv), (wind_h, wv),
            (fd.at[0], dep.at[mid, :]), (fl.at[0], e.at[mid, :]), (ff.at[0], q.at[:, mid, :]),
        ))
    ]
    for c in locals_:
        c.start()

    for buf in (pwb, pkb, c0a, c0b, c1, e0a, e0b, e1, g0a, g0b, g1, hr):
        buf[...] = jnp.zeros(buf.shape, jnp.float32)
    zrow = jnp.zeros((8, breadth), jnp.float32)
    far = jnp.full((8, 128), FAR, jnp.float32)
    for missing, s, b, bs in ((-1, halo_n, 0, slice(8, 16)), (1, halo_s, 1, slice(24, 32))):
        @pl.when(jnp.logical_not(have(missing)))
        def _():
            dep[s, :] = zrow
            lim[s, :] = far
            be[b, bs, :] = zrow
            bq[b, 0, bs, :] = zrow
            bq[b, 1, bs, :] = zrow

    barrier = pltpu.get_barrier_semaphore()

    def greet(nest, d, only=None):
        ok = have(d)
        if only is not None:
            ok = ok & (k == only)

        @pl.when(ok)
        def _():
            pl.semaphore_signal(barrier, inc=1, device_id=(nest, t + d), device_id_type=pl.DeviceIdType.MESH)

    def expect(d, only=None):
        ok = have(d)
        if only is not None:
            ok = ok & (k == only)
        return ok.astype(jnp.int32)

    for d in (1, -1):
        greet(k, d)
    greet(ko, 0)
    greet(ko, -1)
    greet(k, 2, 0)
    greet(ko, 1, 0)
    greet(ko, 2, 0)
    greet(ko, -2, 1)
    count = (expect(1) + expect(-1) + 1 + expect(1) + expect(-2, 0) + expect(2, 0)
             + expect(-1, 1) + expect(-2, 1))

    pushes = []

    class Push:
        def __init__(self, src, dst, same, d, only=None):
            n = len(pushes)
            pushes.append(self)
            self.go, self.come = have(d), have(-d)
            if only is not None:
                self.go = self.go & (k == only)
                self.come = self.come & (k == (only if same else 1 - only))
            self.c = pltpu.make_async_remote_copy(
                src_ref=src, dst_ref=dst, send_sem=ssem.at[n], recv_sem=rsem.at[n],
                device_id=(k if same else ko, t + d), device_id_type=pl.DeviceIdType.MESH)

        def start(self):
            pl.when(self.go)(lambda: self.c.start())

        def sent(self):
            pl.when(self.go)(lambda: self.c.wait_send())

        def arrive(self):
            pl.when(self.come)(lambda: self.c.wait_recv())

    def start(group):
        for c in group:
            c.start()
        return group

    def arrive(group):
        for c in group:
            c.arrive()

    for c in locals_[:3]:
        c.wait()
    offset = jnp.where(k == 0, ins[0, 0], ins[1, 0])
    col_a = jnp.where(k == 0, ins[0, 1], ins[1, 1])
    col_b = jnp.where(k == 0, ins[1, 1], ins[0, 1])

    for c in locals_[3:7]:
        c.wait()
    parent = [plv[...], pdv[...], pfv[1], pfv[0], wv[0], wv[1]]
    block = 0
    for b in range(1, pc // 128):
        block = jnp.where(col_a + WIN >= 128 * b, b, block)
    skip = col_a + WIN - 128 * block
    lane_p = iota((ph, 128), 1)
    packed_w = jnp.zeros((ph, 128), jnp.float32)
    for i, x in enumerate((parent[0], parent[3], parent[2], parent[1], parent[4], parent[5])):
        cut = [x[:, 128 * b:128 * (b + 1)] for b in range(pc // 128)]
        here, then = cut[0], cut[1]
        for b in range(1, pc // 128):
            here = jnp.where(block == b, cut[b], here)
            then = jnp.where(block == b, cut[(b + 1) % (pc // 128)], then)
        by = jnp.where(skip > 16 * i, 128 + 16 * i - skip, 16 * i - skip)
        both = pltpu.roll(jnp.where(lane_p >= skip, here, then), by, 1)
        packed_w = jnp.where((lane_p >> 4) == i, both, packed_w)
    pws[...] = packed_w
    pl.semaphore_wait(barrier, count)
    windows = [
        Push(pws.at[0:8, :], pwb.at[3 * ph:3 * ph + 8, :], True, -2, 0),
        Push(pws.at[:, :], pwb.at[2 * ph:3 * ph, :], True, -1),
        Push(pws.at[8:ph, :], pwb.at[8:ph, :], True, 1),
    ]
    start(windows)
    halo = []
    for d in (1, -1):
        own = slice(height - 8, height) if d == 1 else slice(0, 8)
        to = halo_n if d == 1 else halo_s
        b, bs = (0, slice(8, 16)) if d == 1 else (1, slice(24, 32))
        halo += [
            Push(fd.at[0, own, :], dep.at[to, :], True, d),
            Push(fl.at[0, own, :], be.at[b, bs, :], True, d),
            Push(ff.at[0, :, own, :], bq.at[b, :, bs, :], True, d),
        ]
    start(halo)

    pwb[ph:2 * ph, :] = packed_w

    diag = iota((height, height), 0) == iota((height, height), 1)
    limit = jnp.sum(jnp.where(diag, shv[...].astype(jnp.float32), 0.0), axis=1, keepdims=True)
    r = iota((height, 128), 0)
    live = (r < exs[0, 0]) & (offset + t * (height // RATIO) + fdiv5(r) < ph * T)
    lim[mid, :] = jnp.where(live, limit, FAR)
    limits = [
        Push(lim.at[top + height - 8:top + height, :], lim.at[halo_n, :], True, 1),
        Push(lim.at[top:top + 8, :], lim.at[halo_s, :], True, -1),
    ]
    start(limits)

    pair = iota((8, pc), 0) >> 1
    for at, tile, first in ((0, slice(ph - 8, ph), 2), (1, slice(0, 8), 0)):
        for part, members in ((0, parent[:4]), (1, parent[4:])):
            out = jnp.zeros((8, pc), jnp.float32)
            for i, x in enumerate(members):
                out = jnp.where(pair == i, shift_rows(x[tile], 2 * i + first), out)
            hs[at, 8 * part:8 * part + 8, :] = out
    parent_halo = [
        Push(hs.at[0], hr.at[0], True, 1),
        Push(hs.at[1], hr.at[1], True, -1),
    ]
    start(parent_halo)

    for s in (slice(0, 8), slice(rows - 8, rows)):
        e[s, :] = zrow
        dep[s, :] = zrow
        q[0, s, :] = zrow
        q[1, s, :] = zrow
        lim[s, :] = far
        er[s, :] = zrow[:, :128]
        qr[0, s, :] = zrow[:, :128]
        qr[1, s, :] = zrow[:, :128]
    for b in range(2):
        for s in (slice(0, 8), slice(32, 40)):
            be[b, s, :] = zrow
            bq[b, 1, s, :] = zrow

    colc = iota((CH, breadth), 1)
    last = colc == breadth - 1
    reps = breadth // 128

    def coefficients(r0):
        sl = slice(r0, r0 + CH)
        ss = slice(r0 + 1, r0 + CH + 1)
        colf = colc.astype(jnp.float32)
        wide = lambda s: jnp.concatenate([lim[s, :]] * reps, axis=1)
        act = jnp.where(colf >= wide(sl), 1.0, 0.0)
        act_s = jnp.where(colf >= wide(ss), 1.0, 0.0)
        d0 = dep[sl, :]
        fx = jnp.where(last, 0.0, act * shift_cols(act, -1))
        fxr[sl, :] = fx * RF
        along = (DT_FINE * RF * 0.5) * fx * (d0 + shift_cols(d0, -1))
        cx[sl, :] = along
        cxe[sl, :] = jnp.where(
            last[:, edge], act[:, edge] * jnp.sqrt(d0[:, edge]), along[:, edge])
        fy = act * act_s
        fyr[sl, :] = fy * RF
        cy[sl, :] = (DT_FINE * RF * 0.5) * fy * (d0 + dep[ss, :])

    def advance(ef, qf, r0, n, off):
        sl = slice(r0, r0 + n)
        co = slice(r0 + off, r0 + off + n)
        e0 = ef[sl, :]
        east = shift_cols(e0, -1)
        nx = fxr[co, :] * qf[0, sl, :] - cx[co, :] * (east - e0)
        ny = fyr[co, :] * qf[1, sl, :] - cy[co, :] * (ef[r0 + 1:r0 + n + 1, :] - e0)
        qf[0, sl, :] = nx
        qf[1, sl, :] = ny
        west = shift_cols(nx, 1)
        north = qf[1, r0 - 1:r0 + n - 1, :]
        ef[sl, :] = e0 - DT_FINE * (nx - west + ny - north)

    locals_[7].wait()
    for r0 in range(8 + CH, rows - 8 - CH, CH):
        coefficients(r0)
    for c in locals_[8:]:
        c.wait()
    be[0, 16:32, :] = e[top:top + 16, :]
    be[1, 8:24, :] = e[top + height - 16:top + height, :]
    er[mid, :] = e[mid, edge]
    for i in range(2):
        bq[0, i, 16:32, :] = q[i, top:top + 16, :]
        bq[1, i, 8:24, :] = q[i, top + height - 16:top + height, :]
        qr[i, mid, :] = q[i, mid, edge]

    def inside(step, carry):
        for r0 in range(8 + CH, rows - 8 - CH, CH):
            advance(e, q, r0, CH, 0)
        return carry

    lax.fori_loop(0, SUBSTEPS, inside, 0)

    lane = iota((4 * ph, 128), 1)
    lane_f = iota((rows - 16, 128), 1)
    lev_at = 128 - WIN
    flux_at = 127 - WIN
    rowsum = hot_of(iota((32, height), 0) == offset + fdiv5(iota((32, height), 1)))
    begin = 0
    for s in range(128, breadth - 255, 128):
        begin = jnp.where(RATIO * (col_b - col_a + 127) >= s, s, begin)
    sum_other = hot_of(
        fdiv5(iota((256, 128), 0) + begin) == col_b - col_a + WIN + (iota((256, 128), 1) & 15))
    spread = hot_of(
        iota((rows - 16, 4 * ph), 1)
        == ph + offset + fdiv5(iota((rows - 16, 4 * ph), 0) + 32) - 8
    )
    wrow = (t - 1) * ph + iota((4 * ph, 128), 0)
    wcol = col_a + WIN + iota((4 * ph, 128), 1)
    w_row_open = jnp.where((wrow >= 0) & (wrow < ph * T - 1), 1.0, 0.0)
    w_col_open = jnp.where(wcol < pc - 1, 1.0, 0.0)

    arrive(halo)
    arrive(limits)
    arrive(windows)

    er[halo_n, :] = be[0, 8:16, edge]
    er[halo_s, :] = be[1, 24:32, edge]
    for i in range(2):
        qr[i, halo_n, :] = bq[0, i, 8:16, edge]
        qr[i, halo_s, :] = bq[1, i, 24:32, edge]
    coefficients(8)
    coefficients(rows - 8 - CH)

    we = pwb[...]
    wux, wuy, wd, wwx, wwy = [shift_cols(we, -16 * i) for i in range(1, 6)]
    whx = 0.5 * (wd + shift_cols(wd, -1))
    why = 0.5 * (wd + shift_rows(wd, -1))

    def window_step(we, wux, wuy):
        nx, ny = parent_step(we, wux, wuy, whx, why, wwx, wwy, w_col_open, w_row_open)
        ne = we - CP * (nx - shift_cols(nx, 1) + ny - shift_rows(ny, 1))
        return ne, nx, ny

    def set_sea(oe, oux, ne, nux):
        z = jnp.where(lane == 127, shift_cols(oe, 127 - lev_at), 0.0)
        z = jnp.where(lane == 126, shift_cols(oux, 126 - flux_at), z)
        z = jnp.where(lane == 125, shift_cols(ne, 125 - lev_at), z)
        z = jnp.where(lane == 124, shift_cols(nux, 124 - flux_at), z)
        s = left_hot(spread, z, 3)
        act = jnp.where(float(breadth - 1) >= lim[inner, :], 1.0, 0.0)
        cel = cxe[inner, :]
        old = act * shift_cols(s, 1) - cel * s
        new = act * shift_cols(s, 3) - cel * shift_cols(s, 2)
        keep = lane_f == 127
        sea0[inner, :] = jnp.where(keep, old, 0.0)
        sead[inner, :] = jnp.where(keep, new - old, 0.0)

    def edge_columns():
        for n in range(SUBSTEPS):
            w = (n + 0.5) / SUBSTEPS
            e0 = er[inner, :]
            east = jnp.where(lane_f == 127, 0.0, shift_cols(e0, -1))
            sea = sea0[inner, :] + w * sead[inner, :]
            nx = fxr[inner, edge] * qr[0, inner, :] - cxe[inner, :] * (east - e0) + sea
            ny = fyr[inner, edge] * qr[1, inner, :] - cy[inner, edge] * (er[9:rows - 7, :] - e0)
            qr[0, inner, :] = nx
            qr[1, inner, :] = ny
            north = qr[1, 7:rows - 9, :]
            er[inner, :] = e0 - DT_FINE * (nx - shift_cols(nx, 1) + ny - north)

    def merge_edge(where):
        n = where.stop - where.start
        keep = iota((n, 128), 1) >= 64
        e[where, edge] = jnp.where(keep, er[where, :], e[where, edge])
        for i in range(2):
            q[i, where, edge] = jnp.where(keep, qr[i, where, :], q[i, where, edge])

    for n in range(SUBSTEPS):
        for r0 in (8, 16, 24):
            advance(be.at[0], bq.at[0], r0, 8, 0)
            advance(be.at[1], bq.at[1], r0, 8, rows - 40)
    r8 = iota((8, breadth), 0)
    for dst, bnd in ((e, lambda b: be.at[b]), (q.at[0], lambda b: bq.at[b, 0]), (q.at[1], lambda b: bq.at[b, 1])):
        dst[8:24, :] = bnd(0)[8:24, :]
        dst[24:32, :] = jnp.where(r8 < 4, bnd(0)[24:32, :], dst[24:32, :])
        dst[rows - 32:rows - 24, :] = jnp.where(r8 >= 4, bnd(1)[8:16, :], dst[rows - 32:rows - 24, :])
        dst[rows - 24:rows - 8, :] = bnd(1)[16:32, :]

    n1e, n1x, n1y = window_step(we, wux, wuy)
    set_sea(we, wux, n1e, n1x)
    edge_columns()
    merge_edge(inner)

    glane = iota((32, 128), 1) >> 4

    def packed(res, n):
        out = res[0:32]
        for i in range(1, n):
            out = jnp.where(glane == i, res[32 * i:32 * (i + 1)], out)
        return out

    def wet(width, start):
        colf = (iota((height, width), 1) + start).astype(jnp.float32)
        return jnp.where(colf >= jnp.concatenate([lim[mid, :]] * (width // 128), axis=1), 1.0, 0.0)

    def restrict(act, lev, qx, qy, columns, with_count):
        part = [
            left_hot(rowsum, act * lev, 2),
            left_hot(rowsum, qx, 2),
            left_hot(rowsum, qy, 2),
        ]
        if with_count:
            part = [mm(rowsum, act.astype(jnp.bfloat16))] + part
        return right_hot(jnp.concatenate(part, axis=0), columns, 2)


    def last_sums(with_count, first, step):
        act = wet(128, breadth - 128)
        parts = [act * er[mid, :], qr[0, mid, :], qr[1, mid, :]]
        if with_count:
            parts = [act] + parts
        lane_m = iota((height, 128), 1)
        out = jnp.zeros((height, 128), jnp.float32)
        for i, x in enumerate(parts):
            y = x + shift_cols(x, 1)
            y = y + shift_cols(y, 2) + shift_cols(x, 4)
            at = first + step * i
            out = jnp.where(lane_m == at, shift_cols(y, at + 1), out)
        return left_hot(rowsum, out, 2)

    pks[0] = last_sums(True, 127 - WIN, 16)

    def there(ref):
        out = ref[mid, 0:256]
        for s in range(128, breadth - 255, 128):
            out = jnp.where(begin == s, ref[mid, s:s + 256], out)
        return out

    pks[1] = packed(restrict(wet(256, begin), there(e), there(q.at[0]), there(q.at[1]), sum_other, True), 4)
    near = start([
        Push(pks.at[1], pkb.at[0], False, 0),
        Push(pks.at[1, 8:32, :], pkb.at[1, 8:32, :], False, 1),
        Push(pks.at[1, 0:16, :], pkb.at[2, 0:16, :], False, -1, 1),
        Push(pks.at[1, 24:32, :], pkb.at[3, 24:32, :], False, 2, 0),
        Push(pks.at[1, 0:8, :], pkb.at[4, 0:8, :], False, -2, 1),
        Push(pks.at[0, 8:32, :], pkb.at[5, 8:32, :], True, 1),
        Push(pks.at[0, 0:24, :], pkb.at[6, 0:24, :], True, -1),
    ])

    colsum = hot_of(fdiv5(iota((breadth, 128), 0)) == iota((breadth, 128), 1))
    s1 = restrict(wet(breadth, 0), e[mid, :], q[0, mid, :], q[1, mid, :], colsum, True)
    for i in range(4):
        cs[i] = s1[32 * i:32 * (i + 1)]

    sums1 = start([
        Push(cs.at[:, 0:24, :], c0a.at[:, 8:32, :], False, 0, 0),
        Push(cs.at[:, 0:16, :], c1.at[:, 8:24, :], False, 0, 1),
        Push(cs.at[:, 8:32, :], c0b.at[:, 0:24, :], True, 1, 0),
        Push(cs.at[:, 8:32, :], c0b.at[:, 0:24, :], False, 1, 0),
        Push(cs.at[:, 8:16, :], c1.at[:, 0:8, :], True, 1, 1),
        Push(cs.at[:, 8:16, :], c1.at[:, 0:8, :], False, 1, 1),
        Push(cs.at[:, 0:8, :], c1.at[:, 24:32, :], True, -1, 1),
        Push(cs.at[:, 0:8, :], c1.at[:, 24:32, :], False, -1, 1),
    ])

    er[...] = e[:, edge]
    qr[...] = q[:, :, edge]

    def everywhere(step, carry):
        for r0 in range(8, rows - 8, CH):
            advance(e, q, r0, CH, 0)
        return carry

    lax.fori_loop(0, SUBSTEPS, everywhere, 0)

    bulk = hot_of((fdiv5(iota((breadth, 128), 0)) == iota((breadth, 128), 1)) & (iota((breadth, 128), 1) < breadth // RATIO - 1))
    s2 = restrict(wet(breadth, 0), e[mid, :], q[0, mid, :], q[1, mid, :], bulk, False)
    for i in range(3):
        es[i] = s2[32 * i:32 * (i + 1)]

    def final_sums(src, a0, b0, one, idx):
        return start([
            Push(src.at[idx(0)], a0, False, 0, 0),
            Push(src.at[idx(0)], one, False, 0, 1),
            Push(src.at[idx(1)], b0, True, 1, 0),
            Push(src.at[idx(1)], b0, False, 1, 0),
        ])

    sums2 = final_sums(es, e0a, e0b, e1, lambda i: (slice(None), slice(ph * i, ph * (i + 1)), slice(None)))

    xn = 16 + ph
    grow = t * ph - 8 + iota((xn, pc), 0)
    row_open = jnp.where((grow >= 0) & (grow < ph * T - 1), 1.0, 0.0)
    gcol = iota((xn, pc), 1)
    col_open = jnp.where(gcol < pc - 1, 1.0, 0.0)
    col_0 = jnp.where(k == 0, col_a, col_b)
    col_1 = jnp.where(k == 0, col_b, col_a)
    place_0 = hot_of(iota((128, pc), 1) == col_0 + iota((128, pc), 0))
    place_1 = hot_of(iota((128, pc), 1) == col_1 + iota((128, pc), 0))

    arrive(near)
    beside = pkb[0] + pks[0]
    prev = pkb[1] + pkb[5]
    nxt = pkb[2] + pkb[6]
    sums = jnp.concatenate([
        prev[0:ph] + pkb[3][ph:2 * ph],
        beside[0:ph] + prev[ph:2 * ph],
        nxt[0:ph] + beside[ph:2 * ph],
        pkb[4][0:ph] + nxt[ph:2 * ph],
    ], axis=0) * (1.0 / (RATIO * RATIO))
    keep = 1.0 - sums
    u1e = n1e * keep + shift_cols(sums, -16)
    u1x = n1x * keep + shift_cols(sums, -32)
    u1y = n1y * keep + shift_cols(sums, -48)
    n2e, n2x, _ = window_step(u1e, u1x, u1y)
    set_sea(u1e, u1x, n2e, n2x)
    edge_columns()

    gs[...] = last_sums(False, 0, 1)
    sums3 = final_sums(gs, g0a, g0b, g1, lambda i: (slice(ph * i, ph * (i + 1)), slice(None)))

    merge_edge(mid)
    fl_out[0] = e[mid, :]
    ff_out[0] = q[:, mid, :]

    arrive(parent_halo)

    def extended(own, i):
        part, j = (0, i) if i < 4 else (8, i - 4)
        return jnp.concatenate([
            shift_rows(hr[0, part:part + 8, :], 6 - 2 * j), own, shift_rows(hr[1, part:part + 8, :], -2 * j)], axis=0)

    xe, xd, xuy, xux, xwx, xwy = [
        extended(x, i) for i, x in enumerate((plv[...], pdv[...], pfv[1], pfv[0], wv[0], wv[1]))]
    hx_p = 0.5 * (xd + shift_cols(xd, -1))
    hy_p = 0.5 * (xd + shift_rows(xd, -1))

    def tile_step(xe, ux, uy):
        nx, ny = parent_step(xe, ux, uy, hx_p, hy_p, xwx, xwy, col_open, row_open)
        west = jnp.where(gcol == 0, 0.0, shift_cols(nx, 1))
        return xe - CP * (nx - west + ny - shift_rows(ny, 1)), nx, ny

    t1e, t1x, t1y = tile_step(xe, xux, xuy)

    arrive(sums1)

    @pl.when(k == 0)
    def _():
        c0a[:, 8:32, :] = cs[:, 0:24, :]

    @pl.when(k == 1)
    def _():
        c1[:, 8:24, :] = cs[:, 0:16, :]

    def spread_sums(a0, b0, one, comps):
        nest0 = jnp.concatenate([a0[i] + b0[i] for i in range(comps)], axis=0)
        nest1 = jnp.concatenate([one[i] for i in range(comps)], axis=0)
        both = right_hot(nest0, place_0, 2) + right_hot(nest1, place_1, 2)
        both = both * (1.0 / (RATIO * RATIO))
        n = both.shape[0] // comps
        return [both[i * n:(i + 1) * n] for i in range(comps)]

    g = spread_sums(c0a, c0b, c1, 4)
    retained = 1.0 - g[0]
    t2 = tile_step(t1e * retained + g[1], t1x * retained + g[2], t1y * retained + g[3])
    own_p = slice(8, 8 + ph)
    held = retained[own_p]

    arrive(sums2)

    @pl.when(k == 0)
    def _():
        e0a[...] = es[:, 0:ph, :]
        g0a[...] = gs[0:ph, :]

    @pl.when(k == 1)
    def _():
        e1[...] = es[:, 0:ph, :]
        g1[...] = gs[0:ph, :]

    g = spread_sums(e0a, e0b, e1, 3)
    base = [t2[i][own_p] * held + g[i] for i in range(3)]
    at_0 = gcol[own_p] == col_0 + (breadth // RATIO - 1)
    at_1 = gcol[own_p] == col_1 + (breadth // RATIO - 1)
    arrive(sums3)
    z0 = (g0a[...] + g0b[...]) * (1.0 / (RATIO * RATIO))
    z1 = g1[...] * (1.0 / (RATIO * RATIO))
    outs = []
    for i in range(3):
        v0 = jnp.broadcast_to(z0[:, i:i + 1], (ph, pc))
        v1 = jnp.broadcast_to(z1[:, i:i + 1], (ph, pc))
        outs.append(base[i] + jnp.where(at_0, v0, 0.0) + jnp.where(at_1, v1, 0.0))
    pl_out[...] = outs[0]
    pf_out[0] = outs[1]
    pf_out[1] = outs[2]
    for c in pushes:
        c.sent()


def store(*refs):
    outs = [pltpu.make_async_copy(refs[i], refs[4 + i], refs[8].at[i]) for i in range(4)]
    for i in (1, 0, 3, 2):
        outs[i].start()
    for c in outs:
        c.wait()


def on_device(fl, ff, fd, shore, ext, inter, plev, pflux, pdep, wind):
    _, height, breadth = fl.shape
    ph, pc = plev.shape
    T = lax.axis_size("tile")
    rows = height + 32
    f32 = jnp.float32

    def vmem(*shape):
        return pltpu.VMEM(shape, f32)

    fine, strip = vmem(rows, breadth), vmem(rows, 128)
    dma = pltpu.SemaphoreType.DMA
    vm = pl.BlockSpec(memory_space=pltpu.VMEM)
    hb = pl.BlockSpec(memory_space=pltpu.HBM)
    pin = lambda x: pltpu.with_memory_space_constraint(x, pltpu.HBM)
    outs = pl.pallas_call(
        functools.partial(kernel, T, height, breadth, ph, pc),
        out_shape=[pltpu.VMEM(x.shape, f32) for x in (fl, ff, plev, pflux)],
        in_specs=[hb] * 10,
        out_specs=[vm] * 4,
        scratch_shapes=[
            fine, vmem(2, rows, breadth), fine, strip,
            fine, fine, fine, fine, strip, strip, strip, strip, vmem(2, rows, 128),
            vmem(2, 40, breadth), vmem(2, 2, 40, breadth),
            vmem(ph, pc), vmem(2, ph, pc), vmem(ph, pc), vmem(2, ph, pc),
            pltpu.VMEM((1, height), jnp.int32), pltpu.SMEM((1, 1), jnp.int32), pltpu.SMEM((2, 2), jnp.int32),
            vmem(ph, 128), vmem(4 * ph, 128), vmem(2, 16, pc), vmem(2, 16, pc),
            vmem(2, 2 * ph, 128), vmem(7, 2 * ph, 128),
            vmem(4, 2 * ph, 128), vmem(4, 2 * ph, 128), vmem(4, 2 * ph, 128), vmem(4, 2 * ph, 128),
            vmem(3, 2 * ph, 128), vmem(3, ph, 128), vmem(3, ph, 128), vmem(3, ph, 128),
            vmem(2 * ph, 128), vmem(ph, 128), vmem(ph, 128), vmem(ph, 128),
            dma((36,)), dma((36,)), dma((10,)),
        ],
        compiler_params=pltpu.CompilerParams(
            collective_id=0, has_side_effects=True, vmem_limit_bytes=48 * 1024 * 1024),
        name="nested",
    )(pin(fl), pin(ff), pin(fd), pin(shore), ext, pin(inter), pin(plev), pin(pflux), pin(pdep), pin(wind))
    return pl.pallas_call(
        store,
        out_shape=[jax.ShapeDtypeStruct(x.shape, f32) for x in (fl, ff, plev, pflux)],
        in_specs=[vm] * 4,
        out_specs=[hb] * 4,
        scratch_shapes=[dma((4,))],
        compiler_params=pltpu.CompilerParams(vmem_limit_bytes=48 * 1024 * 1024),
        name="store",
    )(*outs)


def solution(mesh):
    in_specs = (
        P("nest", "tile", None),
        P("nest", None, "tile", None),
        P("nest", "tile", None),
        P("nest", "tile"),
        P("nest", "tile"),
        P(),
        P("tile", None),
        P(None, "tile", None),
        P("tile", None),
        P(None, "tile", None),
    )
    out_specs = (
        P("nest", "tile", None),
        P("nest", None, "tile", None),
        P("tile", None),
        P(None, "tile", None),
    )
    return jax.shard_map(
        on_device, mesh=mesh, in_specs=in_specs, out_specs=out_specs, check_vma=False
    )
```

```python
import functools

import jax
import jax.numpy as jnp
from jax import lax
from jax.experimental import pallas as pl
from jax.experimental.pallas import tpu as pltpu
from jax.sharding import PartitionSpec as P

RATIO = 5
SUBSTEPS = 4
DT_FINE = 0.4
DT_COARSE = 1.6
DX_COARSE = 5.0
FRICTION = 0.05
RF = 1.0 / (1.0 + DT_FINE * FRICTION)
RP = 1.0 / (1.0 + DT_COARSE * FRICTION)
CP = DT_COARSE / DX_COARSE
FAR = 1.0e6
WIN = 120
CH = 16


def parts_of(x, n):
    out = []
    for _ in range(n):
        hi = x.astype(jnp.bfloat16)
        out.append(hi)
        x = x - hi.astype(jnp.float32)
    return out


def mm(a, b):
    return lax.dot_general(a, b, (((1,), (0,)), ((), ())), preferred_element_type=jnp.float32)


def left_hot(hot, x, n):
    return sum(mm(hot, p) for p in parts_of(x, n))


def right_hot(x, hot, n):
    return sum(mm(p, hot) for p in parts_of(x, n))


def hot_of(mask):
    return jnp.where(mask, 1.0, 0.0).astype(jnp.bfloat16)


def iota(shape, axis):
    return lax.broadcasted_iota(jnp.int32, shape, axis)


def fdiv5(x):
    return jnp.floor((x.astype(jnp.float32) + 0.5) * 0.2).astype(jnp.int32)


def shift_rows(x, by):
    return pltpu.roll(x, by % x.shape[0], 0)


def shift_cols(x, by):
    return pltpu.roll(x, by % x.shape[1], 1)


def parent_step(e, ux, uy, hx, hy, wx, wy, col_open, row_open):
    nx = col_open * (ux - CP * hx * (shift_cols(e, -1) - e) + DT_COARSE * wx) * RP
    ny = row_open * (uy - CP * hy * (shift_rows(e, -1) - e) + DT_COARSE * wy) * RP
    return nx, ny


def kernel(
    T, height, breadth, ph, pc,
    fl, ff, fd, shore, ext, inter, plev_h, pflux_h, pdep_h, wind_h,
    fl_out, ff_out, pl_out, pf_out,
    e, q, dep, lim, fxr, cx, fyr, cy, cxe, sea0, sead, er, qr, be, bq,
    plv, pfv, pdv, wv, shv, exs, ins, pws, pwb, hs, hr, pks, pkb,
    cs, c0a, c0b, c1, es, e0a, e0b, e1, gs, g0a, g0b, g1,
    ssem, rsem, lsem,
):
    k = lax.axis_index("nest")
    t = lax.axis_index("tile")
    ko = 1 - k
    top = 16
    rows = height + 32
    mid = slice(top, top + height)
    inner = slice(8, rows - 8)
    edge = slice(breadth - 128, breadth)
    halo_n = slice(top - 8, top)
    halo_s = slice(top + height, top + height + 8)

    def have(d):
        return (t + d >= 0) & (t + d < T)

    locals_ = [
        pltpu.make_async_copy(src, dst, lsem.at[i])
        for i, (src, dst) in enumerate((
            (shore, shv), (ext, exs), (inter, ins),
            (plev_h, plv), (pflux_h, pfv), (pdep_h, pdv), (wind_h, wv),
            (fd.at[0], dep.at[mid, :]), (fl.at[0], e.at[mid, :]), (ff.at[0], q.at[:, mid, :]),
        ))
    ]
    for c in locals_:
        c.start()

    for buf in (pwb, pkb, c0a, c0b, c1, e0a, e0b, e1, g0a, g0b, g1, hr):
        buf[...] = jnp.zeros(buf.shape, jnp.float32)
    zrow = jnp.zeros((8, breadth), jnp.float32)
    far = jnp.full((8, 128), FAR, jnp.float32)
    for missing, s, b, bs in ((-1, halo_n, 0, slice(8, 16)), (1, halo_s, 1, slice(24, 32))):
        @pl.when(jnp.logical_not(have(missing)))
        def _():
            dep[s, :] = zrow
            lim[s, :] = far
            be[b, bs, :] = zrow
            bq[b, 0, bs, :] = zrow
            bq[b, 1, bs, :] = zrow

    barrier = pltpu.get_barrier_semaphore()

    def greet(nest, d, only=None):
        ok = have(d)
        if only is not None:
            ok = ok & (k == only)

        @pl.when(ok)
        def _():
            pl.semaphore_signal(barrier, inc=1, device_id=(nest, t + d), device_id_type=pl.DeviceIdType.MESH)

    def expect(d, only=None):
        ok = have(d)
        if only is not None:
            ok = ok & (k == only)
        return ok.astype(jnp.int32)

    for d in (1, -1):
        greet(k, d)
    greet(ko, 0)
    greet(ko, -1)
    greet(k, 2, 0)
    greet(ko, 1, 0)
    greet(ko, 2, 0)
    greet(ko, -2, 1)
    count = (expect(1) + expect(-1) + 1 + expect(1) + expect(-2, 0) + expect(2, 0)
             + expect(-1, 1) + expect(-2, 1))

    pushes = []

    class Push:
        def __init__(self, src, dst, same, d, only=None):
            n = len(pushes)
            pushes.append(self)
            self.go, self.come = have(d), have(-d)
            if only is not None:
                self.go = self.go & (k == only)
                self.come = self.come & (k == (only if same else 1 - only))
            self.c = pltpu.make_async_remote_copy(
                src_ref=src, dst_ref=dst, send_sem=ssem.at[n], recv_sem=rsem.at[n],
                device_id=(k if same else ko, t + d), device_id_type=pl.DeviceIdType.MESH)

        def start(self):
            pl.when(self.go)(lambda: self.c.start())

        def sent(self):
            pl.when(self.go)(lambda: self.c.wait_send())

        def arrive(self):
            pl.when(self.come)(lambda: self.c.wait_recv())

    def start(group):
        for c in group:
            c.start()
        return group

    def arrive(group):
        for c in group:
            c.arrive()

    for c in locals_[:3]:
        c.wait()
    offset = jnp.where(k == 0, ins[0, 0], ins[1, 0])
    col_a = jnp.where(k == 0, ins[0, 1], ins[1, 1])
    col_b = jnp.where(k == 0, ins[1, 1], ins[0, 1])

    for c in locals_[3:7]:
        c.wait()
    parent = [plv[...], pdv[...], pfv[1], pfv[0], wv[0], wv[1]]
    block = 0
    for b in range(1, pc // 128):
        block = jnp.where(col_a + WIN >= 128 * b, b, block)
    skip = col_a + WIN - 128 * block
    lane_p = iota((ph, 128), 1)
    packed_w = jnp.zeros((ph, 128), jnp.float32)
    for i, x in enumerate((parent[0], parent[3], parent[2], parent[1], parent[4], parent[5])):
        cut = [x[:, 128 * b:128 * (b + 1)] for b in range(pc // 128)]
        here, then = cut[0], cut[1]
        for b in range(1, pc // 128):
            here = jnp.where(block == b, cut[b], here)
            then = jnp.where(block == b, cut[(b + 1) % (pc // 128)], then)
        by = jnp.where(skip > 16 * i, 128 + 16 * i - skip, 16 * i - skip)
        both = pltpu.roll(jnp.where(lane_p >= skip, here, then), by, 1)
        packed_w = jnp.where((lane_p >> 4) == i, both, packed_w)
    pws[...] = packed_w
    pl.semaphore_wait(barrier, count)
    windows = [
        Push(pws.at[0:8, :], pwb.at[3 * ph:3 * ph + 8, :], True, -2, 0),
        Push(pws.at[:, :], pwb.at[2 * ph:3 * ph, :], True, -1),
        Push(pws.at[8:ph, :], pwb.at[8:ph, :], True, 1),
    ]
    start(windows)
    halo = []
    for d in (1, -1):
        own = slice(height - 8, height) if d == 1 else slice(0, 8)
        to = halo_n if d == 1 else halo_s
        b, bs = (0, slice(8, 16)) if d == 1 else (1, slice(24, 32))
        halo += [
            Push(fd.at[0, own, :], dep.at[to, :], True, d),
            Push(fl.at[0, own, :], be.at[b, bs, :], True, d),
            Push(ff.at[0, :, own, :], bq.at[b, :, bs, :], True, d),
        ]
    start(halo)

    pwb[ph:2 * ph, :] = packed_w

    diag = iota((height, height), 0) == iota((height, height), 1)
    limit = jnp.sum(jnp.where(diag, shv[...].astype(jnp.float32), 0.0), axis=1, keepdims=True)
    r = iota((height, 128), 0)
    live = (r < exs[0, 0]) & (offset + t * (height // RATIO) + fdiv5(r) < ph * T)
    lim[mid, :] = jnp.where(live, limit, FAR)
    limits = [
        Push(lim.at[top + height - 8:top + height, :], lim.at[halo_n, :], True, 1),
        Push(lim.at[top:top + 8, :], lim.at[halo_s, :], True, -1),
    ]
    start(limits)

    pair = iota((8, pc), 0) >> 1
    for at, tile, first in ((0, slice(ph - 8, ph), 2), (1, slice(0, 8), 0)):
        for part, members in ((0, parent[:4]), (1, parent[4:])):
            out = jnp.zeros((8, pc), jnp.float32)
            for i, x in enumerate(members):
                out = jnp.where(pair == i, shift_rows(x[tile], 2 * i + first), out)
            hs[at, 8 * part:8 * part + 8, :] = out
    parent_halo = [
        Push(hs.at[0], hr.at[0], True, 1),
        Push(hs.at[1], hr.at[1], True, -1),
    ]
    start(parent_halo)

    for s in (slice(0, 8), slice(rows - 8, rows)):
        e[s, :] = zrow
        dep[s, :] = zrow
        q[0, s, :] = zrow
        q[1, s, :] = zrow
        lim[s, :] = far
        er[s, :] = zrow[:, :128]
        qr[0, s, :] = zrow[:, :128]
        qr[1, s, :] = zrow[:, :128]
    for b in range(2):
        for s in (slice(0, 8), slice(32, 40)):
            be[b, s, :] = zrow
            bq[b, 1, s, :] = zrow

    colc = iota((CH, breadth), 1)
    last = colc == breadth - 1
    reps = breadth // 128

    def coefficients(r0):
        sl = slice(r0, r0 + CH)
        ss = slice(r0 + 1, r0 + CH + 1)
        colf = colc.astype(jnp.float32)
        wide = lambda s: jnp.concatenate([lim[s, :]] * reps, axis=1)
        act = jnp.where(colf >= wide(sl), 1.0, 0.0)
        act_s = jnp.where(colf >= wide(ss), 1.0, 0.0)
        d0 = dep[sl, :]
        fx = jnp.where(last, 0.0, act * shift_cols(act, -1))
        fxr[sl, :] = fx * RF
        along = (DT_FINE * RF * 0.5) * fx * (d0 + shift_cols(d0, -1))
        cx[sl, :] = along
        cxe[sl, :] = jnp.where(
            last[:, edge], act[:, edge] * jnp.sqrt(d0[:, edge]), along[:, edge])
        fy = act * act_s
        fyr[sl, :] = fy * RF
        cy[sl, :] = (DT_FINE * RF * 0.5) * fy * (d0 + dep[ss, :])

    r8 = iota((8, breadth), 0)

    def advance(ef, qf, first, past, off):
        after = ef[first:first + 8, :]
        after_up = shift_rows(after, -1)
        before_down = shift_rows(qf[1, first - 8:first, :], 1)
        for r0 in range(first, past, 8):
            sl = slice(r0, r0 + 8)
            co = slice(r0 + off, r0 + off + 8)
            e0, e0_up = after, after_up
            after = ef[r0 + 8:r0 + 16, :]
            after_up = shift_rows(after, -1)
            south = jnp.where(r8 == 7, after_up, e0_up)
            nx = fxr[co, :] * qf[0, sl, :] - cx[co, :] * (shift_cols(e0, -1) - e0)
            ny = fyr[co, :] * qf[1, sl, :] - cy[co, :] * (south - e0)
            qf[0, sl, :] = nx
            qf[1, sl, :] = ny
            down = shift_rows(ny, 1)
            north = jnp.where(r8 == 0, before_down, down)
            before_down = down
            ef[sl, :] = e0 - DT_FINE * (nx - shift_cols(nx, 1) + ny - north)

    locals_[7].wait()
    for r0 in range(8 + CH, rows - 8 - CH, CH):
        coefficients(r0)
    for c in locals_[8:]:
        c.wait()
    be[0, 16:32, :] = e[top:top + 16, :]
    be[1, 8:24, :] = e[top + height - 16:top + height, :]
    er[mid, :] = e[mid, edge]
    for i in range(2):
        bq[0, i, 16:32, :] = q[i, top:top + 16, :]
        bq[1, i, 8:24, :] = q[i, top + height - 16:top + height, :]
        qr[i, mid, :] = q[i, mid, edge]

    def inside(step, carry):
        advance(e, q, 8 + CH, rows - 8 - CH, 0)
        return carry

    lax.fori_loop(0, SUBSTEPS, inside, 0)

    lane_f = iota((rows - 16, 128), 1)
    level_at = 128 - WIN
    rowsum = hot_of(iota((32, height), 0) == offset + fdiv5(iota((32, height), 1)))
    begin = 0
    for s in range(128, breadth - 255, 128):
        begin = jnp.where(RATIO * (col_b - col_a + 127) >= s, s, begin)
    sum_other = hot_of(
        fdiv5(iota((256, 128), 0) + begin) == col_b - col_a + WIN + (iota((256, 128), 1) & 15))
    spread = hot_of(
        iota((rows - 16, 4 * ph), 1)
        == ph + offset + fdiv5(iota((rows - 16, 4 * ph), 0) + 32) - 8
    )
    wrow = (t - 1) * ph + iota((4 * ph, 128), 0)
    wlane = iota((4 * ph, 128), 1)
    wcol = col_a + 1 + jnp.where(wlane < 64, wlane + 128, wlane)
    w_row_open = jnp.where((wrow >= 0) & (wrow < ph * T - 1), 1.0, 0.0)
    w_col_open = jnp.where(wcol < pc - 1, 1.0, 0.0)

    arrive(halo)
    arrive(limits)
    arrive(windows)

    er[halo_n, :] = be[0, 8:16, edge]
    er[halo_s, :] = be[1, 24:32, edge]
    for i in range(2):
        qr[i, halo_n, :] = bq[0, i, 8:16, edge]
        qr[i, halo_s, :] = bq[1, i, 24:32, edge]
    coefficients(8)
    coefficients(rows - 8 - CH)

    pw = pwb[...]
    here = lambda x, i: shift_cols(x, 127 - level_at - 16 * i)
    west_of = lambda x, i: shift_cols(x, 128 - level_at - 16 * i)
    we, wux, wuy, wd, wwx, wwy = [here(pw, i) for i in range(6)]
    wuxw, wdw, wwxw = [west_of(pw, i) for i in (1, 3, 4)]
    whx = 0.5 * (wd + shift_cols(pw, 126 - level_at - 48))
    whxw = 0.5 * (wdw + wd)
    why = 0.5 * (wd + shift_rows(wd, -1))

    def window_step(we, wux, wuxw, wuy):
        nx = w_col_open * (wux - CP * whx * (shift_cols(we, -1) - we) + DT_COARSE * wwx) * RP
        nxw = (wuxw - CP * whxw * (we - shift_cols(we, 1)) + DT_COARSE * wwxw) * RP
        ny = w_row_open * (wuy - CP * why * (shift_rows(we, -1) - we) + DT_COARSE * wwy) * RP
        ne = we - CP * (nx - nxw + ny - shift_rows(ny, 1))
        return ne, nx, nxw, ny

    def set_sea(oe, oux, ne, nux):
        s = left_hot(spread, jnp.concatenate([oe, oux, ne, nux], axis=1), 3)
        ea, qb, ea_new, qb_new = [s[:, 128 * i:128 * (i + 1)] for i in range(4)]
        act = jnp.where(float(breadth - 1) >= lim[inner, :], 1.0, 0.0)
        cel = cxe[inner, :]
        old = act * qb - cel * ea
        new = act * qb_new - cel * ea_new
        keep = lane_f == 127
        sea0[inner, :] = jnp.where(keep, old, 0.0)
        sead[inner, :] = jnp.where(keep, new - old, 0.0)

    def edge_columns():
        e0, qx, qy = er[inner, :], qr[0, inner, :], qr[1, inner, :]
        sea, more = sea0[inner, :], sead[inner, :]
        kx, ky = cxe[inner, :], cy[inner, edge]
        fx, fy = fxr[inner, edge], fyr[inner, edge]
        qxw, kxw, fxw = shift_cols(qx, 1), shift_cols(kx, 1), shift_cols(fx, 1)
        for n in range(SUBSTEPS):
            w = (n + 0.5) / SUBSTEPS
            east = jnp.where(lane_f == 127, 0.0, shift_cols(e0, -1))
            qx = fx * qx - kx * (east - e0) + (sea + w * more)
            qxw = fxw * qxw - kxw * (e0 - shift_cols(e0, 1))
            qy = fy * qy - ky * (shift_rows(e0, -1) - e0)
            e0 = e0 - DT_FINE * (qx - qxw + qy - shift_rows(qy, 1))
        er[inner, :] = e0
        qr[0, inner, :] = qx
        qr[1, inner, :] = qy

    def merge_edge(where):
        n = where.stop - where.start
        keep = iota((n, 128), 1) >= 64
        e[where, edge] = jnp.where(keep, er[where, :], e[where, edge])
        for i in range(2):
            q[i, where, edge] = jnp.where(keep, qr[i, where, :], q[i, where, edge])

    for n in range(SUBSTEPS):
        advance(be.at[0], bq.at[0], 8, 32, 0)
        advance(be.at[1], bq.at[1], 8, 32, rows - 40)
    for dst, bnd in ((e, lambda b: be.at[b]), (q.at[0], lambda b: bq.at[b, 0]), (q.at[1], lambda b: bq.at[b, 1])):
        dst[8:24, :] = bnd(0)[8:24, :]
        dst[24:32, :] = jnp.where(r8 < 4, bnd(0)[24:32, :], dst[24:32, :])
        dst[rows - 32:rows - 24, :] = jnp.where(r8 >= 4, bnd(1)[8:16, :], dst[rows - 32:rows - 24, :])
        dst[rows - 24:rows - 8, :] = bnd(1)[16:32, :]

    n1e, n1x, n1xw, n1y = window_step(we, wux, wuxw, wuy)
    set_sea(we, wuxw, n1e, n1xw)
    edge_columns()
    merge_edge(inner)

    glane = iota((32, 128), 1) >> 4

    def packed(res, n):
        out = res[0:32]
        for i in range(1, n):
            out = jnp.where(glane == i, res[32 * i:32 * (i + 1)], out)
        return out

    def wet(width, start):
        colf = (iota((height, width), 1) + start).astype(jnp.float32)
        return jnp.where(colf >= jnp.concatenate([lim[mid, :]] * (width // 128), axis=1), 1.0, 0.0)

    def restrict(act, lev, qx, qy, columns, with_count):
        part = [
            left_hot(rowsum, act * lev, 2),
            left_hot(rowsum, qx, 2),
            left_hot(rowsum, qy, 2),
        ]
        if with_count:
            part = [mm(rowsum, act.astype(jnp.bfloat16))] + part
        return right_hot(jnp.concatenate(part, axis=0), columns, 2)


    lane_m = iota((height, 128), 1)

    def last_sums(with_count):
        act = wet(128, breadth - 128)
        parts = [act * er[mid, :], qr[0, mid, :], qr[1, mid, :]]
        if with_count:
            parts = [act] + parts
        x = 0.0
        for i, part in enumerate(parts):
            x = jnp.where((lane_m >> 4) == i, shift_cols(part, 16 * i + level_at), x)
        y = x + ((shift_cols(x, 1) + shift_cols(x, 2)) + (shift_cols(x, 3) + shift_cols(x, 4)))
        out = jnp.where((lane_m & 15) == 127 - WIN, y, 0.0)
        return left_hot(rowsum, out, 2)

    pks[0] = last_sums(True)

    def there(ref):
        out = ref[mid, 0:256]
        for s in range(128, breadth - 255, 128):
            out = jnp.where(begin == s, ref[mid, s:s + 256], out)
        return out

    pks[1] = packed(restrict(wet(256, begin), there(e), there(q.at[0]), there(q.at[1]), sum_other, True), 4)
    near = start([
        Push(pks.at[1], pkb.at[0], False, 0),
        Push(pks.at[1, 8:32, :], pkb.at[1, 8:32, :], False, 1),
        Push(pks.at[1, 0:16, :], pkb.at[2, 0:16, :], False, -1, 1),
        Push(pks.at[1, 24:32, :], pkb.at[3, 24:32, :], False, 2, 0),
        Push(pks.at[1, 0:8, :], pkb.at[4, 0:8, :], False, -2, 1),
        Push(pks.at[0, 8:32, :], pkb.at[5, 8:32, :], True, 1),
        Push(pks.at[0, 0:24, :], pkb.at[6, 0:24, :], True, -1),
    ])

    colsum = hot_of(fdiv5(iota((breadth, 128), 0)) == iota((breadth, 128), 1))
    s1 = restrict(wet(breadth, 0), e[mid, :], q[0, mid, :], q[1, mid, :], colsum, True)
    for i in range(4):
        cs[i] = s1[32 * i:32 * (i + 1)]

    sums1 = start([
        Push(cs.at[:, 0:24, :], c0a.at[:, 8:32, :], False, 0, 0),
        Push(cs.at[:, 0:16, :], c1.at[:, 8:24, :], False, 0, 1),
        Push(cs.at[:, 8:32, :], c0b.at[:, 0:24, :], True, 1, 0),
        Push(cs.at[:, 8:32, :], c0b.at[:, 0:24, :], False, 1, 0),
        Push(cs.at[:, 8:16, :], c1.at[:, 0:8, :], True, 1, 1),
        Push(cs.at[:, 8:16, :], c1.at[:, 0:8, :], False, 1, 1),
        Push(cs.at[:, 0:8, :], c1.at[:, 24:32, :], True, -1, 1),
        Push(cs.at[:, 0:8, :], c1.at[:, 24:32, :], False, -1, 1),
    ])

    er[...] = e[:, edge]
    qr[...] = q[:, :, edge]

    def everywhere(step, carry):
        advance(e, q, 8, rows - 8, 0)
        return carry

    lax.fori_loop(0, SUBSTEPS, everywhere, 0)

    bulk = hot_of((fdiv5(iota((breadth, 128), 0)) == iota((breadth, 128), 1)) & (iota((breadth, 128), 1) < breadth // RATIO - 1))
    s2 = restrict(wet(breadth, 0), e[mid, :], q[0, mid, :], q[1, mid, :], bulk, False)
    for i in range(3):
        es[i] = s2[32 * i:32 * (i + 1)]

    def final_sums(src, a0, b0, one, idx):
        return start([
            Push(src.at[idx(0)], a0, False, 0, 0),
            Push(src.at[idx(0)], one, False, 0, 1),
            Push(src.at[idx(1)], b0, True, 1, 0),
            Push(src.at[idx(1)], b0, False, 1, 0),
        ])

    sums2 = final_sums(es, e0a, e0b, e1, lambda i: (slice(None), slice(ph * i, ph * (i + 1)), slice(None)))

    xn = 16 + ph
    grow = t * ph - 8 + iota((xn, pc), 0)
    row_open = jnp.where((grow >= 0) & (grow < ph * T - 1), 1.0, 0.0)
    gcol = iota((xn, pc), 1)
    col_open = jnp.where(gcol < pc - 1, 1.0, 0.0)
    col_0 = jnp.where(k == 0, col_a, col_b)
    col_1 = jnp.where(k == 0, col_b, col_a)
    place_0 = hot_of(iota((128, pc), 1) == col_0 + iota((128, pc), 0))
    place_1 = hot_of(iota((128, pc), 1) == col_1 + iota((128, pc), 0))

    arrive(near)
    beside = pkb[0] + pks[0]
    prev = pkb[1] + pkb[5]
    nxt = pkb[2] + pkb[6]
    sums = jnp.concatenate([
        prev[0:ph] + pkb[3][ph:2 * ph],
        beside[0:ph] + prev[ph:2 * ph],
        nxt[0:ph] + beside[ph:2 * ph],
        pkb[4][0:ph] + nxt[ph:2 * ph],
    ], axis=0) * (1.0 / (RATIO * RATIO))
    keep = 1.0 - here(sums, 0)
    u1e = n1e * keep + here(sums, 1)
    u1x = n1x * keep + here(sums, 2)
    u1xw = n1xw * (1.0 - west_of(sums, 0)) + west_of(sums, 2)
    u1y = n1y * keep + here(sums, 3)
    n2e, _, n2xw, _ = window_step(u1e, u1x, u1xw, u1y)
    set_sea(u1e, u1xw, n2e, n2xw)
    edge_columns()

    gs[...] = last_sums(False)
    sums3 = final_sums(gs, g0a, g0b, g1, lambda i: (slice(ph * i, ph * (i + 1)), slice(None)))

    merge_edge(mid)
    fl_out[0] = e[mid, :]
    ff_out[0] = q[:, mid, :]

    arrive(parent_halo)

    def extended(own, i):
        part, j = (0, i) if i < 4 else (8, i - 4)
        return jnp.concatenate([
            shift_rows(hr[0, part:part + 8, :], 6 - 2 * j), own, shift_rows(hr[1, part:part + 8, :], -2 * j)], axis=0)

    xe, xd, xuy, xux, xwx, xwy = [
        extended(x, i) for i, x in enumerate((plv[...], pdv[...], pfv[1], pfv[0], wv[0], wv[1]))]
    hx_p = 0.5 * (xd + shift_cols(xd, -1))
    hy_p = 0.5 * (xd + shift_rows(xd, -1))

    def tile_step(xe, ux, uy):
        nx, ny = parent_step(xe, ux, uy, hx_p, hy_p, xwx, xwy, col_open, row_open)
        west = jnp.where(gcol == 0, 0.0, shift_cols(nx, 1))
        return xe - CP * (nx - west + ny - shift_rows(ny, 1)), nx, ny

    t1e, t1x, t1y = tile_step(xe, xux, xuy)

    arrive(sums1)

    @pl.when(k == 0)
    def _():
        c0a[:, 8:32, :] = cs[:, 0:24, :]

    @pl.when(k == 1)
    def _():
        c1[:, 8:24, :] = cs[:, 0:16, :]

    def spread_sums(a0, b0, one, comps):
        nest0 = jnp.concatenate([a0[i] + b0[i] for i in range(comps)], axis=0)
        nest1 = jnp.concatenate([one[i] for i in range(comps)], axis=0)
        both = right_hot(nest0, place_0, 2) + right_hot(nest1, place_1, 2)
        both = both * (1.0 / (RATIO * RATIO))
        n = both.shape[0] // comps
        return [both[i * n:(i + 1) * n] for i in range(comps)]

    g = spread_sums(c0a, c0b, c1, 4)
    retained = 1.0 - g[0]
    t2 = tile_step(t1e * retained + g[1], t1x * retained + g[2], t1y * retained + g[3])
    own_p = slice(8, 8 + ph)
    held = retained[own_p]

    arrive(sums2)

    @pl.when(k == 0)
    def _():
        e0a[...] = es[:, 0:ph, :]
        g0a[...] = gs[0:ph, :]

    @pl.when(k == 1)
    def _():
        e1[...] = es[:, 0:ph, :]
        g1[...] = gs[0:ph, :]

    g = spread_sums(e0a, e0b, e1, 3)
    base = [t2[i][own_p] * held + g[i] for i in range(3)]
    at_0 = gcol[own_p] == col_0 + (breadth // RATIO - 1)
    at_1 = gcol[own_p] == col_1 + (breadth // RATIO - 1)
    arrive(sums3)
    z0 = (g0a[...] + g0b[...]) * (1.0 / (RATIO * RATIO))
    z1 = g1[...] * (1.0 / (RATIO * RATIO))
    outs = []
    for i in range(3):
        v0 = jnp.broadcast_to(z0[:, 127 - WIN + 16 * i:128 - WIN + 16 * i], (ph, pc))
        v1 = jnp.broadcast_to(z1[:, 127 - WIN + 16 * i:128 - WIN + 16 * i], (ph, pc))
        outs.append(base[i] + jnp.where(at_0, v0, 0.0) + jnp.where(at_1, v1, 0.0))
    pl_out[...] = outs[0]
    pf_out[0] = outs[1]
    pf_out[1] = outs[2]
    for c in pushes:
        c.sent()


def store(*refs):
    outs = [pltpu.make_async_copy(refs[i], refs[4 + i], refs[8].at[i]) for i in range(4)]
    for i in (1, 0, 3, 2):
        outs[i].start()
    for c in outs:
        c.wait()


def on_device(fl, ff, fd, shore, ext, inter, plev, pflux, pdep, wind):
    _, height, breadth = fl.shape
    ph, pc = plev.shape
    T = lax.axis_size("tile")
    rows = height + 32
    f32 = jnp.float32

    def vmem(*shape):
        return pltpu.VMEM(shape, f32)

    fine, strip = vmem(rows, breadth), vmem(rows, 128)
    dma = pltpu.SemaphoreType.DMA
    vm = pl.BlockSpec(memory_space=pltpu.VMEM)
    hb = pl.BlockSpec(memory_space=pltpu.HBM)
    pin = lambda x: pltpu.with_memory_space_constraint(x, pltpu.HBM)
    outs = pl.pallas_call(
        functools.partial(kernel, T, height, breadth, ph, pc),
        out_shape=[pltpu.VMEM(x.shape, f32) for x in (fl, ff, plev, pflux)],
        in_specs=[hb] * 10,
        out_specs=[vm] * 4,
        scratch_shapes=[
            fine, vmem(2, rows, breadth), fine, strip,
            fine, fine, fine, fine, strip, strip, strip, strip, vmem(2, rows, 128),
            vmem(2, 40, breadth), vmem(2, 2, 40, breadth),
            vmem(ph, pc), vmem(2, ph, pc), vmem(ph, pc), vmem(2, ph, pc),
            pltpu.VMEM((1, height), jnp.int32), pltpu.SMEM((1, 1), jnp.int32), pltpu.SMEM((2, 2), jnp.int32),
            vmem(ph, 128), vmem(4 * ph, 128), vmem(2, 16, pc), vmem(2, 16, pc),
            vmem(2, 2 * ph, 128), vmem(7, 2 * ph, 128),
            vmem(4, 2 * ph, 128), vmem(4, 2 * ph, 128), vmem(4, 2 * ph, 128), vmem(4, 2 * ph, 128),
            vmem(3, 2 * ph, 128), vmem(3, ph, 128), vmem(3, ph, 128), vmem(3, ph, 128),
            vmem(2 * ph, 128), vmem(ph, 128), vmem(ph, 128), vmem(ph, 128),
            dma((36,)), dma((36,)), dma((10,)),
        ],
        compiler_params=pltpu.CompilerParams(
            collective_id=0, has_side_effects=True, vmem_limit_bytes=48 * 1024 * 1024),
        name="nested",
    )(pin(fl), pin(ff), pin(fd), pin(shore), ext, pin(inter), pin(plev), pin(pflux), pin(pdep), pin(wind))
    return pl.pallas_call(
        store,
        out_shape=[jax.ShapeDtypeStruct(x.shape, f32) for x in (fl, ff, plev, pflux)],
        in_specs=[vm] * 4,
        out_specs=[hb] * 4,
        scratch_shapes=[dma((4,))],
        compiler_params=pltpu.CompilerParams(vmem_limit_bytes=48 * 1024 * 1024),
        name="store",
    )(*outs)


def solution(mesh):
    in_specs = (
        P("nest", "tile", None),
        P("nest", None, "tile", None),
        P("nest", "tile", None),
        P("nest", "tile"),
        P("nest", "tile"),
        P(),
        P("tile", None),
        P(None, "tile", None),
        P("tile", None),
        P(None, "tile", None),
    )
    out_specs = (
        P("nest", "tile", None),
        P("nest", None, "tile", None),
        P("tile", None),
        P(None, "tile", None),
    )
    return jax.shard_map(
        on_device, mesh=mesh, in_specs=in_specs, out_specs=out_specs, check_vma=False
    )
```

```python
import functools

import jax
import jax.numpy as jnp
from jax import lax
from jax.experimental import pallas as pl
from jax.experimental.pallas import tpu as pltpu
from jax.sharding import PartitionSpec as P

RATIO = 5
SUBSTEPS = 4
DT_FINE = 0.4
DT_COARSE = 1.6
DX_COARSE = 5.0
FRICTION = 0.05
RF = 1.0 / (1.0 + DT_FINE * FRICTION)
RP = 1.0 / (1.0 + DT_COARSE * FRICTION)
CP = DT_COARSE / DX_COARSE
FAR = 1.0e6
WIN = 120
CH = 16


def parts_of(x, n):
    out = []
    for _ in range(n):
        hi = x.astype(jnp.bfloat16)
        out.append(hi)
        x = x - hi.astype(jnp.float32)
    return out


def mm(a, b):
    return lax.dot_general(a, b, (((1,), (0,)), ((), ())), preferred_element_type=jnp.float32)


def left_hot(hot, x, n):
    return sum(mm(hot, p) for p in parts_of(x, n))


def stacked_hot(hot, x, n):
    return mm(hot, jnp.concatenate(parts_of(x, n), axis=0))


def right_hot(x, hot, n):
    return sum(mm(p, hot) for p in parts_of(x, n))


def hot_of(mask):
    return jnp.where(mask, 1.0, 0.0).astype(jnp.bfloat16)


def iota(shape, axis):
    return lax.broadcasted_iota(jnp.int32, shape, axis)


def fdiv5(x):
    return jnp.floor((x.astype(jnp.float32) + 0.5) * 0.2).astype(jnp.int32)


def shift_rows(x, by):
    return pltpu.roll(x, by % x.shape[0], 0)


def shift_cols(x, by):
    return pltpu.roll(x, by % x.shape[1], 1)


def parent_step(e, ux, uy, hx, hy, wx, wy, col_open, row_open):
    nx = col_open * (ux - CP * hx * (shift_cols(e, -1) - e) + DT_COARSE * wx) * RP
    ny = row_open * (uy - CP * hy * (shift_rows(e, -1) - e) + DT_COARSE * wy) * RP
    return nx, ny


def kernel(
    T, height, breadth, ph, pc,
    fl, ff, fd, shore, ext, inter, plev_h, pflux_h, pdep_h, wind_h,
    fl_out, ff_out, pl_out, pf_out,
    e, q, dep, lim, fxr, cx, fyr, cy, cxe, sea0, sead, er, qr, be, bq,
    plv, pfv, pdv, wv, shv, exs, ins, pws, pwb, hs, hr, pks, pkb,
    cs, c0a, c0b, c1, es, e0a, e0b, e1, gs, g0a, g0b, g1,
    ssem, rsem, lsem, ready,
):
    k = lax.axis_index("nest")
    t = lax.axis_index("tile")
    ko = 1 - k
    top = 16
    rows = height + 32
    mid = slice(top, top + height)
    inner = slice(8, rows - 8)
    edge = slice(breadth - 128, breadth)
    halo_n = slice(top - 8, top)
    halo_s = slice(top + height, top + height + 8)

    def have(d):
        return (t + d >= 0) & (t + d < T)

    locals_ = [
        pltpu.make_async_copy(src, dst, lsem.at[i])
        for i, (src, dst) in enumerate((
            (shore, shv), (ext, exs), (inter, ins),
            (plev_h, plv), (pflux_h, pfv), (pdep_h, pdv), (wind_h, wv),
            (fd.at[0], dep.at[mid, :]), (fl.at[0], e.at[mid, :]), (ff.at[0], q.at[:, mid, :]),
        ))
    ]
    for c in locals_:
        c.start()

    for buf in (pwb, pkb, c0a, c0b, c1, e0a, e0b, e1, g0a, g0b, g1, hr):
        buf[...] = jnp.zeros(buf.shape, jnp.float32)
    zrow = jnp.zeros((8, breadth), jnp.float32)
    far = jnp.full((8, 128), FAR, jnp.float32)
    for missing, s, b, bs in ((-1, halo_n, 0, slice(8, 16)), (1, halo_s, 1, slice(24, 32))):
        @pl.when(jnp.logical_not(have(missing)))
        def _():
            dep[s, :] = zrow
            lim[s, :] = far
            be[b, bs, :] = zrow
            bq[b, 0, bs, :] = zrow
            bq[b, 1, bs, :] = zrow

    barrier = pltpu.get_barrier_semaphore()

    def greet(nest, d, only=None):
        ok = have(d)
        if only is not None:
            ok = ok & (k == only)

        @pl.when(ok)
        def _():
            pl.semaphore_signal(barrier, inc=1, device_id=(nest, t + d), device_id_type=pl.DeviceIdType.MESH)

    def expect(d, only=None):
        ok = have(d)
        if only is not None:
            ok = ok & (k == only)
        return ok.astype(jnp.int32)

    for d in (1, -1):
        greet(k, d)
    greet(ko, 0)
    greet(k, 2, 0)
    greet(k, -2, 1)
    count = expect(1) + expect(-1) + 1 + expect(-2, 0) + expect(2, 1)

    pushes = []

    class Push:
        def __init__(self, src, dst, same, d, only=None):
            n = len(pushes)
            pushes.append(self)
            self.go, self.come = have(d), have(-d)
            if only is not None:
                self.go = self.go & (k == only)
                self.come = self.come & (k == (only if same else 1 - only))
            self.c = pltpu.make_async_remote_copy(
                src_ref=src, dst_ref=dst, send_sem=ssem.at[n], recv_sem=rsem.at[n],
                device_id=(k if same else ko, t + d), device_id_type=pl.DeviceIdType.MESH)

        def start(self):
            pl.when(self.go)(lambda: self.c.start())

        def sent(self):
            pl.when(self.go)(lambda: self.c.wait_send())

        def arrive(self):
            pl.when(self.come)(lambda: self.c.wait_recv())

    def start(group):
        for c in group:
            c.start()
        return group

    def arrive(group):
        for c in group:
            c.arrive()

    for c in locals_[:3]:
        c.wait()
    offset = jnp.where(k == 0, ins[0, 0], ins[1, 0])
    col_a = jnp.where(k == 0, ins[0, 1], ins[1, 1])
    col_b = jnp.where(k == 0, ins[1, 1], ins[0, 1])

    for c in locals_[3:7]:
        c.wait()
    parent = [plv[...], pdv[...], pfv[1], pfv[0], wv[0], wv[1]]
    block = 0
    for b in range(1, pc // 128):
        block = jnp.where(col_a + WIN >= 128 * b, b, block)
    skip = col_a + WIN - 128 * block
    lane_p = iota((ph, 128), 1)
    packed_w = jnp.zeros((ph, 128), jnp.float32)
    for i, x in enumerate((parent[0], parent[3], parent[2], parent[1], parent[4], parent[5])):
        cut = [x[:, 128 * b:128 * (b + 1)] for b in range(pc // 128)]
        here, then = cut[0], cut[1]
        for b in range(1, pc // 128):
            here = jnp.where(block == b, cut[b], here)
            then = jnp.where(block == b, cut[(b + 1) % (pc // 128)], then)
        by = jnp.where(skip > 16 * i, 128 + 16 * i - skip, 16 * i - skip)
        both = pltpu.roll(jnp.where(lane_p >= skip, here, then), by, 1)
        packed_w = jnp.where((lane_p >> 4) == i, both, packed_w)
    pws[...] = packed_w
    pl.semaphore_wait(barrier, count)
    pl.semaphore_signal(ready, inc=1, device_id=(ko, t), device_id_type=pl.DeviceIdType.MESH)
    windows = [
        Push(pws.at[0:8, :], pwb.at[3 * ph:3 * ph + 8, :], True, -2, 0),
        Push(pws.at[:, :], pwb.at[2 * ph:3 * ph, :], True, -1),
        Push(pws.at[8:ph, :], pwb.at[8:ph, :], True, 1),
    ]
    start(windows)
    halo = []
    for d in (1, -1):
        own = slice(height - 8, height) if d == 1 else slice(0, 8)
        to = halo_n if d == 1 else halo_s
        b, bs = (0, slice(8, 16)) if d == 1 else (1, slice(24, 32))
        halo += [
            Push(fd.at[0, own, :], dep.at[to, :], True, d),
            Push(fl.at[0, own, :], be.at[b, bs, :], True, d),
            Push(ff.at[0, :, own, :], bq.at[b, :, bs, :], True, d),
        ]
    start(halo)

    pwb[ph:2 * ph, :] = packed_w

    diag = iota((height, height), 0) == iota((height, height), 1)
    limit = jnp.sum(jnp.where(diag, shv[...].astype(jnp.float32), 0.0), axis=1, keepdims=True)
    r = iota((height, 128), 0)
    live = (r < exs[0, 0]) & (offset + t * (height // RATIO) + fdiv5(r) < ph * T)
    lim[mid, :] = jnp.where(live, limit, FAR)
    limits = [
        Push(lim.at[top + height - 8:top + height, :], lim.at[halo_n, :], True, 1),
        Push(lim.at[top:top + 8, :], lim.at[halo_s, :], True, -1),
    ]
    start(limits)

    pair = iota((8, pc), 0) >> 1
    for at, tile, first in ((0, slice(ph - 8, ph), 2), (1, slice(0, 8), 0)):
        for part, members in ((0, parent[:4]), (1, parent[4:])):
            out = jnp.zeros((8, pc), jnp.float32)
            for i, x in enumerate(members):
                out = jnp.where(pair == i, shift_rows(x[tile], 2 * i + first), out)
            hs[at, 8 * part:8 * part + 8, :] = out
    parent_halo = [
        Push(hs.at[0], hr.at[0], True, 1),
        Push(hs.at[1], hr.at[1], True, -1),
    ]

    for s in (slice(0, 8), slice(rows - 8, rows)):
        e[s, :] = zrow
        dep[s, :] = zrow
        q[0, s, :] = zrow
        q[1, s, :] = zrow
        lim[s, :] = far
        er[s, :] = zrow[:, :128]
        qr[0, s, :] = zrow[:, :128]
        qr[1, s, :] = zrow[:, :128]
    for b in range(2):
        for s in (slice(0, 8), slice(32, 40)):
            be[b, s, :] = zrow
            bq[b, 1, s, :] = zrow

    colc = iota((CH, breadth), 1)
    last = colc == breadth - 1
    reps = breadth // 128

    def coefficients(r0):
        sl = slice(r0, r0 + CH)
        ss = slice(r0 + 1, r0 + CH + 1)
        colf = colc.astype(jnp.float32)
        wide = lambda s: jnp.concatenate([lim[s, :]] * reps, axis=1)
        act = jnp.where(colf >= wide(sl), 1.0, 0.0)
        act_s = jnp.where(colf >= wide(ss), 1.0, 0.0)
        d0 = dep[sl, :]
        fx = jnp.where(last, 0.0, act * shift_cols(act, -1))
        fxr[sl, :] = fx * RF
        along = (DT_FINE * RF * 0.5) * fx * (d0 + shift_cols(d0, -1))
        cx[sl, :] = along
        cxe[sl, :] = jnp.where(
            last[:, edge], act[:, edge] * jnp.sqrt(d0[:, edge]), along[:, edge])
        fy = act * act_s
        fyr[sl, :] = fy * RF
        cy[sl, :] = (DT_FINE * RF * 0.5) * fy * (d0 + dep[ss, :])

    r8 = iota((8, breadth), 0)

    def advance(ef, qf, first, past, off):
        after = ef[first:first + 8, :]
        after_up = shift_rows(after, -1)
        before_down = shift_rows(qf[1, first - 8:first, :], 1)
        for r0 in range(first, past, 8):
            sl = slice(r0, r0 + 8)
            co = slice(r0 + off, r0 + off + 8)
            e0, e0_up = after, after_up
            after = ef[r0 + 8:r0 + 16, :]
            after_up = shift_rows(after, -1)
            south = jnp.where(r8 == 7, after_up, e0_up)
            nx = fxr[co, :] * qf[0, sl, :] - cx[co, :] * (shift_cols(e0, -1) - e0)
            ny = fyr[co, :] * qf[1, sl, :] - cy[co, :] * (south - e0)
            qf[0, sl, :] = nx
            qf[1, sl, :] = ny
            down = shift_rows(ny, 1)
            north = jnp.where(r8 == 0, before_down, down)
            before_down = down
            ef[sl, :] = e0 - DT_FINE * (nx - shift_cols(nx, 1) + ny - north)

    locals_[7].wait()
    for r0 in range(8 + CH, rows - 8 - CH, CH):
        coefficients(r0)
    for c in locals_[8:]:
        c.wait()
    be[0, 16:32, :] = e[top:top + 16, :]
    be[1, 8:24, :] = e[top + height - 16:top + height, :]
    er[mid, :] = e[mid, edge]
    for i in range(2):
        bq[0, i, 16:32, :] = q[i, top:top + 16, :]
        bq[1, i, 8:24, :] = q[i, top + height - 16:top + height, :]
        qr[i, mid, :] = q[i, mid, edge]

    def inside(step, carry):
        advance(e, q, 8 + CH, rows - 8 - CH, 0)
        return carry

    lax.fori_loop(0, SUBSTEPS, inside, 0)

    lane_f = iota((rows - 16, 128), 1)
    level_at = 128 - WIN
    rowsum = hot_of(iota((32, height), 0) == offset + fdiv5(iota((32, height), 1)))
    begin = 0
    for s in range(128, breadth - 255, 128):
        begin = jnp.where(RATIO * (col_b - col_a + 127) >= s, s, begin)
    sum_other = hot_of(
        fdiv5(iota((256, 128), 0) + begin) == col_b - col_a + WIN + (iota((256, 128), 1) & 15))
    spread = hot_of(
        iota((rows - 16, 8 * ph), 1) % (4 * ph)
        == ph + offset + fdiv5(iota((rows - 16, 8 * ph), 0) + 32) - 8
    )
    twice = iota((32, 2 * height), 1)
    rowsum2 = hot_of(iota((32, 2 * height), 0) == offset + fdiv5(jnp.where(twice >= height, twice - height, twice)))
    wrow = (t - 1) * ph + iota((4 * ph, 128), 0)
    wlane = iota((4 * ph, 128), 1)
    wcol = col_a + 1 + jnp.where(wlane < 64, wlane + 128, wlane)
    w_row_open = jnp.where((wrow >= 0) & (wrow < ph * T - 1), 1.0, 0.0)
    w_col_open = jnp.where(wcol < pc - 1, 1.0, 0.0)

    def window_step(we, wux, wuxw, wuy):
        nx = w_col_open * (wux - CP * whx * (shift_cols(we, -1) - we) + DT_COARSE * wwx) * RP
        nxw = (wuxw - CP * whxw * (we - shift_cols(we, 1)) + DT_COARSE * wwxw) * RP
        ny = w_row_open * (wuy - CP * why * (shift_rows(we, -1) - we) + DT_COARSE * wwy) * RP
        ne = we - CP * (nx - nxw + ny - shift_rows(ny, 1))
        return ne, nx, nxw, ny

    def spread_sea(oe, oux, ne, nux):
        return stacked_hot(spread, jnp.concatenate([oe, oux, ne, nux], axis=1), 2)

    def set_sea(s):
        ea, qb, ea_new, qb_new = [s[:, 128 * i:128 * (i + 1)] for i in range(4)]
        act = jnp.where(float(breadth - 1) >= lim[inner, :], 1.0, 0.0)
        cel = cxe[inner, :]
        old = act * qb - cel * ea
        new = act * qb_new - cel * ea_new
        keep = lane_f == 127
        sea0[inner, :] = jnp.where(keep, old, 0.0)
        sead[inner, :] = jnp.where(keep, new - old, 0.0)

    def edge_columns():
        e0, qx, qy = er[inner, :], qr[0, inner, :], qr[1, inner, :]
        sea, more = sea0[inner, :], sead[inner, :]
        kx, ky = cxe[inner, :], cy[inner, edge]
        fx, fy = fxr[inner, edge], fyr[inner, edge]
        qxw, kxw, fxw = shift_cols(qx, 1), shift_cols(kx, 1), shift_cols(fx, 1)
        for n in range(SUBSTEPS):
            w = (n + 0.5) / SUBSTEPS
            east = jnp.where(lane_f == 127, 0.0, shift_cols(e0, -1))
            qx = fx * qx - kx * (east - e0) + (sea + w * more)
            qxw = fxw * qxw - kxw * (e0 - shift_cols(e0, 1))
            qy = fy * qy - ky * (shift_rows(e0, -1) - e0)
            e0 = e0 - DT_FINE * (qx - qxw + qy - shift_rows(qy, 1))
        er[inner, :] = e0
        qr[0, inner, :] = qx
        qr[1, inner, :] = qy

    def merge_edge(where):
        n = where.stop - where.start
        keep = iota((n, 128), 1) >= 64
        e[where, edge] = jnp.where(keep, er[where, :], e[where, edge])
        for i in range(2):
            q[i, where, edge] = jnp.where(keep, qr[i, where, :], q[i, where, edge])

    arrive(halo)
    arrive(limits)
    er[halo_n, :] = be[0, 8:16, edge]
    er[halo_s, :] = be[1, 24:32, edge]
    for i in range(2):
        qr[i, halo_n, :] = bq[0, i, 8:16, edge]
        qr[i, halo_s, :] = bq[1, i, 24:32, edge]
    coefficients(8)
    coefficients(rows - 8 - CH)

    arrive(windows)
    pw = pwb[...]
    here = lambda x, i: shift_cols(x, 127 - level_at - 16 * i)
    west_of = lambda x, i: shift_cols(x, 128 - level_at - 16 * i)
    we, wux, wuy, wd, wwx, wwy = [here(pw, i) for i in range(6)]
    wuxw, wdw, wwxw = [west_of(pw, i) for i in (1, 3, 4)]
    whx = 0.5 * (wd + shift_cols(pw, 126 - level_at - 48))
    whxw = 0.5 * (wdw + wd)
    why = 0.5 * (wd + shift_rows(wd, -1))

    n1e, n1x, n1xw, n1y = window_step(we, wux, wuxw, wuy)
    sea = spread_sea(we, wuxw, n1e, n1xw)
    for n in range(SUBSTEPS):
        advance(be.at[0], bq.at[0], 8, 32, 0)
        advance(be.at[1], bq.at[1], 8, 32, rows - 40)
    for dst, bnd in ((e, lambda b: be.at[b]), (q.at[0], lambda b: bq.at[b, 0]), (q.at[1], lambda b: bq.at[b, 1])):
        dst[8:24, :] = bnd(0)[8:24, :]
        dst[24:32, :] = jnp.where(r8 < 4, bnd(0)[24:32, :], dst[24:32, :])
        dst[rows - 32:rows - 24, :] = jnp.where(r8 >= 4, bnd(1)[8:16, :], dst[rows - 32:rows - 24, :])
        dst[rows - 24:rows - 8, :] = bnd(1)[16:32, :]

    set_sea(sea)
    edge_columns()
    merge_edge(inner)

    glane = iota((32, 128), 1) >> 4

    def packed(res, n):
        out = res[0:32]
        for i in range(1, n):
            out = jnp.where(glane == i, res[32 * i:32 * (i + 1)], out)
        return out

    def wet(width, start):
        colf = (iota((height, width), 1) + start).astype(jnp.float32)
        return jnp.where(colf >= jnp.concatenate([lim[mid, :]] * (width // 128), axis=1), 1.0, 0.0)

    def restrict(act, lev, qx, qy, columns, with_count):
        part = [
            left_hot(rowsum, act * lev, 2),
            left_hot(rowsum, qx, 2),
            left_hot(rowsum, qy, 2),
        ]
        if with_count:
            part = [mm(rowsum, act.astype(jnp.bfloat16))] + part
        return right_hot(jnp.concatenate(part, axis=0), columns, 2)


    lane_m = iota((height, 128), 1)

    def last_sums(with_count):
        act = wet(128, breadth - 128)
        parts = [act * er[mid, :], qr[0, mid, :], qr[1, mid, :]]
        if with_count:
            parts = [act] + parts
        x = 0.0
        for i, part in enumerate(parts):
            x = jnp.where((lane_m >> 4) == i, shift_cols(part, 16 * i + level_at), x)
        y = x + ((shift_cols(x, 1) + shift_cols(x, 2)) + (shift_cols(x, 3) + shift_cols(x, 4)))
        out = jnp.where((lane_m & 15) == 127 - WIN, y, 0.0)
        return stacked_hot(rowsum2, out, 2)

    pks[0] = last_sums(True)

    def there(ref):
        out = ref[mid, 0:256]
        for s in range(128, breadth - 255, 128):
            out = jnp.where(begin == s, ref[mid, s:s + 256], out)
        return out

    pks[1] = packed(restrict(wet(256, begin), there(e), there(q.at[0]), there(q.at[1]), sum_other, True), 4)
    pl.semaphore_wait(ready, 1)
    near = start([
        Push(pks.at[1], pkb.at[0], False, 0),
        Push(pks.at[1, 8:32, :], pkb.at[1, 8:32, :], False, 1),
        Push(pks.at[1, 0:16, :], pkb.at[2, 0:16, :], False, -1, 1),
        Push(pks.at[1, 24:32, :], pkb.at[3, 24:32, :], False, 2, 0),
        Push(pks.at[1, 0:8, :], pkb.at[4, 0:8, :], False, -2, 1),
        Push(pks.at[0, 8:32, :], pkb.at[5, 8:32, :], True, 1),
        Push(pks.at[0, 0:24, :], pkb.at[6, 0:24, :], True, -1),
    ])

    start(parent_halo)
    colsum = hot_of(fdiv5(iota((breadth, 128), 0)) == iota((breadth, 128), 1))
    s1 = restrict(wet(breadth, 0), e[mid, :], q[0, mid, :], q[1, mid, :], colsum, True)
    for i in range(4):
        cs[i] = s1[32 * i:32 * (i + 1)]

    sums1 = start([
        Push(cs.at[:, 0:24, :], c0a.at[:, 8:32, :], False, 0, 0),
        Push(cs.at[:, 0:16, :], c1.at[:, 8:24, :], False, 0, 1),
        Push(cs.at[:, 8:32, :], c0b.at[:, 0:24, :], True, 1, 0),
        Push(cs.at[:, 8:32, :], c0b.at[:, 0:24, :], False, 1, 0),
        Push(cs.at[:, 8:16, :], c1.at[:, 0:8, :], True, 1, 1),
        Push(cs.at[:, 8:16, :], c1.at[:, 0:8, :], False, 1, 1),
        Push(cs.at[:, 0:8, :], c1.at[:, 24:32, :], True, -1, 1),
        Push(cs.at[:, 0:8, :], c1.at[:, 24:32, :], False, -1, 1),
    ])

    er[...] = e[:, edge]
    qr[...] = q[:, :, edge]

    def everywhere(step, carry):
        advance(e, q, 8, rows - 8, 0)
        return carry

    lax.fori_loop(0, SUBSTEPS, everywhere, 0)

    bulk = hot_of((fdiv5(iota((breadth, 128), 0)) == iota((breadth, 128), 1)) & (iota((breadth, 128), 1) < breadth // RATIO - 1))
    s2 = restrict(wet(breadth, 0), e[mid, :], q[0, mid, :], q[1, mid, :], bulk, False)
    for i in range(3):
        es[i] = s2[32 * i:32 * (i + 1)]

    def final_sums(src, a0, b0, one, idx):
        return start([
            Push(src.at[idx(0)], a0, False, 0, 0),
            Push(src.at[idx(0)], one, False, 0, 1),
            Push(src.at[idx(1)], b0, True, 1, 0),
            Push(src.at[idx(1)], b0, False, 1, 0),
        ])

    sums2 = final_sums(es, e0a, e0b, e1, lambda i: (slice(None), slice(ph * i, ph * (i + 1)), slice(None)))

    xn = 16 + ph
    grow = t * ph - 8 + iota((xn, pc), 0)
    row_open = jnp.where((grow >= 0) & (grow < ph * T - 1), 1.0, 0.0)
    gcol = iota((xn, pc), 1)
    col_open = jnp.where(gcol < pc - 1, 1.0, 0.0)
    col_0 = jnp.where(k == 0, col_a, col_b)
    col_1 = jnp.where(k == 0, col_b, col_a)
    place_0 = hot_of(iota((128, pc), 1) == col_0 + iota((128, pc), 0))
    place_1 = hot_of(iota((128, pc), 1) == col_1 + iota((128, pc), 0))

    arrive(near)
    beside = pkb[0] + pks[0]
    prev = pkb[1] + pkb[5]
    nxt = pkb[2] + pkb[6]
    sums = jnp.concatenate([
        prev[0:ph] + pkb[3][ph:2 * ph],
        beside[0:ph] + prev[ph:2 * ph],
        nxt[0:ph] + beside[ph:2 * ph],
        pkb[4][0:ph] + nxt[ph:2 * ph],
    ], axis=0) * (1.0 / (RATIO * RATIO))
    keep = 1.0 - here(sums, 0)
    u1e = n1e * keep + here(sums, 1)
    u1x = n1x * keep + here(sums, 2)
    u1xw = n1xw * (1.0 - west_of(sums, 0)) + west_of(sums, 2)
    u1y = n1y * keep + here(sums, 3)
    n2e, _, n2xw, _ = window_step(u1e, u1x, u1xw, u1y)
    set_sea(spread_sea(u1e, u1xw, n2e, n2xw))
    edge_columns()

    gs[...] = last_sums(False)
    sums3 = final_sums(gs, g0a, g0b, g1, lambda i: (slice(ph * i, ph * (i + 1)), slice(None)))

    merge_edge(mid)
    fl_out[0] = e[mid, :]
    ff_out[0] = q[:, mid, :]

    arrive(parent_halo)

    def extended(own, i):
        part, j = (0, i) if i < 4 else (8, i - 4)
        return jnp.concatenate([
            shift_rows(hr[0, part:part + 8, :], 6 - 2 * j), own, shift_rows(hr[1, part:part + 8, :], -2 * j)], axis=0)

    xe, xd, xuy, xux, xwx, xwy = [
        extended(x, i) for i, x in enumerate((plv[...], pdv[...], pfv[1], pfv[0], wv[0], wv[1]))]
    hx_p = 0.5 * (xd + shift_cols(xd, -1))
    hy_p = 0.5 * (xd + shift_rows(xd, -1))

    def tile_step(xe, ux, uy):
        nx, ny = parent_step(xe, ux, uy, hx_p, hy_p, xwx, xwy, col_open, row_open)
        west = jnp.where(gcol == 0, 0.0, shift_cols(nx, 1))
        return xe - CP * (nx - west + ny - shift_rows(ny, 1)), nx, ny

    t1e, t1x, t1y = tile_step(xe, xux, xuy)

    arrive(sums1)

    @pl.when(k == 0)
    def _():
        c0a[:, 8:32, :] = cs[:, 0:24, :]

    @pl.when(k == 1)
    def _():
        c1[:, 8:24, :] = cs[:, 0:16, :]

    def spread_sums(a0, b0, one, comps):
        nest0 = jnp.concatenate([a0[i] + b0[i] for i in range(comps)], axis=0)
        nest1 = jnp.concatenate([one[i] for i in range(comps)], axis=0)
        both = right_hot(nest0, place_0, 2) + right_hot(nest1, place_1, 2)
        both = both * (1.0 / (RATIO * RATIO))
        n = both.shape[0] // comps
        return [both[i * n:(i + 1) * n] for i in range(comps)]

    g = spread_sums(c0a, c0b, c1, 4)
    retained = 1.0 - g[0]
    t2 = tile_step(t1e * retained + g[1], t1x * retained + g[2], t1y * retained + g[3])
    own_p = slice(8, 8 + ph)
    held = retained[own_p]

    arrive(sums2)

    @pl.when(k == 0)
    def _():
        e0a[...] = es[:, 0:ph, :]
        g0a[...] = gs[0:ph, :]

    @pl.when(k == 1)
    def _():
        e1[...] = es[:, 0:ph, :]
        g1[...] = gs[0:ph, :]

    g = spread_sums(e0a, e0b, e1, 3)
    base = [t2[i][own_p] * held + g[i] for i in range(3)]
    at_0 = gcol[own_p] == col_0 + (breadth // RATIO - 1)
    at_1 = gcol[own_p] == col_1 + (breadth // RATIO - 1)
    for c in pushes:
        if c not in sums3:
            c.sent()
    arrive(sums3)
    z0 = (g0a[...] + g0b[...]) * (1.0 / (RATIO * RATIO))
    z1 = g1[...] * (1.0 / (RATIO * RATIO))
    outs = []
    for i in range(3):
        v0 = jnp.broadcast_to(z0[:, 127 - WIN + 16 * i:128 - WIN + 16 * i], (ph, pc))
        v1 = jnp.broadcast_to(z1[:, 127 - WIN + 16 * i:128 - WIN + 16 * i], (ph, pc))
        outs.append(base[i] + jnp.where(at_0, v0, 0.0) + jnp.where(at_1, v1, 0.0))
    pl_out[...] = outs[0]
    pf_out[0] = outs[1]
    pf_out[1] = outs[2]
    for c in sums3:
        c.sent()


def store(*refs):
    outs = [pltpu.make_async_copy(refs[i], refs[4 + i], refs[8].at[i]) for i in range(4)]
    for i in (1, 0, 3, 2):
        outs[i].start()
    for c in outs:
        c.wait()


def on_device(fl, ff, fd, shore, ext, inter, plev, pflux, pdep, wind):
    _, height, breadth = fl.shape
    ph, pc = plev.shape
    T = lax.axis_size("tile")
    rows = height + 32
    f32 = jnp.float32

    def vmem(*shape):
        return pltpu.VMEM(shape, f32)

    fine, strip = vmem(rows, breadth), vmem(rows, 128)
    dma = pltpu.SemaphoreType.DMA
    vm = pl.BlockSpec(memory_space=pltpu.VMEM)
    hb = pl.BlockSpec(memory_space=pltpu.HBM)
    pin = lambda x: pltpu.with_memory_space_constraint(x, pltpu.HBM)
    outs = pl.pallas_call(
        functools.partial(kernel, T, height, breadth, ph, pc),
        out_shape=[pltpu.VMEM(x.shape, f32) for x in (fl, ff, plev, pflux)],
        in_specs=[hb] * 10,
        out_specs=[vm] * 4,
        scratch_shapes=[
            fine, vmem(2, rows, breadth), fine, strip,
            fine, fine, fine, fine, strip, strip, strip, strip, vmem(2, rows, 128),
            vmem(2, 40, breadth), vmem(2, 2, 40, breadth),
            vmem(ph, pc), vmem(2, ph, pc), vmem(ph, pc), vmem(2, ph, pc),
            pltpu.VMEM((1, height), jnp.int32), pltpu.SMEM((1, 1), jnp.int32), pltpu.SMEM((2, 2), jnp.int32),
            vmem(ph, 128), vmem(4 * ph, 128), vmem(2, 16, pc), vmem(2, 16, pc),
            vmem(2, 2 * ph, 128), vmem(7, 2 * ph, 128),
            vmem(4, 2 * ph, 128), vmem(4, 2 * ph, 128), vmem(4, 2 * ph, 128), vmem(4, 2 * ph, 128),
            vmem(3, 2 * ph, 128), vmem(3, ph, 128), vmem(3, ph, 128), vmem(3, ph, 128),
            vmem(2 * ph, 128), vmem(ph, 128), vmem(ph, 128), vmem(ph, 128),
            dma((36,)), dma((36,)), dma((10,)), pltpu.SemaphoreType.REGULAR,
        ],
        compiler_params=pltpu.CompilerParams(
            collective_id=0, has_side_effects=True, vmem_limit_bytes=48 * 1024 * 1024),
        name="nested",
    )(pin(fl), pin(ff), pin(fd), pin(shore), ext, pin(inter), pin(plev), pin(pflux), pin(pdep), pin(wind))
    return pl.pallas_call(
        store,
        out_shape=[jax.ShapeDtypeStruct(x.shape, f32) for x in (fl, ff, plev, pflux)],
        in_specs=[vm] * 4,
        out_specs=[hb] * 4,
        scratch_shapes=[dma((4,))],
        compiler_params=pltpu.CompilerParams(vmem_limit_bytes=48 * 1024 * 1024),
        name="store",
    )(*outs)


def solution(mesh):
    in_specs = (
        P("nest", "tile", None),
        P("nest", None, "tile", None),
        P("nest", "tile", None),
        P("nest", "tile"),
        P("nest", "tile"),
        P(),
        P("tile", None),
        P(None, "tile", None),
        P("tile", None),
        P(None, "tile", None),
    )
    out_specs = (
        P("nest", "tile", None),
        P("nest", None, "tile", None),
        P("tile", None),
        P(None, "tile", None),
    )
    return jax.shard_map(
        on_device, mesh=mesh, in_specs=in_specs, out_specs=out_specs, check_vma=False
    )
```

```python
import functools

import jax
import jax.numpy as jnp
from jax import lax
from jax.experimental import pallas as pl
from jax.experimental.pallas import tpu as pltpu
from jax.sharding import PartitionSpec as P

RATIO = 5
SUBSTEPS = 4
DT_FINE = 0.4
DT_COARSE = 1.6
DX_COARSE = 5.0
FRICTION = 0.05
RF = 1.0 / (1.0 + DT_FINE * FRICTION)
RP = 1.0 / (1.0 + DT_COARSE * FRICTION)
CP = DT_COARSE / DX_COARSE
FAR = 1.0e6
WIN = 120
CH = 16


def parts_of(x, n):
    out = []
    for _ in range(n):
        hi = x.astype(jnp.bfloat16)
        out.append(hi)
        x = x - hi.astype(jnp.float32)
    return out


def mm(a, b):
    return lax.dot_general(a, b, (((1,), (0,)), ((), ())), preferred_element_type=jnp.float32)


def left_hot(hot, x, n):
    return sum(mm(hot, p) for p in parts_of(x, n))


def stacked_hot(hot, x, n):
    return mm(hot, jnp.concatenate(parts_of(x, n), axis=0))


def right_hot(x, hot, n):
    return sum(mm(p, hot) for p in parts_of(x, n))


def hot_of(mask):
    return jnp.where(mask, 1.0, 0.0).astype(jnp.bfloat16)


def iota(shape, axis):
    return lax.broadcasted_iota(jnp.int32, shape, axis)


def fdiv5(x):
    return jnp.floor((x.astype(jnp.float32) + 0.5) * 0.2).astype(jnp.int32)


def shift_rows(x, by):
    return pltpu.roll(x, by % x.shape[0], 0)


def shift_cols(x, by):
    return pltpu.roll(x, by % x.shape[1], 1)


def parent_step(e, ux, uy, hx, hy, wx, wy, col_open, row_open):
    nx = col_open * (ux - CP * hx * (shift_cols(e, -1) - e) + DT_COARSE * wx) * RP
    ny = row_open * (uy - CP * hy * (shift_rows(e, -1) - e) + DT_COARSE * wy) * RP
    return nx, ny


def kernel(
    T, height, breadth, ph, pc,
    fl, ff, fd, shore, ext, inter, plev_h, pflux_h, pdep_h, wind_h,
    fl_out, ff_out, pl_out, pf_out,
    e, q, dep, lim, fxr, cx, fyr, cy, cxe, sea0, sead, er, qr, be, bq,
    plv, pfv, pdv, wv, shv, exs, ins, pws, pwb, hs, hr, pks, pkb,
    cs, c0a, c0b, c1, es, e0a, e0b, e1, gs, g0a, g0b, g1,
    ssem, rsem, lsem, ready,
):
    k = lax.axis_index("nest")
    t = lax.axis_index("tile")
    ko = 1 - k
    top = 16
    rows = height + 32
    mid = slice(top, top + height)
    inner = slice(8, rows - 8)
    edge = slice(breadth - 128, breadth)
    halo_n = slice(top - 8, top)
    halo_s = slice(top + height, top + height + 8)

    def have(d):
        return (t + d >= 0) & (t + d < T)

    locals_ = [
        pltpu.make_async_copy(src, dst, lsem.at[i])
        for i, (src, dst) in enumerate((
            (shore, shv), (ext, exs), (inter, ins),
            (plev_h, plv), (pflux_h, pfv), (pdep_h, pdv), (wind_h, wv),
            (fd.at[0], dep.at[mid, :]), (fl.at[0], e.at[mid, :]), (ff.at[0], q.at[:, mid, :]),
        ))
    ]
    for c in locals_:
        c.start()

    for buf in (pwb, pkb, c0a, c0b, c1, e0a, e0b, e1, g0a, g0b, g1, hr):
        buf[...] = jnp.zeros(buf.shape, jnp.float32)
    zrow = jnp.zeros((8, breadth), jnp.float32)
    far = jnp.full((8, 128), FAR, jnp.float32)
    for missing, s, b, bs in ((-1, halo_n, 0, slice(8, 16)), (1, halo_s, 1, slice(24, 32))):
        @pl.when(jnp.logical_not(have(missing)))
        def _():
            dep[s, :] = zrow
            lim[s, :] = far
            be[b, bs, :] = zrow
            bq[b, 0, bs, :] = zrow
            bq[b, 1, bs, :] = zrow

    barrier = pltpu.get_barrier_semaphore()

    def greet(nest, d, only=None):
        ok = have(d)
        if only is not None:
            ok = ok & (k == only)

        @pl.when(ok)
        def _():
            pl.semaphore_signal(barrier, inc=1, device_id=(nest, t + d), device_id_type=pl.DeviceIdType.MESH)

    def expect(d, only=None):
        ok = have(d)
        if only is not None:
            ok = ok & (k == only)
        return ok.astype(jnp.int32)

    for d in (1, -1):
        greet(k, d)
    greet(ko, 0)
    greet(k, 2, 0)
    greet(k, -2, 1)
    count = expect(1) + expect(-1) + 1 + expect(-2, 0) + expect(2, 1)

    pushes = []

    class Push:
        def __init__(self, src, dst, same, d, only=None):
            n = len(pushes)
            pushes.append(self)
            self.go, self.come = have(d), have(-d)
            if only is not None:
                self.go = self.go & (k == only)
                self.come = self.come & (k == (only if same else 1 - only))
            self.c = pltpu.make_async_remote_copy(
                src_ref=src, dst_ref=dst, send_sem=ssem.at[n], recv_sem=rsem.at[n],
                device_id=(k if same else ko, t + d), device_id_type=pl.DeviceIdType.MESH)

        def start(self):
            pl.when(self.go)(lambda: self.c.start())

        def sent(self):
            pl.when(self.go)(lambda: self.c.wait_send())

        def arrive(self):
            pl.when(self.come)(lambda: self.c.wait_recv())

    def start(group):
        for c in group:
            c.start()
        return group

    def arrive(group):
        for c in group:
            c.arrive()

    for c in locals_[:3]:
        c.wait()
    offset = jnp.where(k == 0, ins[0, 0], ins[1, 0])
    col_a = jnp.where(k == 0, ins[0, 1], ins[1, 1])
    col_b = jnp.where(k == 0, ins[1, 1], ins[0, 1])

    for c in locals_[3:7]:
        c.wait()
    parent = [plv[...], pdv[...], pfv[1], pfv[0], wv[0], wv[1]]
    block = 0
    for b in range(1, pc // 128):
        block = jnp.where(col_a + WIN >= 128 * b, b, block)
    skip = col_a + WIN - 128 * block
    lane_p = iota((ph, 128), 1)
    packed_w = jnp.zeros((ph, 128), jnp.float32)
    for i, x in enumerate((parent[0], parent[3], parent[2], parent[1], parent[4], parent[5])):
        cut = [x[:, 128 * b:128 * (b + 1)] for b in range(pc // 128)]
        here, then = cut[0], cut[1]
        for b in range(1, pc // 128):
            here = jnp.where(block == b, cut[b], here)
            then = jnp.where(block == b, cut[(b + 1) % (pc // 128)], then)
        by = jnp.where(skip > 16 * i, 128 + 16 * i - skip, 16 * i - skip)
        both = pltpu.roll(jnp.where(lane_p >= skip, here, then), by, 1)
        packed_w = jnp.where((lane_p >> 4) == i, both, packed_w)
    pws[...] = packed_w
    pl.semaphore_wait(barrier, count)
    pl.semaphore_signal(ready, inc=1, device_id=(ko, t), device_id_type=pl.DeviceIdType.MESH)
    windows = [
        Push(pws.at[0:8, :], pwb.at[3 * ph:3 * ph + 8, :], True, -2, 0),
        Push(pws.at[:, :], pwb.at[2 * ph:3 * ph, :], True, -1),
        Push(pws.at[8:ph, :], pwb.at[8:ph, :], True, 1),
    ]
    start(windows)
    halo = []
    for d in (1, -1):
        own = slice(height - 8, height) if d == 1 else slice(0, 8)
        to = halo_n if d == 1 else halo_s
        b, bs = (0, slice(8, 16)) if d == 1 else (1, slice(24, 32))
        halo += [
            Push(fd.at[0, own, :], dep.at[to, :], True, d),
            Push(fl.at[0, own, :], be.at[b, bs, :], True, d),
            Push(ff.at[0, :, own, :], bq.at[b, :, bs, :], True, d),
        ]
    start(halo)

    pwb[ph:2 * ph, :] = packed_w

    diag = iota((height, height), 0) == iota((height, height), 1)
    limit = jnp.sum(jnp.where(diag, shv[...].astype(jnp.float32), 0.0), axis=1, keepdims=True)
    r = iota((height, 128), 0)
    live = (r < exs[0, 0]) & (offset + t * (height // RATIO) + fdiv5(r) < ph * T)
    lim[mid, :] = jnp.where(live, limit, FAR)
    limits = [
        Push(lim.at[top + height - 8:top + height, :], lim.at[halo_n, :], True, 1),
        Push(lim.at[top:top + 8, :], lim.at[halo_s, :], True, -1),
    ]
    start(limits)

    pair = iota((8, pc), 0) >> 1
    for at, tile, first in ((0, slice(ph - 8, ph), 2), (1, slice(0, 8), 0)):
        for part, members in ((0, parent[:4]), (1, parent[4:])):
            out = jnp.zeros((8, pc), jnp.float32)
            for i, x in enumerate(members):
                out = jnp.where(pair == i, shift_rows(x[tile], 2 * i + first), out)
            hs[at, 8 * part:8 * part + 8, :] = out
    parent_halo = [
        Push(hs.at[0], hr.at[0], True, 1),
        Push(hs.at[1], hr.at[1], True, -1),
    ]

    for s in (slice(0, 8), slice(rows - 8, rows)):
        e[s, :] = zrow
        dep[s, :] = zrow
        q[0, s, :] = zrow
        q[1, s, :] = zrow
        lim[s, :] = far
        er[s, :] = zrow[:, :128]
        qr[0, s, :] = zrow[:, :128]
        qr[1, s, :] = zrow[:, :128]
    for b in range(2):
        for s in (slice(0, 8), slice(32, 40)):
            be[b, s, :] = zrow
            bq[b, 1, s, :] = zrow

    colc = iota((CH, breadth), 1)
    last = colc == breadth - 1
    reps = breadth // 128

    def coefficients(r0):
        sl = slice(r0, r0 + CH)
        ss = slice(r0 + 1, r0 + CH + 1)
        colf = colc.astype(jnp.float32)
        wide = lambda s: jnp.concatenate([lim[s, :]] * reps, axis=1)
        act = jnp.where(colf >= wide(sl), 1.0, 0.0)
        act_s = jnp.where(colf >= wide(ss), 1.0, 0.0)
        d0 = dep[sl, :]
        fx = jnp.where(last, 0.0, act * shift_cols(act, -1))
        fxr[sl, :] = fx * RF
        along = (DT_FINE * RF * 0.5) * fx * (d0 + shift_cols(d0, -1))
        cx[sl, :] = along
        cxe[sl, :] = jnp.where(
            last[:, edge], act[:, edge] * jnp.sqrt(d0[:, edge]), along[:, edge])
        fy = act * act_s
        fyr[sl, :] = fy * RF
        cy[sl, :] = (DT_FINE * RF * 0.5) * fy * (d0 + dep[ss, :])

    r8 = iota((8, breadth), 0)

    def advance(ef, qf, first, past, off):
        after = ef[first:first + 8, :]
        after_up = shift_rows(after, -1)
        before_down = shift_rows(qf[1, first - 8:first, :], 1)
        for r0 in range(first, past, 8):
            sl = slice(r0, r0 + 8)
            co = slice(r0 + off, r0 + off + 8)
            e0, e0_up = after, after_up
            after = ef[r0 + 8:r0 + 16, :]
            after_up = shift_rows(after, -1)
            south = jnp.where(r8 == 7, after_up, e0_up)
            nx = fxr[co, :] * qf[0, sl, :] - cx[co, :] * (shift_cols(e0, -1) - e0)
            ny = fyr[co, :] * qf[1, sl, :] - cy[co, :] * (south - e0)
            qf[0, sl, :] = nx
            qf[1, sl, :] = ny
            down = shift_rows(ny, 1)
            north = jnp.where(r8 == 0, before_down, down)
            before_down = down
            ef[sl, :] = e0 - DT_FINE * (nx - shift_cols(nx, 1) + ny - north)

    locals_[7].wait()
    for r0 in range(8 + CH, rows - 8 - CH, CH):
        coefficients(r0)
    for c in locals_[8:]:
        c.wait()
    be[0, 16:32, :] = e[top:top + 16, :]
    be[1, 8:24, :] = e[top + height - 16:top + height, :]
    er[mid, :] = e[mid, edge]
    for i in range(2):
        bq[0, i, 16:32, :] = q[i, top:top + 16, :]
        bq[1, i, 8:24, :] = q[i, top + height - 16:top + height, :]
        qr[i, mid, :] = q[i, mid, edge]

    def inside(step, carry):
        advance(e, q, 8 + CH, rows - 8 - CH, 0)
        return carry

    lax.fori_loop(0, SUBSTEPS, inside, 0)

    lane_f = iota((rows - 16, 128), 1)
    level_at = 128 - WIN
    rowsum = hot_of(iota((32, height), 0) == offset + fdiv5(iota((32, height), 1)))
    begin = 0
    for s in range(128, breadth - 255, 128):
        begin = jnp.where(RATIO * (col_b - col_a + 127) >= s, s, begin)
    sum_other = hot_of(
        fdiv5(iota((256, 128), 0) + begin) == col_b - col_a + WIN + (iota((256, 128), 1) & 15))
    spread = hot_of(
        iota((rows - 16, 8 * ph), 1) % (4 * ph)
        == ph + offset + fdiv5(iota((rows - 16, 8 * ph), 0) + 32) - 8
    )
    twice = iota((32, 2 * height), 1)
    rowsum2 = hot_of(iota((32, 2 * height), 0) == offset + fdiv5(jnp.where(twice >= height, twice - height, twice)))
    wrow = (t - 1) * ph + iota((4 * ph, 128), 0)
    wlane = iota((4 * ph, 128), 1)
    wcol = col_a + 1 + jnp.where(wlane < 64, wlane + 128, wlane)
    w_row_open = jnp.where((wrow >= 0) & (wrow < ph * T - 1), 1.0, 0.0)
    w_col_open = jnp.where(wcol < pc - 1, 1.0, 0.0)

    def window_step(we, wux, wuxw, wuy):
        nx = w_col_open * (wux - CP * whx * (shift_cols(we, -1) - we) + DT_COARSE * wwx) * RP
        nxw = (wuxw - CP * whxw * (we - shift_cols(we, 1)) + DT_COARSE * wwxw) * RP
        ny = w_row_open * (wuy - CP * why * (shift_rows(we, -1) - we) + DT_COARSE * wwy) * RP
        ne = we - CP * (nx - nxw + ny - shift_rows(ny, 1))
        return ne, nx, nxw, ny

    def spread_sea(oe, oux, ne, nux):
        return stacked_hot(spread, jnp.concatenate([oe, oux, ne, nux], axis=1), 2)

    def set_sea(s):
        ea, qb, ea_new, qb_new = [s[:, 128 * i:128 * (i + 1)] for i in range(4)]
        act = jnp.where(float(breadth - 1) >= lim[inner, :], 1.0, 0.0)
        cel = cxe[inner, :]
        old = act * qb - cel * ea
        new = act * qb_new - cel * ea_new
        keep = lane_f == 127
        sea0[inner, :] = jnp.where(keep, old, 0.0)
        sead[inner, :] = jnp.where(keep, new - old, 0.0)

    def edge_columns():
        e0, qx, qy = er[inner, :], qr[0, inner, :], qr[1, inner, :]
        sea, more = sea0[inner, :], sead[inner, :]
        kx, ky = cxe[inner, :], cy[inner, edge]
        fx, fy = fxr[inner, edge], fyr[inner, edge]
        qxw, kxw, fxw = shift_cols(qx, 1), shift_cols(kx, 1), shift_cols(fx, 1)
        for n in range(SUBSTEPS):
            w = (n + 0.5) / SUBSTEPS
            east = jnp.where(lane_f == 127, 0.0, shift_cols(e0, -1))
            qx = fx * qx - kx * (east - e0) + (sea + w * more)
            qxw = fxw * qxw - kxw * (e0 - shift_cols(e0, 1))
            qy = fy * qy - ky * (shift_rows(e0, -1) - e0)
            e0 = e0 - DT_FINE * (qx - qxw + qy - shift_rows(qy, 1))
        er[inner, :] = e0
        qr[0, inner, :] = qx
        qr[1, inner, :] = qy

    def merge_edge(where):
        n = where.stop - where.start
        keep = iota((n, 128), 1) >= 64
        e[where, edge] = jnp.where(keep, er[where, :], e[where, edge])
        for i in range(2):
            q[i, where, edge] = jnp.where(keep, qr[i, where, :], q[i, where, edge])

    arrive(windows)
    pw = pwb[...]
    here = lambda x, i: shift_cols(x, 127 - level_at - 16 * i)
    west_of = lambda x, i: shift_cols(x, 128 - level_at - 16 * i)
    we, wux, wuy, wd, wwx, wwy = [here(pw, i) for i in range(6)]
    wuxw, wdw, wwxw = [west_of(pw, i) for i in (1, 3, 4)]
    whx = 0.5 * (wd + shift_cols(pw, 126 - level_at - 48))
    whxw = 0.5 * (wdw + wd)
    why = 0.5 * (wd + shift_rows(wd, -1))

    n1e, n1x, n1xw, n1y = window_step(we, wux, wuxw, wuy)
    sea = spread_sea(we, wuxw, n1e, n1xw)
    arrive(halo)
    arrive(limits)
    er[halo_n, :] = be[0, 8:16, edge]
    er[halo_s, :] = be[1, 24:32, edge]
    for i in range(2):
        qr[i, halo_n, :] = bq[0, i, 8:16, edge]
        qr[i, halo_s, :] = bq[1, i, 24:32, edge]
    coefficients(8)
    coefficients(rows - 8 - CH)

    for n in range(SUBSTEPS):
        advance(be.at[0], bq.at[0], 8, 32, 0)
        advance(be.at[1], bq.at[1], 8, 32, rows - 40)
    for dst, bnd in ((e, lambda b: be.at[b]), (q.at[0], lambda b: bq.at[b, 0]), (q.at[1], lambda b: bq.at[b, 1])):
        dst[8:24, :] = bnd(0)[8:24, :]
        dst[24:32, :] = jnp.where(r8 < 4, bnd(0)[24:32, :], dst[24:32, :])
        dst[rows - 32:rows - 24, :] = jnp.where(r8 >= 4, bnd(1)[8:16, :], dst[rows - 32:rows - 24, :])
        dst[rows - 24:rows - 8, :] = bnd(1)[16:32, :]

    set_sea(sea)
    edge_columns()
    merge_edge(inner)

    glane = iota((32, 128), 1) >> 4

    def packed(res, n):
        out = res[0:32]
        for i in range(1, n):
            out = jnp.where(glane == i, res[32 * i:32 * (i + 1)], out)
        return out

    def wet(width, start):
        colf = (iota((height, width), 1) + start).astype(jnp.float32)
        return jnp.where(colf >= jnp.concatenate([lim[mid, :]] * (width // 128), axis=1), 1.0, 0.0)

    def restrict(act, lev, qx, qy, columns, with_count):
        part = [
            left_hot(rowsum, act * lev, 2),
            left_hot(rowsum, qx, 2),
            left_hot(rowsum, qy, 2),
        ]
        if with_count:
            part = [mm(rowsum, act.astype(jnp.bfloat16))] + part
        return right_hot(jnp.concatenate(part, axis=0), columns, 2)


    lane_m = iota((height, 128), 1)

    def last_sums(with_count):
        act = wet(128, breadth - 128)
        parts = [act * er[mid, :], qr[0, mid, :], qr[1, mid, :]]
        if with_count:
            parts = [act] + parts
        x = 0.0
        for i, part in enumerate(parts):
            x = jnp.where((lane_m >> 4) == i, shift_cols(part, 16 * i + level_at), x)
        y = x + ((shift_cols(x, 1) + shift_cols(x, 2)) + (shift_cols(x, 3) + shift_cols(x, 4)))
        out = jnp.where((lane_m & 15) == 127 - WIN, y, 0.0)
        return stacked_hot(rowsum2, out, 2)

    pks[0] = last_sums(True)

    def there(ref):
        out = ref[mid, 0:256]
        for s in range(128, breadth - 255, 128):
            out = jnp.where(begin == s, ref[mid, s:s + 256], out)
        return out

    pks[1] = packed(restrict(wet(256, begin), there(e), there(q.at[0]), there(q.at[1]), sum_other, True), 4)
    pl.semaphore_wait(ready, 1)
    near = start([
        Push(pks.at[1], pkb.at[0], False, 0),
        Push(pks.at[1, 8:32, :], pkb.at[1, 8:32, :], False, 1),
        Push(pks.at[1, 0:16, :], pkb.at[2, 0:16, :], False, -1, 1),
        Push(pks.at[1, 24:32, :], pkb.at[3, 24:32, :], False, 2, 0),
        Push(pks.at[1, 0:8, :], pkb.at[4, 0:8, :], False, -2, 1),
        Push(pks.at[0, 8:32, :], pkb.at[5, 8:32, :], True, 1),
        Push(pks.at[0, 0:24, :], pkb.at[6, 0:24, :], True, -1),
    ])

    start(parent_halo)
    colsum = hot_of(fdiv5(iota((breadth, 128), 0)) == iota((breadth, 128), 1))
    s1 = restrict(wet(breadth, 0), e[mid, :], q[0, mid, :], q[1, mid, :], colsum, True)
    for i in range(4):
        cs[i] = s1[32 * i:32 * (i + 1)]

    sums1 = start([
        Push(cs.at[:, 0:24, :], c0a.at[:, 8:32, :], False, 0, 0),
        Push(cs.at[:, 0:16, :], c1.at[:, 8:24, :], False, 0, 1),
        Push(cs.at[:, 8:32, :], c0b.at[:, 0:24, :], True, 1, 0),
        Push(cs.at[:, 8:32, :], c0b.at[:, 0:24, :], False, 1, 0),
        Push(cs.at[:, 8:16, :], c1.at[:, 0:8, :], True, 1, 1),
        Push(cs.at[:, 8:16, :], c1.at[:, 0:8, :], False, 1, 1),
        Push(cs.at[:, 0:8, :], c1.at[:, 24:32, :], True, -1, 1),
        Push(cs.at[:, 0:8, :], c1.at[:, 24:32, :], False, -1, 1),
    ])

    er[...] = e[:, edge]
    qr[...] = q[:, :, edge]

    def everywhere(step, carry):
        advance(e, q, 8, rows - 8, 0)
        return carry

    lax.fori_loop(0, SUBSTEPS, everywhere, 0)

    bulk = hot_of((fdiv5(iota((breadth, 128), 0)) == iota((breadth, 128), 1)) & (iota((breadth, 128), 1) < breadth // RATIO - 1))
    s2 = restrict(wet(breadth, 0), e[mid, :], q[0, mid, :], q[1, mid, :], bulk, False)
    for i in range(3):
        es[i] = s2[32 * i:32 * (i + 1)]

    def final_sums(src, a0, b0, one, idx):
        return start([
            Push(src.at[idx(0)], a0, False, 0, 0),
            Push(src.at[idx(0)], one, False, 0, 1),
            Push(src.at[idx(1)], b0, True, 1, 0),
            Push(src.at[idx(1)], b0, False, 1, 0),
        ])

    sums2 = final_sums(es, e0a, e0b, e1, lambda i: (slice(None), slice(ph * i, ph * (i + 1)), slice(None)))

    xn = 16 + ph
    grow = t * ph - 8 + iota((xn, pc), 0)
    row_open = jnp.where((grow >= 0) & (grow < ph * T - 1), 1.0, 0.0)
    gcol = iota((xn, pc), 1)
    col_open = jnp.where(gcol < pc - 1, 1.0, 0.0)
    col_0 = jnp.where(k == 0, col_a, col_b)
    col_1 = jnp.where(k == 0, col_b, col_a)
    place_0 = hot_of(iota((128, pc), 1) == col_0 + iota((128, pc), 0))
    place_1 = hot_of(iota((128, pc), 1) == col_1 + iota((128, pc), 0))

    arrive(near)
    beside = pkb[0] + pks[0]
    prev = pkb[1] + pkb[5]
    nxt = pkb[2] + pkb[6]
    sums = jnp.concatenate([
        prev[0:ph] + pkb[3][ph:2 * ph],
        beside[0:ph] + prev[ph:2 * ph],
        nxt[0:ph] + beside[ph:2 * ph],
        pkb[4][0:ph] + nxt[ph:2 * ph],
    ], axis=0) * (1.0 / (RATIO * RATIO))
    keep = 1.0 - here(sums, 0)
    u1e = n1e * keep + here(sums, 1)
    u1x = n1x * keep + here(sums, 2)
    u1xw = n1xw * (1.0 - west_of(sums, 0)) + west_of(sums, 2)
    u1y = n1y * keep + here(sums, 3)
    n2e, _, n2xw, _ = window_step(u1e, u1x, u1xw, u1y)
    set_sea(spread_sea(u1e, u1xw, n2e, n2xw))
    edge_columns()

    gs[...] = last_sums(False)
    sums3 = final_sums(gs, g0a, g0b, g1, lambda i: (slice(ph * i, ph * (i + 1)), slice(None)))

    merge_edge(mid)
    fl_out[0] = e[mid, :]
    ff_out[0] = q[:, mid, :]

    arrive(parent_halo)

    def extended(own, i):
        part, j = (0, i) if i < 4 else (8, i - 4)
        return jnp.concatenate([
            shift_rows(hr[0, part:part + 8, :], 6 - 2 * j), own, shift_rows(hr[1, part:part + 8, :], -2 * j)], axis=0)

    xe, xd, xuy, xux, xwx, xwy = [
        extended(x, i) for i, x in enumerate((plv[...], pdv[...], pfv[1], pfv[0], wv[0], wv[1]))]
    hx_p = 0.5 * (xd + shift_cols(xd, -1))
    hy_p = 0.5 * (xd + shift_rows(xd, -1))

    def tile_step(xe, ux, uy):
        nx, ny = parent_step(xe, ux, uy, hx_p, hy_p, xwx, xwy, col_open, row_open)
        west = jnp.where(gcol == 0, 0.0, shift_cols(nx, 1))
        return xe - CP * (nx - west + ny - shift_rows(ny, 1)), nx, ny

    t1e, t1x, t1y = tile_step(xe, xux, xuy)

    arrive(sums1)

    @pl.when(k == 0)
    def _():
        c0a[:, 8:32, :] = cs[:, 0:24, :]

    @pl.when(k == 1)
    def _():
        c1[:, 8:24, :] = cs[:, 0:16, :]

    def spread_sums(a0, b0, one, comps):
        nest0 = jnp.concatenate([a0[i] + b0[i] for i in range(comps)], axis=0)
        nest1 = jnp.concatenate([one[i] for i in range(comps)], axis=0)
        both = right_hot(nest0, place_0, 2) + right_hot(nest1, place_1, 2)
        both = both * (1.0 / (RATIO * RATIO))
        n = both.shape[0] // comps
        return [both[i * n:(i + 1) * n] for i in range(comps)]

    g = spread_sums(c0a, c0b, c1, 4)
    retained = 1.0 - g[0]
    t2 = tile_step(t1e * retained + g[1], t1x * retained + g[2], t1y * retained + g[3])
    own_p = slice(8, 8 + ph)
    held = retained[own_p]

    arrive(sums2)

    @pl.when(k == 0)
    def _():
        e0a[...] = es[:, 0:ph, :]
        g0a[...] = gs[0:ph, :]

    @pl.when(k == 1)
    def _():
        e1[...] = es[:, 0:ph, :]
        g1[...] = gs[0:ph, :]

    g = spread_sums(e0a, e0b, e1, 3)
    base = [t2[i][own_p] * held + g[i] for i in range(3)]
    at_0 = gcol[own_p] == col_0 + (breadth // RATIO - 1)
    at_1 = gcol[own_p] == col_1 + (breadth // RATIO - 1)
    for c in pushes:
        if c not in sums3:
            c.sent()
    arrive(sums3)
    z0 = (g0a[...] + g0b[...]) * (1.0 / (RATIO * RATIO))
    z1 = g1[...] * (1.0 / (RATIO * RATIO))
    outs = []
    for i in range(3):
        v0 = jnp.broadcast_to(z0[:, 127 - WIN + 16 * i:128 - WIN + 16 * i], (ph, pc))
        v1 = jnp.broadcast_to(z1[:, 127 - WIN + 16 * i:128 - WIN + 16 * i], (ph, pc))
        outs.append(base[i] + jnp.where(at_0, v0, 0.0) + jnp.where(at_1, v1, 0.0))
    pl_out[...] = outs[0]
    pf_out[0] = outs[1]
    pf_out[1] = outs[2]
    for c in sums3:
        c.sent()


def store(*refs):
    outs = [pltpu.make_async_copy(refs[i], refs[4 + i], refs[8].at[i]) for i in range(4)]
    for i in (1, 0, 3, 2):
        outs[i].start()
    for c in outs:
        c.wait()


def on_device(fl, ff, fd, shore, ext, inter, plev, pflux, pdep, wind):
    _, height, breadth = fl.shape
    ph, pc = plev.shape
    T = lax.axis_size("tile")
    rows = height + 32
    f32 = jnp.float32

    def vmem(*shape):
        return pltpu.VMEM(shape, f32)

    fine, strip = vmem(rows, breadth), vmem(rows, 128)
    dma = pltpu.SemaphoreType.DMA
    vm = pl.BlockSpec(memory_space=pltpu.VMEM)
    hb = pl.BlockSpec(memory_space=pltpu.HBM)
    pin = lambda x: pltpu.with_memory_space_constraint(x, pltpu.HBM)
    outs = pl.pallas_call(
        functools.partial(kernel, T, height, breadth, ph, pc),
        out_shape=[pltpu.VMEM(x.shape, f32) for x in (fl, ff, plev, pflux)],
        in_specs=[hb] * 10,
        out_specs=[vm] * 4,
        scratch_shapes=[
            fine, vmem(2, rows, breadth), fine, strip,
            fine, fine, fine, fine, strip, strip, strip, strip, vmem(2, rows, 128),
            vmem(2, 40, breadth), vmem(2, 2, 40, breadth),
            vmem(ph, pc), vmem(2, ph, pc), vmem(ph, pc), vmem(2, ph, pc),
            pltpu.VMEM((1, height), jnp.int32), pltpu.SMEM((1, 1), jnp.int32), pltpu.SMEM((2, 2), jnp.int32),
            vmem(ph, 128), vmem(4 * ph, 128), vmem(2, 16, pc), vmem(2, 16, pc),
            vmem(2, 2 * ph, 128), vmem(7, 2 * ph, 128),
            vmem(4, 2 * ph, 128), vmem(4, 2 * ph, 128), vmem(4, 2 * ph, 128), vmem(4, 2 * ph, 128),
            vmem(3, 2 * ph, 128), vmem(3, ph, 128), vmem(3, ph, 128), vmem(3, ph, 128),
            vmem(2 * ph, 128), vmem(ph, 128), vmem(ph, 128), vmem(ph, 128),
            dma((36,)), dma((36,)), dma((10,)), pltpu.SemaphoreType.REGULAR,
        ],
        compiler_params=pltpu.CompilerParams(
            collective_id=0, has_side_effects=True, vmem_limit_bytes=48 * 1024 * 1024),
        name="nested",
    )(pin(fl), pin(ff), pin(fd), pin(shore), ext, pin(inter), pin(plev), pin(pflux), pin(pdep), pin(wind))
    return pl.pallas_call(
        store,
        out_shape=[jax.ShapeDtypeStruct(x.shape, f32) for x in (fl, ff, plev, pflux)],
        in_specs=[vm] * 4,
        out_specs=[hb] * 4,
        scratch_shapes=[dma((4,))],
        compiler_params=pltpu.CompilerParams(vmem_limit_bytes=48 * 1024 * 1024),
        name="store",
    )(*outs)


def solution(mesh):
    in_specs = (
        P("nest", "tile", None),
        P("nest", None, "tile", None),
        P("nest", "tile", None),
        P("nest", "tile"),
        P("nest", "tile"),
        P(),
        P("tile", None),
        P(None, "tile", None),
        P("tile", None),
        P(None, "tile", None),
    )
    out_specs = (
        P("nest", "tile", None),
        P("nest", None, "tile", None),
        P("tile", None),
        P(None, "tile", None),
    )
    return jax.shard_map(
        on_device, mesh=mesh, in_specs=in_specs, out_specs=out_specs, check_vma=False
    )
```

```python
import functools

import jax
import jax.numpy as jnp
from jax import lax
from jax.experimental import pallas as pl
from jax.experimental.pallas import tpu as pltpu
from jax.sharding import PartitionSpec as P

RATIO = 5
SUBSTEPS = 4
DT_FINE = 0.4
DT_COARSE = 1.6
DX_COARSE = 5.0
FRICTION = 0.05
RF = 1.0 / (1.0 + DT_FINE * FRICTION)
RP = 1.0 / (1.0 + DT_COARSE * FRICTION)
CP = DT_COARSE / DX_COARSE
FAR = 1.0e6
WIN = 120
CH = 16


def parts_of(x, n):
    out = []
    for _ in range(n):
        hi = x.astype(jnp.bfloat16)
        out.append(hi)
        x = x - hi.astype(jnp.float32)
    return out


def mm(a, b):
    return lax.dot_general(a, b, (((1,), (0,)), ((), ())), preferred_element_type=jnp.float32)


def left_hot(hot, x, n):
    return sum(mm(hot, p) for p in parts_of(x, n))


def stacked_hot(hot, x, n):
    return mm(hot, jnp.concatenate(parts_of(x, n), axis=0))


def right_hot(x, hot, n):
    return sum(mm(p, hot) for p in parts_of(x, n))


def hot_of(mask):
    return jnp.where(mask, 1.0, 0.0).astype(jnp.bfloat16)


def iota(shape, axis):
    return lax.broadcasted_iota(jnp.int32, shape, axis)


def fdiv5(x):
    return jnp.floor((x.astype(jnp.float32) + 0.5) * 0.2).astype(jnp.int32)


def shift_rows(x, by):
    return pltpu.roll(x, by % x.shape[0], 0)


def shift_cols(x, by):
    return pltpu.roll(x, by % x.shape[1], 1)


def parent_step(e, ux, uy, hx, hy, wx, wy, col_open, row_open):
    nx = col_open * (ux - CP * hx * (shift_cols(e, -1) - e) + DT_COARSE * wx) * RP
    ny = row_open * (uy - CP * hy * (shift_rows(e, -1) - e) + DT_COARSE * wy) * RP
    return nx, ny


def kernel(
    T, height, breadth, ph, pc,
    fl, ff, fd, shore, ext, inter, plev_h, pflux_h, pdep_h, wind_h,
    fl_out, ff_out, pl_out, pf_out,
    e, q, dep, lim, fxr, cx, fyr, cy, cxe, sea0, sead, er, qr, be, bq,
    plv, pfv, pdv, wv, shv, exs, ins, pws, pwb, hs, hr, pks, pkb,
    cs, c0a, c0b, c1, es, e0a, e0b, e1, gs, g0a, g0b, g1,
    ssem, rsem, lsem, ready,
):
    k = lax.axis_index("nest")
    t = lax.axis_index("tile")
    ko = 1 - k
    top = 16
    rows = height + 32
    mid = slice(top, top + height)
    inner = slice(8, rows - 8)
    edge = slice(breadth - 128, breadth)
    halo_n = slice(top - 8, top)
    halo_s = slice(top + height, top + height + 8)

    def have(d):
        return (t + d >= 0) & (t + d < T)

    locals_ = [
        pltpu.make_async_copy(src, dst, lsem.at[i])
        for i, (src, dst) in enumerate((
            (shore, shv), (ext, exs), (inter, ins),
            (plev_h, plv), (pflux_h, pfv), (pdep_h, pdv), (wind_h, wv),
            (fd.at[0], dep.at[mid, :]), (fl.at[0], e.at[mid, :]), (ff.at[0], q.at[:, mid, :]),
        ))
    ]
    for c in locals_:
        c.start()

    for buf in (pwb, pkb, c0a, c0b, c1, e0a, e0b, e1, g0a, g0b, g1, hr):
        buf[...] = jnp.zeros(buf.shape, jnp.float32)
    zrow = jnp.zeros((8, breadth), jnp.float32)
    far = jnp.full((8, 128), FAR, jnp.float32)
    for missing, s, b, bs in ((-1, halo_n, 0, slice(8, 16)), (1, halo_s, 1, slice(24, 32))):
        @pl.when(jnp.logical_not(have(missing)))
        def _():
            dep[s, :] = zrow
            lim[s, :] = far
            be[b, bs, :] = zrow
            bq[b, 0, bs, :] = zrow
            bq[b, 1, bs, :] = zrow

    barrier = pltpu.get_barrier_semaphore()

    def greet(nest, d, only=None):
        ok = have(d)
        if only is not None:
            ok = ok & (k == only)

        @pl.when(ok)
        def _():
            pl.semaphore_signal(barrier, inc=1, device_id=(nest, t + d), device_id_type=pl.DeviceIdType.MESH)

    def expect(d, only=None):
        ok = have(d)
        if only is not None:
            ok = ok & (k == only)
        return ok.astype(jnp.int32)

    for d in (1, -1):
        greet(k, d)
    greet(ko, 0)
    greet(k, 2, 0)
    greet(k, -2, 1)
    count = expect(1) + expect(-1) + 1 + expect(-2, 0) + expect(2, 1)

    pushes = []

    class Push:
        def __init__(self, src, dst, same, d, only=None):
            n = len(pushes)
            pushes.append(self)
            self.go, self.come = have(d), have(-d)
            if only is not None:
                self.go = self.go & (k == only)
                self.come = self.come & (k == (only if same else 1 - only))
            self.c = pltpu.make_async_remote_copy(
                src_ref=src, dst_ref=dst, send_sem=ssem.at[n], recv_sem=rsem.at[n],
                device_id=(k if same else ko, t + d), device_id_type=pl.DeviceIdType.MESH)

        def start(self):
            pl.when(self.go)(lambda: self.c.start())

        def sent(self):
            pl.when(self.go)(lambda: self.c.wait_send())

        def arrive(self):
            pl.when(self.come)(lambda: self.c.wait_recv())

    def start(group):
        for c in group:
            c.start()
        return group

    def arrive(group):
        for c in group:
            c.arrive()

    for c in locals_[:3]:
        c.wait()
    offset = jnp.where(k == 0, ins[0, 0], ins[1, 0])
    col_a = jnp.where(k == 0, ins[0, 1], ins[1, 1])
    col_b = jnp.where(k == 0, ins[1, 1], ins[0, 1])

    for c in locals_[3:7]:
        c.wait()
    parent = [plv[...], pdv[...], pfv[1], pfv[0], wv[0], wv[1]]
    block = 0
    for b in range(1, pc // 128):
        block = jnp.where(col_a + WIN >= 128 * b, b, block)
    skip = col_a + WIN - 128 * block
    lane_p = iota((ph, 128), 1)
    packed_w = jnp.zeros((ph, 128), jnp.float32)
    for i, x in enumerate((parent[0], parent[3], parent[2], parent[1], parent[4], parent[5])):
        cut = [x[:, 128 * b:128 * (b + 1)] for b in range(pc // 128)]
        here, then = cut[0], cut[1]
        for b in range(1, pc // 128):
            here = jnp.where(block == b, cut[b], here)
            then = jnp.where(block == b, cut[(b + 1) % (pc // 128)], then)
        by = jnp.where(skip > 16 * i, 128 + 16 * i - skip, 16 * i - skip)
        both = pltpu.roll(jnp.where(lane_p >= skip, here, then), by, 1)
        packed_w = jnp.where((lane_p >> 4) == i, both, packed_w)
    pws[...] = packed_w
    pl.semaphore_wait(barrier, count)
    pl.semaphore_signal(ready, inc=1, device_id=(ko, t), device_id_type=pl.DeviceIdType.MESH)
    windows = [
        Push(pws.at[0:8, :], pwb.at[3 * ph:3 * ph + 8, :], True, -2, 0),
        Push(pws.at[:, :], pwb.at[2 * ph:3 * ph, :], True, -1),
        Push(pws.at[8:ph, :], pwb.at[8:ph, :], True, 1),
    ]
    start(windows)
    halo = []
    for d in (1, -1):
        own = slice(height - 8, height) if d == 1 else slice(0, 8)
        to = halo_n if d == 1 else halo_s
        b, bs = (0, slice(8, 16)) if d == 1 else (1, slice(24, 32))
        halo += [
            Push(fd.at[0, own, :], dep.at[to, :], True, d),
            Push(fl.at[0, own, :], be.at[b, bs, :], True, d),
            Push(ff.at[0, :, own, :], bq.at[b, :, bs, :], True, d),
        ]
    start([halo[2], halo[5], halo[1], halo[4], halo[0], halo[3]])

    pwb[ph:2 * ph, :] = packed_w

    diag = iota((height, height), 0) == iota((height, height), 1)
    limit = jnp.sum(jnp.where(diag, shv[...].astype(jnp.float32), 0.0), axis=1, keepdims=True)
    r = iota((height, 128), 0)
    live = (r < exs[0, 0]) & (offset + t * (height // RATIO) + fdiv5(r) < ph * T)
    lim[mid, :] = jnp.where(live, limit, FAR)
    limits = [
        Push(lim.at[top + height - 8:top + height, :], lim.at[halo_n, :], True, 1),
        Push(lim.at[top:top + 8, :], lim.at[halo_s, :], True, -1),
    ]
    start(limits)

    pair = iota((8, pc), 0) >> 1
    for at, tile, first in ((0, slice(ph - 8, ph), 2), (1, slice(0, 8), 0)):
        for part, members in ((0, parent[:4]), (1, parent[4:])):
            out = jnp.zeros((8, pc), jnp.float32)
            for i, x in enumerate(members):
                out = jnp.where(pair == i, shift_rows(x[tile], 2 * i + first), out)
            hs[at, 8 * part:8 * part + 8, :] = out
    parent_halo = [
        Push(hs.at[0], hr.at[0], True, 1),
        Push(hs.at[1], hr.at[1], True, -1),
    ]

    for s in (slice(0, 8), slice(rows - 8, rows)):
        e[s, :] = zrow
        dep[s, :] = zrow
        q[0, s, :] = zrow
        q[1, s, :] = zrow
        lim[s, :] = far
        er[s, :] = zrow[:, :128]
        qr[0, s, :] = zrow[:, :128]
        qr[1, s, :] = zrow[:, :128]
    for b in range(2):
        for s in (slice(0, 8), slice(32, 40)):
            be[b, s, :] = zrow
            bq[b, 1, s, :] = zrow

    colc = iota((CH, breadth), 1)
    last = colc == breadth - 1
    reps = breadth // 128

    def coefficients(r0):
        sl = slice(r0, r0 + CH)
        ss = slice(r0 + 1, r0 + CH + 1)
        colf = colc.astype(jnp.float32)
        wide = lambda s: jnp.concatenate([lim[s, :]] * reps, axis=1)
        act = jnp.where(colf >= wide(sl), 1.0, 0.0)
        act_s = jnp.where(colf >= wide(ss), 1.0, 0.0)
        d0 = dep[sl, :]
        fx = jnp.where(last, 0.0, act * shift_cols(act, -1))
        fxr[sl, :] = fx * RF
        along = (DT_FINE * RF * 0.5) * fx * (d0 + shift_cols(d0, -1))
        cx[sl, :] = along
        cxe[sl, :] = jnp.where(
            last[:, edge], act[:, edge] * jnp.sqrt(d0[:, edge]), along[:, edge])
        fy = act * act_s
        fyr[sl, :] = fy * RF
        cy[sl, :] = (DT_FINE * RF * 0.5) * fy * (d0 + dep[ss, :])

    r8 = iota((8, breadth), 0)

    def advance(ef, qf, first, past, off):
        after = ef[first:first + 8, :]
        after_up = shift_rows(after, -1)
        before_down = shift_rows(qf[1, first - 8:first, :], 1)
        for r0 in range(first, past, 8):
            sl = slice(r0, r0 + 8)
            co = slice(r0 + off, r0 + off + 8)
            e0, e0_up = after, after_up
            after = ef[r0 + 8:r0 + 16, :]
            after_up = shift_rows(after, -1)
            south = jnp.where(r8 == 7, after_up, e0_up)
            nx = fxr[co, :] * qf[0, sl, :] - cx[co, :] * (shift_cols(e0, -1) - e0)
            ny = fyr[co, :] * qf[1, sl, :] - cy[co, :] * (south - e0)
            qf[0, sl, :] = nx
            qf[1, sl, :] = ny
            down = shift_rows(ny, 1)
            north = jnp.where(r8 == 0, before_down, down)
            before_down = down
            ef[sl, :] = e0 - DT_FINE * (nx - shift_cols(nx, 1) + ny - north)

    locals_[7].wait()
    for r0 in range(8 + CH, rows - 8 - CH, CH):
        coefficients(r0)
    for c in locals_[8:]:
        c.wait()
    be[0, 16:32, :] = e[top:top + 16, :]
    be[1, 8:24, :] = e[top + height - 16:top + height, :]
    er[mid, :] = e[mid, edge]
    for i in range(2):
        bq[0, i, 16:32, :] = q[i, top:top + 16, :]
        bq[1, i, 8:24, :] = q[i, top + height - 16:top + height, :]
        qr[i, mid, :] = q[i, mid, edge]

    def inside(step, carry):
        advance(e, q, 8 + CH, rows - 8 - CH, 0)
        return carry

    lax.fori_loop(0, SUBSTEPS, inside, 0)

    lane_f = iota((rows - 16, 128), 1)
    level_at = 128 - WIN
    rowsum = hot_of(iota((32, height), 0) == offset + fdiv5(iota((32, height), 1)))
    begin = 0
    for s in range(128, breadth - 255, 128):
        begin = jnp.where(RATIO * (col_b - col_a + 127) >= s, s, begin)
    sum_other = hot_of(
        fdiv5(iota((256, 128), 0) + begin) == col_b - col_a + WIN + (iota((256, 128), 1) & 15))
    spread = hot_of(
        iota((rows - 16, 8 * ph), 1) % (4 * ph)
        == ph + offset + fdiv5(iota((rows - 16, 8 * ph), 0) + 32) - 8
    )
    twice = iota((32, 2 * height), 1)
    rowsum2 = hot_of(iota((32, 2 * height), 0) == offset + fdiv5(jnp.where(twice >= height, twice - height, twice)))
    wrow = (t - 1) * ph + iota((4 * ph, 128), 0)
    wlane = iota((4 * ph, 128), 1)
    wcol = col_a + 1 + jnp.where(wlane < 64, wlane + 128, wlane)
    w_row_open = jnp.where((wrow >= 0) & (wrow < ph * T - 1), 1.0, 0.0)
    w_col_open = jnp.where(wcol < pc - 1, 1.0, 0.0)

    def window_step(we, wux, wuxw, wuy):
        nx = w_col_open * (wux - CP * whx * (shift_cols(we, -1) - we) + DT_COARSE * wwx) * RP
        nxw = (wuxw - CP * whxw * (we - shift_cols(we, 1)) + DT_COARSE * wwxw) * RP
        ny = w_row_open * (wuy - CP * why * (shift_rows(we, -1) - we) + DT_COARSE * wwy) * RP
        ne = we - CP * (nx - nxw + ny - shift_rows(ny, 1))
        return ne, nx, nxw, ny

    def spread_sea(oe, oux, ne, nux):
        return stacked_hot(spread, jnp.concatenate([oe, oux, ne, nux], axis=1), 2)

    def set_sea(s):
        ea, qb, ea_new, qb_new = [s[:, 128 * i:128 * (i + 1)] for i in range(4)]
        act = jnp.where(float(breadth - 1) >= lim[inner, :], 1.0, 0.0)
        cel = cxe[inner, :]
        old = act * qb - cel * ea
        new = act * qb_new - cel * ea_new
        keep = lane_f == 127
        sea0[inner, :] = jnp.where(keep, old, 0.0)
        sead[inner, :] = jnp.where(keep, new - old, 0.0)

    def edge_columns():
        e0, qx, qy = er[inner, :], qr[0, inner, :], qr[1, inner, :]
        sea, more = sea0[inner, :], sead[inner, :]
        kx, ky = cxe[inner, :], cy[inner, edge]
        fx, fy = fxr[inner, edge], fyr[inner, edge]
        qxw, kxw, fxw = shift_cols(qx, 1), shift_cols(kx, 1), shift_cols(fx, 1)
        for n in range(SUBSTEPS):
            w = (n + 0.5) / SUBSTEPS
            east = jnp.where(lane_f == 127, 0.0, shift_cols(e0, -1))
            qx = fx * qx - kx * (east - e0) + (sea + w * more)
            qxw = fxw * qxw - kxw * (e0 - shift_cols(e0, 1))
            qy = fy * qy - ky * (shift_rows(e0, -1) - e0)
            e0 = e0 - DT_FINE * (qx - qxw + qy - shift_rows(qy, 1))
        er[inner, :] = e0
        qr[0, inner, :] = qx
        qr[1, inner, :] = qy

    def merge_edge(where):
        n = where.stop - where.start
        keep = iota((n, 128), 1) >= 64
        e[where, edge] = jnp.where(keep, er[where, :], e[where, edge])
        for i in range(2):
            q[i, where, edge] = jnp.where(keep, qr[i, where, :], q[i, where, edge])

    arrive(windows)
    pw = pwb[...]
    here = lambda x, i: shift_cols(x, 127 - level_at - 16 * i)
    west_of = lambda x, i: shift_cols(x, 128 - level_at - 16 * i)
    we, wux, wuy, wd, wwx, wwy = [here(pw, i) for i in range(6)]
    wuxw, wdw, wwxw = [west_of(pw, i) for i in (1, 3, 4)]
    whx = 0.5 * (wd + shift_cols(pw, 126 - level_at - 48))
    whxw = 0.5 * (wdw + wd)
    why = 0.5 * (wd + shift_rows(wd, -1))

    n1e, n1x, n1xw, n1y = window_step(we, wux, wuxw, wuy)
    sea = spread_sea(we, wuxw, n1e, n1xw)
    arrive(halo)
    arrive(limits)
    er[halo_n, :] = be[0, 8:16, edge]
    er[halo_s, :] = be[1, 24:32, edge]
    for i in range(2):
        qr[i, halo_n, :] = bq[0, i, 8:16, edge]
        qr[i, halo_s, :] = bq[1, i, 24:32, edge]
    coefficients(8)
    coefficients(rows - 8 - CH)

    for n in range(SUBSTEPS):
        advance(be.at[0], bq.at[0], 8, 32, 0)
        advance(be.at[1], bq.at[1], 8, 32, rows - 40)
    for dst, bnd in ((e, lambda b: be.at[b]), (q.at[0], lambda b: bq.at[b, 0]), (q.at[1], lambda b: bq.at[b, 1])):
        dst[8:24, :] = bnd(0)[8:24, :]
        dst[24:32, :] = jnp.where(r8 < 4, bnd(0)[24:32, :], dst[24:32, :])
        dst[rows - 32:rows - 24, :] = jnp.where(r8 >= 4, bnd(1)[8:16, :], dst[rows - 32:rows - 24, :])
        dst[rows - 24:rows - 8, :] = bnd(1)[16:32, :]

    set_sea(sea)
    edge_columns()
    merge_edge(inner)

    glane = iota((32, 128), 1) >> 4

    def packed(res, n):
        out = res[0:32]
        for i in range(1, n):
            out = jnp.where(glane == i, res[32 * i:32 * (i + 1)], out)
        return out

    def wet(width, start):
        colf = (iota((height, width), 1) + start).astype(jnp.float32)
        return jnp.where(colf >= jnp.concatenate([lim[mid, :]] * (width // 128), axis=1), 1.0, 0.0)

    def restrict(act, lev, qx, qy, columns, with_count):
        part = [
            left_hot(rowsum, act * lev, 2),
            left_hot(rowsum, qx, 2),
            left_hot(rowsum, qy, 2),
        ]
        if with_count:
            part = [mm(rowsum, act.astype(jnp.bfloat16))] + part
        return right_hot(jnp.concatenate(part, axis=0), columns, 2)


    lane_m = iota((height, 128), 1)

    def last_sums(with_count):
        act = wet(128, breadth - 128)
        parts = [act * er[mid, :], qr[0, mid, :], qr[1, mid, :]]
        if with_count:
            parts = [act] + parts
        x = 0.0
        for i, part in enumerate(parts):
            x = jnp.where((lane_m >> 4) == i, shift_cols(part, 16 * i + level_at), x)
        y = x + ((shift_cols(x, 1) + shift_cols(x, 2)) + (shift_cols(x, 3) + shift_cols(x, 4)))
        out = jnp.where((lane_m & 15) == 127 - WIN, y, 0.0)
        return stacked_hot(rowsum2, out, 2)

    pks[0] = last_sums(True)

    def there(ref):
        out = ref[mid, 0:256]
        for s in range(128, breadth - 255, 128):
            out = jnp.where(begin == s, ref[mid, s:s + 256], out)
        return out

    pks[1] = packed(restrict(wet(256, begin), there(e), there(q.at[0]), there(q.at[1]), sum_other, True), 4)
    pl.semaphore_wait(ready, 1)
    near = start([
        Push(pks.at[1], pkb.at[0], False, 0),
        Push(pks.at[1, 8:32, :], pkb.at[1, 8:32, :], False, 1),
        Push(pks.at[1, 0:16, :], pkb.at[2, 0:16, :], False, -1, 1),
        Push(pks.at[1, 24:32, :], pkb.at[3, 24:32, :], False, 2, 0),
        Push(pks.at[1, 0:8, :], pkb.at[4, 0:8, :], False, -2, 1),
        Push(pks.at[0, 8:32, :], pkb.at[5, 8:32, :], True, 1),
        Push(pks.at[0, 0:24, :], pkb.at[6, 0:24, :], True, -1),
    ])

    start(parent_halo)
    colsum = hot_of(fdiv5(iota((breadth, 128), 0)) == iota((breadth, 128), 1))
    s1 = restrict(wet(breadth, 0), e[mid, :], q[0, mid, :], q[1, mid, :], colsum, True)
    for i in range(4):
        cs[i] = s1[32 * i:32 * (i + 1)]

    sums1 = start([
        Push(cs.at[:, 0:24, :], c0a.at[:, 8:32, :], False, 0, 0),
        Push(cs.at[:, 0:16, :], c1.at[:, 8:24, :], False, 0, 1),
        Push(cs.at[:, 8:32, :], c0b.at[:, 0:24, :], True, 1, 0),
        Push(cs.at[:, 8:32, :], c0b.at[:, 0:24, :], False, 1, 0),
        Push(cs.at[:, 8:16, :], c1.at[:, 0:8, :], True, 1, 1),
        Push(cs.at[:, 8:16, :], c1.at[:, 0:8, :], False, 1, 1),
        Push(cs.at[:, 0:8, :], c1.at[:, 24:32, :], True, -1, 1),
        Push(cs.at[:, 0:8, :], c1.at[:, 24:32, :], False, -1, 1),
    ])

    er[...] = e[:, edge]
    qr[...] = q[:, :, edge]

    def everywhere(step, carry):
        advance(e, q, 8, rows - 8, 0)
        return carry

    lax.fori_loop(0, SUBSTEPS, everywhere, 0)

    bulk = hot_of((fdiv5(iota((breadth, 128), 0)) == iota((breadth, 128), 1)) & (iota((breadth, 128), 1) < breadth // RATIO - 1))
    s2 = restrict(wet(breadth, 0), e[mid, :], q[0, mid, :], q[1, mid, :], bulk, False)
    for i in range(3):
        es[i] = s2[32 * i:32 * (i + 1)]

    def final_sums(src, a0, b0, one, idx):
        return start([
            Push(src.at[idx(0)], a0, False, 0, 0),
            Push(src.at[idx(0)], one, False, 0, 1),
            Push(src.at[idx(1)], b0, True, 1, 0),
            Push(src.at[idx(1)], b0, False, 1, 0),
        ])

    sums2 = final_sums(es, e0a, e0b, e1, lambda i: (slice(None), slice(ph * i, ph * (i + 1)), slice(None)))

    xn = 16 + ph
    grow = t * ph - 8 + iota((xn, pc), 0)
    row_open = jnp.where((grow >= 0) & (grow < ph * T - 1), 1.0, 0.0)
    gcol = iota((xn, pc), 1)
    col_open = jnp.where(gcol < pc - 1, 1.0, 0.0)
    col_0 = jnp.where(k == 0, col_a, col_b)
    col_1 = jnp.where(k == 0, col_b, col_a)
    place_0 = hot_of(iota((128, pc), 1) == col_0 + iota((128, pc), 0))
    place_1 = hot_of(iota((128, pc), 1) == col_1 + iota((128, pc), 0))

    arrive(near)
    beside = pkb[0] + pks[0]
    prev = pkb[1] + pkb[5]
    nxt = pkb[2] + pkb[6]
    sums = jnp.concatenate([
        prev[0:ph] + pkb[3][ph:2 * ph],
        beside[0:ph] + prev[ph:2 * ph],
        nxt[0:ph] + beside[ph:2 * ph],
        pkb[4][0:ph] + nxt[ph:2 * ph],
    ], axis=0) * (1.0 / (RATIO * RATIO))
    keep = 1.0 - here(sums, 0)
    u1e = n1e * keep + here(sums, 1)
    u1x = n1x * keep + here(sums, 2)
    u1xw = n1xw * (1.0 - west_of(sums, 0)) + west_of(sums, 2)
    u1y = n1y * keep + here(sums, 3)
    n2e, _, n2xw, _ = window_step(u1e, u1x, u1xw, u1y)
    set_sea(spread_sea(u1e, u1xw, n2e, n2xw))
    edge_columns()

    gs[...] = last_sums(False)
    sums3 = final_sums(gs, g0a, g0b, g1, lambda i: (slice(ph * i, ph * (i + 1)), slice(None)))

    merge_edge(mid)
    fl_out[0] = e[mid, :]
    ff_out[0] = q[:, mid, :]

    arrive(parent_halo)

    def extended(own, i):
        part, j = (0, i) if i < 4 else (8, i - 4)
        return jnp.concatenate([
            shift_rows(hr[0, part:part + 8, :], 6 - 2 * j), own, shift_rows(hr[1, part:part + 8, :], -2 * j)], axis=0)

    xe, xd, xuy, xux, xwx, xwy = [
        extended(x, i) for i, x in enumerate((plv[...], pdv[...], pfv[1], pfv[0], wv[0], wv[1]))]
    hx_p = 0.5 * (xd + shift_cols(xd, -1))
    hy_p = 0.5 * (xd + shift_rows(xd, -1))

    def tile_step(xe, ux, uy):
        nx, ny = parent_step(xe, ux, uy, hx_p, hy_p, xwx, xwy, col_open, row_open)
        west = jnp.where(gcol == 0, 0.0, shift_cols(nx, 1))
        return xe - CP * (nx - west + ny - shift_rows(ny, 1)), nx, ny

    t1e, t1x, t1y = tile_step(xe, xux, xuy)

    arrive(sums1)

    @pl.when(k == 0)
    def _():
        c0a[:, 8:32, :] = cs[:, 0:24, :]

    @pl.when(k == 1)
    def _():
        c1[:, 8:24, :] = cs[:, 0:16, :]

    def spread_sums(a0, b0, one, comps):
        nest0 = jnp.concatenate([a0[i] + b0[i] for i in range(comps)], axis=0)
        nest1 = jnp.concatenate([one[i] for i in range(comps)], axis=0)
        both = right_hot(nest0, place_0, 2) + right_hot(nest1, place_1, 2)
        both = both * (1.0 / (RATIO * RATIO))
        n = both.shape[0] // comps
        return [both[i * n:(i + 1) * n] for i in range(comps)]

    g = spread_sums(c0a, c0b, c1, 4)
    retained = 1.0 - g[0]
    t2 = tile_step(t1e * retained + g[1], t1x * retained + g[2], t1y * retained + g[3])
    own_p = slice(8, 8 + ph)
    held = retained[own_p]

    arrive(sums2)

    @pl.when(k == 0)
    def _():
        e0a[...] = es[:, 0:ph, :]
        g0a[...] = gs[0:ph, :]

    @pl.when(k == 1)
    def _():
        e1[...] = es[:, 0:ph, :]
        g1[...] = gs[0:ph, :]

    g = spread_sums(e0a, e0b, e1, 3)
    base = [t2[i][own_p] * held + g[i] for i in range(3)]
    at_0 = gcol[own_p] == col_0 + (breadth // RATIO - 1)
    at_1 = gcol[own_p] == col_1 + (breadth // RATIO - 1)
    for c in pushes:
        if c not in sums3:
            c.sent()
    arrive(sums3)
    z0 = (g0a[...] + g0b[...]) * (1.0 / (RATIO * RATIO))
    z1 = g1[...] * (1.0 / (RATIO * RATIO))
    outs = []
    for i in range(3):
        v0 = jnp.broadcast_to(z0[:, 127 - WIN + 16 * i:128 - WIN + 16 * i], (ph, pc))
        v1 = jnp.broadcast_to(z1[:, 127 - WIN + 16 * i:128 - WIN + 16 * i], (ph, pc))
        outs.append(base[i] + jnp.where(at_0, v0, 0.0) + jnp.where(at_1, v1, 0.0))
    pl_out[...] = outs[0]
    pf_out[0] = outs[1]
    pf_out[1] = outs[2]
    for c in sums3:
        c.sent()


def store(*refs):
    outs = [pltpu.make_async_copy(refs[i], refs[4 + i], refs[8].at[i]) for i in range(4)]
    for i in (1, 0, 3, 2):
        outs[i].start()
    for c in outs:
        c.wait()


def on_device(fl, ff, fd, shore, ext, inter, plev, pflux, pdep, wind):
    _, height, breadth = fl.shape
    ph, pc = plev.shape
    T = lax.axis_size("tile")
    rows = height + 32
    f32 = jnp.float32

    def vmem(*shape):
        return pltpu.VMEM(shape, f32)

    fine, strip = vmem(rows, breadth), vmem(rows, 128)
    dma = pltpu.SemaphoreType.DMA
    vm = pl.BlockSpec(memory_space=pltpu.VMEM)
    hb = pl.BlockSpec(memory_space=pltpu.HBM)
    pin = lambda x: pltpu.with_memory_space_constraint(x, pltpu.HBM)
    outs = pl.pallas_call(
        functools.partial(kernel, T, height, breadth, ph, pc),
        out_shape=[pltpu.VMEM(x.shape, f32) for x in (fl, ff, plev, pflux)],
        in_specs=[hb] * 10,
        out_specs=[vm] * 4,
        scratch_shapes=[
            fine, vmem(2, rows, breadth), fine, strip,
            fine, fine, fine, fine, strip, strip, strip, strip, vmem(2, rows, 128),
            vmem(2, 40, breadth), vmem(2, 2, 40, breadth),
            vmem(ph, pc), vmem(2, ph, pc), vmem(ph, pc), vmem(2, ph, pc),
            pltpu.VMEM((1, height), jnp.int32), pltpu.SMEM((1, 1), jnp.int32), pltpu.SMEM((2, 2), jnp.int32),
            vmem(ph, 128), vmem(4 * ph, 128), vmem(2, 16, pc), vmem(2, 16, pc),
            vmem(2, 2 * ph, 128), vmem(7, 2 * ph, 128),
            vmem(4, 2 * ph, 128), vmem(4, 2 * ph, 128), vmem(4, 2 * ph, 128), vmem(4, 2 * ph, 128),
            vmem(3, 2 * ph, 128), vmem(3, ph, 128), vmem(3, ph, 128), vmem(3, ph, 128),
            vmem(2 * ph, 128), vmem(ph, 128), vmem(ph, 128), vmem(ph, 128),
            dma((36,)), dma((36,)), dma((10,)), pltpu.SemaphoreType.REGULAR,
        ],
        compiler_params=pltpu.CompilerParams(
            collective_id=0, has_side_effects=True, vmem_limit_bytes=48 * 1024 * 1024),
        name="nested",
    )(pin(fl), pin(ff), pin(fd), pin(shore), ext, pin(inter), pin(plev), pin(pflux), pin(pdep), pin(wind))
    return pl.pallas_call(
        store,
        out_shape=[jax.ShapeDtypeStruct(x.shape, f32) for x in (fl, ff, plev, pflux)],
        in_specs=[vm] * 4,
        out_specs=[hb] * 4,
        scratch_shapes=[dma((4,))],
        compiler_params=pltpu.CompilerParams(vmem_limit_bytes=48 * 1024 * 1024),
        name="store",
    )(*outs)


def solution(mesh):
    in_specs = (
        P("nest", "tile", None),
        P("nest", None, "tile", None),
        P("nest", "tile", None),
        P("nest", "tile"),
        P("nest", "tile"),
        P(),
        P("tile", None),
        P(None, "tile", None),
        P("tile", None),
        P(None, "tile", None),
    )
    out_specs = (
        P("nest", "tile", None),
        P("nest", None, "tile", None),
        P("tile", None),
        P(None, "tile", None),
    )
    return jax.shard_map(
        on_device, mesh=mesh, in_specs=in_specs, out_specs=out_specs, check_vma=False
    )
```
